32 devices in a mesh: wide: 8 (over z, x), narrow: 4 (over y, core).
Axes of the slice: x: 2, y: 2, z: 4, core: 2. Of those that a mesh axis runs over, the one named last changes fastest.
Arguments:
- inputs: bfloat16 [64, 128, 1024], P(('wide', 'narrow')), may hold values from -6 to 6
- memory: bfloat16 [64, 1024, 1024], P(('wide', 'narrow')), may hold values from -6 to 6
- cotangent: bfloat16 [64, 128, 1024], P(('wide', 'narrow')), may hold values from -6 to 6
- dec_lengths: int32 [64, 4], P(('wide', 'narrow')), may hold values from 1 to 80, 128 in all within a row
- mem_lengths: int32 [64, 4], P(('wide', 'narrow')), may hold values from 1 to 640, 1024 in all within a row
- seg_table: int32 [64, 4], P(('wide', 'narrow')), may hold values from 0 to 3
- self_qkv: bfloat16 [1024, 3072], P('wide', 'narrow'), may hold values from -0.1875 to 0.1875
- self_out: bfloat16 [1024, 1024], P('wide', 'narrow'), may hold values from -0.375 to 0.375
- cross_q: bfloat16 [1024, 1024], P('wide', 'narrow'), may hold values from -0.1875 to 0.1875
- cross_kv: bfloat16 [1024, 2048], P('wide', 'narrow'), may hold values from -0.1875 to 0.1875
- cross_out: bfloat16 [1024, 1024], P('wide', 'narrow'), may hold values from -0.75 to 0.75
- fc_in: bfloat16 [1024, 4096], P('wide', 'narrow'), may hold values from -0.1875 to 0.1875
- fc_out: bfloat16 [4096, 1024], P('wide', 'narrow'), may hold values from -0.09375 to 0.09375
- vec_bias: bfloat16 [10, 1024], P(None, ('wide', 'narrow')), may hold values from -1.1953125 to 1.1953125
- norm_gain: bfloat16 [3, 1024], P(None, ('wide', 'narrow')), may hold values from 0.5 to 1.5
- fc_in_bias: bfloat16 [4096], P(('wide', 'narrow')), may hold values from -1.1953125 to 1.1953125
Outputs:
- output: bfloat16 [64, 128, 1024], P(('wide', 'narrow'))
- input_grad: float32 [64, 128, 1024], P(('wide', 'narrow'))
- memory_grad: float32 [64, 1024, 1024], P(('wide', 'narrow'))
- self_qkv_grad: float32 [1024, 3072], P('wide', 'narrow')
- self_out_grad: float32 [1024, 1024], P('wide', 'narrow')
- cross_q_grad: float32 [1024, 1024], P('wide', 'narrow')
- cross_kv_grad: float32 [1024, 2048], P('wide', 'narrow')
- cross_out_grad: float32 [1024, 1024], P('wide', 'narrow')
- fc_in_grad: float32 [1024, 4096], P('wide', 'narrow')
- fc_out_grad: float32 [4096, 1024], P('wide', 'narrow')
- vec_bias_grad: float32 [10, 1024], P(None, ('wide', 'narrow'))
- norm_gain_grad: float32 [3, 1024], P(None, ('wide', 'narrow'))
- fc_in_bias_grad: float32 [4096], P(('wide', 'narrow'))
The draws below stay inside these ranges and needn't reach their ends.
Inputs may be any that keep to these rules, and one draw needn't show every extreme that they name: `dec_lengths`: each pair's 4 query segments fill its 128 positions in order; the longest has exactly 80. `mem_lengths`: each pair's 4 tables fill its 1024 memory positions in order; the longest has exactly 640.
All inputs are finite; a program needn't handle non-finite values.
Results may differ from the reference program's by a relative error of at most 0.02.
Values may be sent and summed in bfloat16 or wider, within the bound.
No kernel may reach another device: no remote copies, remote signals or barrier semaphores. Data moves between devices by JAX's collectives and lax.ppermute only.
A program may use at most 192 MiB of HBM per device.

```python
import math
import jax
import jax.numpy as jnp
import numpy as np
from jax import lax

D = 1024
HEADS = 16
HD = 64
FF = 4096
LEN = 128
MEM = 1024
SEGS = 4
TABS = 4
PAIRS_DEV = 2
PAIRS = 64


def place_ends(values, own_key, least, high):
    dims = values.shape
    spot = [jax.random.randint(jax.random.fold_in(own_key, axis), (), 0, dims[axis]) for axis in range(len(dims))]
    values = values.at[tuple(spot)].set(least)
    longest = dims.index(max(dims))
    spot[longest] = (spot[longest] + 1) % dims[longest]
    return values.at[tuple(spot)].set(high)


def levels(key, shape, shards, least, largest):
    def one(dim, shards_of):
        draws = jax.random.uniform(jax.random.fold_in(jax.random.fold_in(key, 6), dim), (shards_of,), jnp.float32, least / len(shards), largest / len(shards))
        return jnp.repeat(jnp.exp(draws), shape[dim] // shards_of).reshape((-1,) + (1,) * (len(shape) - dim - 1))

    loudness = one(*shards[0])
    for cut in shards[1:]:
        loudness = loudness * one(*cut)
    return loudness


def split_up(number_of, total, bound, lean):
    portions = [(1 << 20) // math.isqrt(grade ** lean) + 1 for grade in range(2, number_of + 1)]
    rest, counts = total - bound - (number_of - 1), [1] * (number_of - 1)
    while rest > 0:
        movable = [i for i in range(number_of - 1) if counts[i] < bound]
        pool, remaining = sum([portions[i] for i in movable]), rest
        for i in movable:
            more = min(bound - counts[i], max(1, remaining * portions[i] // pool), rest)
            counts[i] = counts[i] + more
            rest = rest - more
    return np.array([bound] + counts)


def ragged_sizes(key, amount, total, limit, lean):
    if amount == 2:
        one = jax.random.randint(key, (), max(1, total - limit), min(limit, total - 1) + 1)
        return jnp.stack([one, total - one])
    sizes = jnp.asarray(split_up(amount, total, limit, lean), jnp.int32)
    pairs = (amount - 1) // 2
    donor, receiver = sizes[1:1 + 2 * pairs:2], sizes[2:2 + 2 * pairs:2]
    room = jnp.minimum(donor - 1, limit - receiver)
    shifted = jax.random.randint(jax.random.fold_in(key, 1), (pairs,), 0, 1 << 20) % (room + 1)
    sizes = sizes.at[1:1 + 2 * pairs:2].set(donor - shifted).at[2:2 + 2 * pairs:2].set(receiver + shifted)
    return sizes[jax.random.permutation(jax.random.fold_in(key, 2), amount)]


def gaussian(key, shape, width, most, cuts=(), held_as=jnp.bfloat16):
    level = levels(key, shape, cuts, -0.22, 0.18) if cuts else 1.0
    values = jax.random.normal(key, shape, jnp.float32) * width * level
    return jnp.minimum(jnp.maximum(values, -most), most).astype(held_as)


def setup_inputs(seed: int = 0) -> dict:
    streams_of = jax.random.split(jax.random.key(seed), 17)
    inputs = gaussian(streams_of[0], (PAIRS, LEN, D), 1.0, 6.0, ((0, 32),))
    memory = gaussian(streams_of[1], (PAIRS, MEM, D), 1.0, 6.0, ((0, 32),))
    cotangent = gaussian(streams_of[2], (PAIRS, LEN, D), 1.0, 6.0, ((0, 32),))
    dec_lengths = jax.vmap(lambda own: ragged_sizes(own, SEGS, LEN, LEN * 5 // 8, 1))(jax.random.split(streams_of[3], PAIRS)).reshape((PAIRS, SEGS)).astype(jnp.int32)
    mem_lengths = jax.vmap(lambda own: ragged_sizes(own, TABS, MEM, MEM * 5 // 8, 1))(jax.random.split(streams_of[4], PAIRS)).reshape((PAIRS, TABS)).astype(jnp.int32)
    seg_table = place_ends(jax.random.randint(streams_of[5], (PAIRS, SEGS), 0, TABS), jax.random.fold_in(streams_of[5], 1), 0, TABS - 1).astype(jnp.int32)
    self_qkv = gaussian(streams_of[6], (D, 3 * D), D ** -0.5, 0.1875, ((0, 8), (1, 4)))
    self_out = gaussian(streams_of[7], (D, D), (D // 4) ** -0.5, 0.375, ((0, 8), (1, 4)))
    cross_q = gaussian(streams_of[8], (D, D), D ** -0.5, 0.1875, ((0, 8), (1, 4)))
    cross_kv = gaussian(streams_of[9], (D, 2 * D), D ** -0.5, 0.1875, ((0, 8), (1, 4)))
    cross_out = gaussian(streams_of[10], (D, D), (D // 16) ** -0.5, 0.75, ((0, 8), (1, 4)))
    fc_in = gaussian(streams_of[11], (D, FF), D ** -0.5, 0.1875, ((0, 8), (1, 4)))
    fc_out = gaussian(streams_of[12], (FF, D), FF ** -0.5, 0.09375, ((0, 8), (1, 4)))
    vec_bias = gaussian(streams_of[13], (10, D), 0.3, 1.1953125, ((1, 32),))
    norm_gain = jnp.clip(1.0 + 0.1 * jax.random.normal(streams_of[14], (3, D), jnp.float32), 0.5, 1.5).astype(jnp.bfloat16)
    fc_in_bias = gaussian(streams_of[15], (FF,), 0.3, 1.1953125, ((0, 32),))
    return {"inputs": inputs, "memory": memory, "cotangent": cotangent, "dec_lengths": dec_lengths, "mem_lengths": mem_lengths, "seg_table": seg_table, "self_qkv": self_qkv, "self_out": self_out, "cross_q": cross_q, "cross_kv": cross_kv, "cross_out": cross_out, "fc_in": fc_in, "fc_out": fc_out, "vec_bias": vec_bias, "norm_gain": norm_gain, "fc_in_bias": fc_in_bias}


EPS = 1e-05
MASKED_SCORE = -1000000000.0

@jax.custom_vjp
def low(v):
    return lax.optimization_barrier(v.astype(jnp.bfloat16)).astype(jnp.float32)

@jax.custom_vjp
def low_back(v):
    return v

def low_keep(v):
    return (low(v), None)

def low_pass(kept, grad):
    return (grad,)

def back_keep(v):
    return (v, None)

def back_low(kept, grad):
    return (low(grad),)
low.defvjp(low_keep, low_pass)
low_back.defvjp(back_keep, back_low)

def product(left, right):
    return jnp.einsum('plk,kn->pln', left, right, precision=lax.Precision.HIGHEST)

def layer_norm(summed, gain, shift):
    row_mean = lax.optimization_barrier(jnp.mean(summed, axis=-1, keepdims=True))
    centred = summed - row_mean
    variance = lax.optimization_barrier(jnp.mean(centred * centred, axis=-1, keepdims=True))
    return centred * lax.rsqrt(variance + EPS) * gain + shift

def segment_index(lengths, count):
    segment_ends = jnp.cumsum(lengths, axis=-1).astype(jnp.int32)
    position = jnp.arange(count, dtype=jnp.int32)
    passed = (position[None, :, None] >= segment_ends[:, None, :]).astype(jnp.int32)
    return lax.optimization_barrier(jnp.sum(passed, axis=-1)).astype(jnp.int32)

def build_masks(dec_lengths, mem_lengths, seg_table, dec_count, mem_count):
    segment_ids = segment_index(dec_lengths, dec_count)
    table_ids = segment_index(mem_lengths, mem_count)
    segment_range = jnp.arange(dec_lengths.shape[-1], dtype=jnp.int32)
    matches = segment_ids[:, :, None] == segment_range[None, None, :]
    query_table = lax.optimization_barrier(jnp.sum(jnp.where(matches, seg_table[:, None, :], 0), axis=-1)).astype(jnp.int32)
    position = jnp.arange(dec_count, dtype=jnp.int32)
    self_mask = (segment_ids[:, :, None] == segment_ids[:, None, :]) & (position[None, :, None] >= position[None, None, :])
    cross_mask = query_table[:, :, None] == table_ids[:, None, :]
    return (self_mask, cross_mask)

def split_heads(values):
    return values.reshape(values.shape[0], values.shape[1], HEADS, HD)

def attention(query, keys, values, allowed):
    logits = jnp.einsum('pqhe,pkhe->phqk', split_heads(query), split_heads(keys), precision=lax.Precision.HIGHEST) * HD ** (-0.5)
    logits = low_back(jnp.where(allowed[:, None], logits, MASKED_SCORE))
    probs = jax.nn.softmax(logits, axis=-1)
    mixed = jnp.einsum('phqk,pkhe->pqhe', low(probs), split_heads(values), precision=lax.Precision.HIGHEST)
    return mixed.reshape(query.shape)

def forward(tokens_in, memory_in, params, self_mask, cross_mask):
    w_qkv, w_self_out, w_cross_q, w_cross_kv, w_cross_out, w_fc_in, w_fc_out, bias_rows, gain_rows, fc_bias = params
    model_width = tokens_in.shape[-1]
    zero_bias = jnp.zeros((model_width,), jnp.float32)
    joined = low(low_back(product(tokens_in, w_qkv) + jnp.concatenate([bias_rows[0], zero_bias, bias_rows[1]])))
    query, keys, values = jnp.split(joined, 3, axis=-1)
    self_mix = low(low_back(attention(query, keys, values, self_mask)))
    first_sum = tokens_in + low_back(product(self_mix, w_self_out) + bias_rows[2])
    first_norm = layer_norm(first_sum, gain_rows[0], bias_rows[7])
    cross_query = low(low_back(product(low(first_norm), w_cross_q) + bias_rows[3]))
    cross_pair = low(low_back(product(memory_in, w_cross_kv) + jnp.concatenate([zero_bias, bias_rows[4]])))
    cross_keys, cross_values = jnp.split(cross_pair, 2, axis=-1)
    cross_mix = low(low_back(attention(cross_query, cross_keys, cross_values, cross_mask)))
    second_sum = first_norm + low_back(product(cross_mix, w_cross_out) + bias_rows[5])
    second_norm = layer_norm(second_sum, gain_rows[1], bias_rows[8])
    hidden = low_back(product(low(second_norm), w_fc_in) + fc_bias)
    active = low(jax.nn.gelu(hidden, approximate=False))
    third_sum = second_norm + low_back(product(active, w_fc_out) + bias_rows[6])
    return layer_norm(third_sum, gain_rows[2], bias_rows[9])

def reference(inputs, memory, cotangent, dec_lengths, mem_lengths, seg_table, self_qkv, self_out, cross_q, cross_kv, cross_out, fc_in, fc_out, vec_bias, norm_gain, fc_in_bias):
    params = tuple((item.astype(jnp.float32) for item in (self_qkv, self_out, cross_q, cross_kv, cross_out, fc_in, fc_out, vec_bias, norm_gain, fc_in_bias)))
    groups = inputs.shape[0] // PAIRS_DEV

    def regroup(array):
        return array.reshape((groups, PAIRS_DEV) + array.shape[1:])

    def one_group(running, pieces):
        tokens_in, memory_in, grad_in, dec_piece, mem_piece, table_piece = pieces
        self_mask, cross_mask = build_masks(dec_piece, mem_piece, table_piece, LEN, MEM)

        def forward_run(tokens_f, memory_f, *weights):
            return forward(tokens_f, memory_f, weights, self_mask, cross_mask)
        result, pullback = jax.vjp(forward_run, tokens_in.astype(jnp.float32), memory_in.astype(jnp.float32), *params)
        grads = pullback(grad_in.astype(jnp.float32))
        running = jax.tree.map(jnp.add, running, tuple(grads[2:]))
        return (running, (result.astype(jnp.bfloat16), grads[0], grads[1]))
    initial = tuple((jnp.zeros_like(item) for item in params))
    totals, (results, input_grads, memory_grads) = lax.scan(one_group, initial, (regroup(inputs), regroup(memory), regroup(cotangent), regroup(dec_lengths), regroup(mem_lengths), regroup(seg_table)))
    output = results.reshape(inputs.shape)
    input_grad = input_grads.reshape(inputs.shape)
    memory_grad = memory_grads.reshape(memory.shape)
    return (output, input_grad, memory_grad, totals[0], totals[1], totals[2], totals[3], totals[4], totals[5], totals[6], totals[7], totals[8], totals[9])
```

```python
from functools import partial

import jax
import jax.numpy as jnp
from jax import lax
from jax.sharding import PartitionSpec as P

HD = 64
BOTH = ("wide", "narrow")
EPS = 1e-05
MASKED_SCORE = -1000000000.0
LOW = jnp.bfloat16
FULL = jnp.float32


def layer_norm(summed, gain, shift):
    row_mean = jnp.mean(summed, axis=-1, keepdims=True)
    centred = summed - row_mean
    variance = jnp.mean(centred * centred, axis=-1, keepdims=True)
    return centred * lax.rsqrt(variance + EPS) * gain + shift


def segment_index(lengths, count):
    segment_ends = jnp.cumsum(lengths, axis=-1)
    position = jnp.arange(count, dtype=jnp.int32)
    passed = (position[None, :, None] >= segment_ends[:, None, :]).astype(jnp.int32)
    return jnp.sum(passed, axis=-1)


def build_masks(dec_lengths, mem_lengths, seg_table, dec_count, mem_count):
    segment_ids = segment_index(dec_lengths, dec_count)
    table_ids = segment_index(mem_lengths, mem_count)
    segment_range = jnp.arange(dec_lengths.shape[-1], dtype=jnp.int32)
    matches = segment_ids[:, :, None] == segment_range[None, None, :]
    query_table = jnp.sum(jnp.where(matches, seg_table[:, None, :], 0), axis=-1)
    position = jnp.arange(dec_count, dtype=jnp.int32)
    self_mask = (segment_ids[:, :, None] == segment_ids[:, None, :]) & (
        position[None, :, None] >= position[None, None, :]
    )
    cross_mask = query_table[:, :, None] == table_ids[:, None, :]
    return (self_mask, cross_mask)


def factors(count):
    out = []
    while count > 1:
        step = 4 if count % 4 == 0 else 2
        out.append(step)
        count //= step
    return out


class Net:
    def __init__(self, wide, narrow):
        self.wide, self.narrow, self.lines = wide, narrow, wide // 2
        w, n = lax.axis_index("wide"), lax.axis_index("narrow")
        self.z, self.x, self.y, self.c = w // 2, w % 2, n // 2, n % 2
        both = [(i, j) for i in range(wide) for j in range(narrow)]

        def flat(i, j):
            return i * narrow + j

        def pairs(x_core):
            return [
                (flat(i, j), flat(i ^ 1, j) if j % 2 == x_core else flat(i, j ^ 2)) for i, j in both
            ]

        self.first, self.second = pairs(0), pairs(1)
        self.core = [(j, j ^ 1) for j in range(narrow)]

    def shift(self, stride, size, step):
        out = []
        for w in range(self.wide):
            z, x = divmod(w, 2)
            digit = z // stride % size
            to = z + ((digit + step) % size - digit) * stride
            out.append((w, to * 2 + x))
        return out

    def gather(self, shard):
        held, stride = shard[None], 1
        for size in factors(self.lines):
            digit = self.z // stride % size
            new = jnp.zeros((size,) + held.shape, held.dtype)
            new = lax.dynamic_update_index_in_dim(new, held, digit, 0)
            for step in range(1, size):
                got = lax.ppermute(held, "wide", self.shift(stride, size, step))
                new = lax.dynamic_update_index_in_dim(new, got, (digit - step) % size, 0)
            held = new.reshape((-1,) + shard.shape)
            stride *= size
        one = lax.ppermute(held, BOTH, self.first)
        two = lax.ppermute(held, BOTH, self.second)
        three = lax.ppermute(one, BOTH, self.second)
        full = jnp.zeros((2, self.lines, 2) + shard.shape, held.dtype)

        def put(full, piece, dy, dx):
            at = ((self.y + dy) % 2, 0, (self.x + dx) % 2, 0, 0)
            return lax.dynamic_update_slice(full, piece[None, :, None], at)

        full = put(full, held, 0, 0)
        full = put(full, one, self.c, 1 - self.c)
        full = put(full, two, 1 - self.c, self.c)
        full = put(full, three, 1, 1)
        mine = full.reshape((2, -1) + shard.shape[1:])
        return mine, lax.ppermute(mine, "narrow", self.core)

    def reduce(self, mine, other, rows):
        cols = mine.shape[-1]
        got = lax.ppermute(other, "narrow", self.core)
        shape = (2, self.lines, 2, rows, cols)
        mine, got = mine.reshape(shape), got.reshape(shape)

        def quad(dy, dx):
            at = ((self.y + dy) % 2, 0, (self.x + dx) % 2, 0, 0)
            size = (1, self.lines, 1, rows, cols)
            return sum(lax.dynamic_slice(a, at, size)[0, :, 0].astype(FULL) for a in (mine, got))

        half = lax.ppermute(quad(1 - self.c, self.c).astype(LOW), BOTH, self.second)
        far = lax.ppermute(quad(1, 1).astype(LOW), BOTH, self.second)
        near = (quad(self.c, 1 - self.c) + far.astype(FULL)).astype(LOW)
        near = lax.ppermute(near, BOTH, self.first)
        total = quad(0, 0) + half.astype(FULL) + near.astype(FULL)
        stride = self.lines
        for size in reversed(factors(self.lines)):
            stride //= size
            digit = self.z // stride % size
            total = total.reshape((size, stride, rows, cols))
            low = total.astype(LOW)
            total = lax.dynamic_index_in_dim(total, digit, 0, keepdims=False)
            for step in range(1, size):
                out = lax.dynamic_index_in_dim(low, (digit + step) % size, 0, keepdims=False)
                total += lax.ppermute(out, "wide", self.shift(stride, size, step)).astype(FULL)
        return total.reshape(rows, cols)

    def swap(self, a, b):
        first = self.c == 0
        return jnp.where(first, a, b), jnp.where(first, b, a)


def blocks_out(tokens, weight):
    return jnp.einsum("tk,ykj->tyj", tokens, weight, preferred_element_type=FULL)


def project(net, tokens, weights):
    mine, other = (blocks_out(tokens, w) for w in weights)
    return jnp.stack(net.swap(mine, other), axis=2).reshape(tokens.shape[0], -1)


def split_cores(net, values):
    parts = values.reshape(values.shape[0], 2, 2, -1)
    return net.swap(parts[:, :, 0], parts[:, :, 1])


def weight_grad(left, parts):
    return tuple(
        jnp.einsum("tk,tyj->ykj", left, p, preferred_element_type=FULL).astype(LOW) for p in parts
    )


def back_through(parts, weights):
    return sum(
        jnp.einsum("tyj,ykj->tk", p, w, preferred_element_type=FULL)
        for p, w in zip(parts, weights)
    )


def column_sums(values):
    return jnp.sum(values, axis=0, dtype=FULL)


def split_heads(values, pairs):
    return values.reshape(pairs, values.shape[0] // pairs, -1, HD)


def score_block(query, keys, allowed):
    logits = jnp.einsum("pqhe,pkhe->phqk", query, keys, preferred_element_type=FULL) * HD ** (-0.5)
    return jnp.where(allowed[:, None], logits, MASKED_SCORE)


def attend_forward(query, keys, values, allowed):
    pairs = allowed.shape[0]
    q, k, v = (split_heads(a, pairs) for a in (query, keys, values))
    logits = score_block(q, k, allowed)
    row_max = jnp.max(logits, axis=-1, keepdims=True)
    log_total = row_max + jnp.log(jnp.sum(jnp.exp(logits - row_max), axis=-1, keepdims=True))
    probs_low = jnp.exp(logits - log_total).astype(LOW)
    mixed = jnp.einsum("phqk,pkhe->pqhe", probs_low, v, preferred_element_type=FULL)
    return (mixed.reshape(query.shape).astype(LOW), log_total)


def attend_backward(query, keys, values, allowed, log_total, grad_mix):
    pairs = allowed.shape[0]
    q, k, v, m = (split_heads(a, pairs) for a in (query, keys, values, grad_mix))
    probs = jnp.exp(score_block(q, k, allowed) - log_total)
    grad_probs = jnp.einsum("pqhe,pkhe->phqk", m, v, preferred_element_type=FULL)
    row_dot = jnp.sum(probs * grad_probs, axis=-1, keepdims=True)
    grad_logits = (probs * (grad_probs - row_dot)).astype(LOW)
    scale = HD ** (-0.5)
    grad_query = jnp.einsum("phqk,pkhe->pqhe", grad_logits, k, preferred_element_type=FULL) * scale
    grad_keys = jnp.einsum("phqk,pqhe->pkhe", grad_logits, q, preferred_element_type=FULL) * scale
    grad_values = jnp.einsum(
        "phqk,pqhe->pkhe", probs.astype(LOW), m, preferred_element_type=FULL
    )
    return tuple(
        g.reshape(a.shape).astype(LOW)
        for g, a in ((grad_query, query), (grad_keys, keys), (grad_values, values))
    )


def per_device(
    inputs,
    memory,
    cotangent,
    dec_lengths,
    mem_lengths,
    seg_table,
    self_qkv,
    self_out,
    cross_q,
    cross_kv,
    cross_out,
    fc_in,
    fc_out,
    vec_bias,
    norm_gain,
    fc_in_bias,
    *,
    wide,
    narrow,
):
    net = Net(wide, narrow)
    pairs, length, width = inputs.shape
    self_mask, cross_mask = build_masks(
        dec_lengths, mem_lengths, seg_table, length, memory.shape[1]
    )
    tokens = inputs.reshape(-1, width)
    table = memory.reshape(-1, width)
    upstream = cotangent.reshape(-1, width).astype(FULL)

    rows = jnp.concatenate([vec_bias, norm_gain])
    packed = jnp.concatenate([rows.reshape(-1), fc_in_bias])
    vectors = lax.all_gather(packed, BOTH, axis=0).astype(FULL)
    fc_bias = vectors[:, rows.size :].reshape(-1)
    vectors = vectors[:, : rows.size].reshape(wide * narrow, rows.shape[0], -1)
    vectors = jnp.transpose(vectors, (1, 0, 2)).reshape(rows.shape[0], -1)
    bias_rows, gain_rows = vectors[:10], vectors[10:]

    w_qkv = net.gather(self_qkv)
    middle = jnp.concatenate([self_out, cross_q, cross_kv, cross_out], axis=1)
    w_middle = net.gather(middle)
    w_fc_in = net.gather(fc_in)
    w_fc_out = net.gather(fc_out)
    quarter = width // narrow

    def part(start, count):
        return tuple(w[:, :, start * quarter : (start + count) * quarter] for w in w_middle)

    w_self_out, w_cross_q, w_cross_kv, w_cross_out = part(0, 1), part(1, 1), part(2, 2), part(4, 1)

    zero_bias = jnp.zeros((width,), FULL)
    joined = (
        project(net, tokens, w_qkv) + jnp.concatenate([bias_rows[0], zero_bias, bias_rows[1]])
    ).astype(LOW)
    query, keys, values = jnp.split(joined, 3, axis=-1)
    self_mix, self_total = attend_forward(query, keys, values, self_mask)
    first_sum = tokens.astype(FULL) + (project(net, self_mix, w_self_out) + bias_rows[2])
    first_norm = layer_norm(first_sum, gain_rows[0], bias_rows[7])
    first_low = first_norm.astype(LOW)
    cross_query = (project(net, first_low, w_cross_q) + bias_rows[3]).astype(LOW)
    value_bias = net.swap(*jnp.split(bias_rows[4], 2))
    pair_parts = tuple(
        (blocks_out(table, w) + jnp.stack([jnp.zeros_like(b), b])).astype(LOW)
        for w, b in zip(w_cross_kv, value_bias)
    )
    query_parts = net.swap(*jnp.split(cross_query, 2, axis=1))
    mixed = [
        attend_forward(q, kv[:, 0], kv[:, 1], cross_mask)
        for q, kv in zip(query_parts, pair_parts)
    ]
    cross_mix = jnp.concatenate(net.swap(mixed[0][0], mixed[1][0]), axis=1)
    second_sum = first_norm + (project(net, cross_mix, w_cross_out) + bias_rows[5])
    second_norm = layer_norm(second_sum, gain_rows[1], bias_rows[8])
    second_low = second_norm.astype(LOW)
    hidden = project(net, second_low, w_fc_in) + fc_bias
    active = jax.nn.gelu(hidden, approximate=False).astype(LOW)
    third_sum = second_norm + (project(net, active, w_fc_out) + bias_rows[6])
    output = layer_norm(third_sum, gain_rows[2], bias_rows[9]).astype(LOW)

    _, third_back = jax.vjp(layer_norm, third_sum, gain_rows[2], bias_rows[9])
    d_third, d_gain3, d_shift3 = third_back(upstream)
    d_branch3 = d_third.astype(LOW)
    parts3 = split_cores(net, d_branch3)
    g_fc_out = net.reduce(*weight_grad(active, parts3), fc_out.shape[0])
    d_bias_fc_out = column_sums(d_branch3)
    d_active = back_through(parts3, w_fc_out)
    _, gelu_back = jax.vjp(partial(jax.nn.gelu, approximate=False), hidden)
    d_hidden = gelu_back(d_active)[0].astype(LOW)
    parts_hidden = split_cores(net, d_hidden)
    g_fc_in = net.reduce(*weight_grad(second_low, parts_hidden), fc_in.shape[0])
    g_fc_bias = column_sums(d_hidden)
    d_second = d_third + back_through(parts_hidden, w_fc_in)
    _, second_back = jax.vjp(layer_norm, second_sum, gain_rows[1], bias_rows[8])
    d_sum2, d_gain2, d_shift2 = second_back(d_second)
    d_branch2 = d_sum2.astype(LOW)
    parts2 = split_cores(net, d_branch2)
    wg_cross_out = weight_grad(cross_mix, parts2)
    d_bias_cross_out = column_sums(d_branch2)
    d_cross_mix = back_through(parts2, w_cross_out).astype(LOW)
    mix_parts = net.swap(*jnp.split(d_cross_mix, 2, axis=1))
    d_query_parts, d_pair_parts = [], []
    for q, kv, m, (_, total) in zip(query_parts, pair_parts, mix_parts, mixed):
        dq, dk, dv = attend_backward(q, kv[:, 0], kv[:, 1], cross_mask, total, m)
        d_query_parts.append(dq)
        d_pair_parts.append(jnp.stack([dk, dv], axis=1))
    d_cross_query = jnp.concatenate(net.swap(*d_query_parts), axis=1)
    parts_cq = split_cores(net, d_cross_query)
    wg_cross_q = weight_grad(first_low, parts_cq)
    d_bias_cross_q = column_sums(d_cross_query)
    wg_cross_kv = weight_grad(table, d_pair_parts)
    d_bias_cross_v = jnp.concatenate(net.swap(*(column_sums(d[:, 1]) for d in d_pair_parts)))
    memory_grad = back_through(d_pair_parts, w_cross_kv)
    d_first = d_sum2 + back_through(parts_cq, w_cross_q)
    _, first_back = jax.vjp(layer_norm, first_sum, gain_rows[0], bias_rows[7])
    d_sum1, d_gain1, d_shift1 = first_back(d_first)
    d_branch1 = d_sum1.astype(LOW)
    parts1 = split_cores(net, d_branch1)
    wg_self_out = weight_grad(self_mix, parts1)
    wg_middle = [
        jnp.concatenate(group, axis=2)
        for group in zip(wg_self_out, wg_cross_q, wg_cross_kv, wg_cross_out)
    ]
    g_middle = net.reduce(*wg_middle, self_out.shape[0])
    d_bias_self_out = column_sums(d_branch1)
    d_self_mix = back_through(parts1, w_self_out).astype(LOW)
    d_joined = jnp.concatenate(
        attend_backward(query, keys, values, self_mask, self_total, d_self_mix), axis=1
    )
    parts_joined = split_cores(net, d_joined)
    g_qkv = net.reduce(*weight_grad(tokens, parts_joined), self_qkv.shape[0])
    d_bias_query = column_sums(d_joined[:, :width])
    d_bias_value = column_sums(d_joined[:, 2 * width :])
    input_grad = d_sum1 + back_through(parts_joined, w_qkv)

    g_rows = jnp.stack(
        [
            d_bias_query,
            d_bias_value,
            d_bias_self_out,
            d_bias_cross_q,
            d_bias_cross_v,
            d_bias_cross_out,
            d_bias_fc_out,
            d_shift1,
            d_shift2,
            d_shift3,
            d_gain1,
            d_gain2,
            d_gain3,
        ]
    )
    g_rows = jnp.transpose(g_rows.reshape(rows.shape[0], wide * narrow, -1), (1, 0, 2))
    g_packed = jnp.concatenate(
        [g_rows.reshape(wide * narrow, -1), g_fc_bias.reshape(wide * narrow, -1)], axis=1
    )
    g_packed = lax.psum_scatter(g_packed, BOTH, scatter_dimension=0, tiled=True)[0]
    g_rows, g_fc_bias = g_packed[: rows.size].reshape(rows.shape), g_packed[rows.size :]
    return (
        output.reshape(inputs.shape),
        input_grad.reshape(inputs.shape),
        memory_grad.reshape(memory.shape),
        g_qkv,
        g_middle[:, :quarter],
        g_middle[:, quarter : 2 * quarter],
        g_middle[:, 2 * quarter : 4 * quarter],
        g_middle[:, 4 * quarter :],
        g_fc_in,
        g_fc_out,
        g_rows[:10],
        g_rows[10:],
        g_fc_bias,
    )


def solution(mesh):
    tokens = P(BOTH, None, None)
    lengths = P(BOTH, None)
    weight = P("wide", "narrow")
    vector = P(None, BOTH)
    return jax.shard_map(
        partial(per_device, wide=mesh.shape["wide"], narrow=mesh.shape["narrow"]),
        mesh=mesh,
        in_specs=(tokens,) * 3 + (lengths,) * 3 + (weight,) * 7 + (vector, vector, P(BOTH)),
        out_specs=(tokens,) * 3 + (weight,) * 7 + (vector, vector, P(BOTH)),
        check_vma=False,
    )
```

```python
import math
from functools import partial

import jax
import jax.numpy as jnp
from jax import lax
from jax.experimental import pallas as pl
from jax.experimental.pallas import tpu as pltpu
from jax.sharding import PartitionSpec as P

HD = 64
PAIR = 2 * HD
BOTH = ("wide", "narrow")
EPS = 1e-05
MASKED_SCORE = -1000000000.0
LOW = jnp.bfloat16
FULL = jnp.float32
VMEM_BYTES = 56 * 1024 * 1024
B_QUERY, B_VALUE, B_SELF_OUT, B_CROSS_Q, B_CROSS_V, B_CROSS_OUT, B_FC_OUT = range(7)
SHIFT, GAIN = 7, 10


def factors(count):
    out = []
    while count > 1:
        step = 4 if count % 4 == 0 else 2
        out.append(step)
        count //= step
    return out


def after(value, *others):
    return lax.optimization_barrier((value, others))[0]


class Net:
    def __init__(self, wide, narrow):
        self.wide, self.narrow, self.lines = wide, narrow, wide // 2
        w, n = lax.axis_index("wide"), lax.axis_index("narrow")
        self.x, self.y, self.c = w % 2, n // 2, n % 2
        self.which = self.c.reshape(1).astype(jnp.int32)
        self.sizes = factors(self.lines)
        self.strides = [math.prod(self.sizes[:i]) for i in range(len(self.sizes))]
        digits = [w // 2 // stride % size for stride, size in zip(self.strides, self.sizes)]
        self.place = jnp.stack([self.y, self.x, self.c, *digits]).astype(jnp.int32)
        both = [(i, j) for i in range(wide) for j in range(narrow)]

        def flat(i, j):
            return i * narrow + j

        def pairs(x_core):
            return [
                (flat(i, j), flat(i ^ 1, j) if j % 2 == x_core else flat(i, j ^ 2)) for i, j in both
            ]

        self.first, self.second = pairs(0), pairs(1)
        self.core = [(j, j ^ 1) for j in range(narrow)]
        self.sent = []

    def shift(self, level, step):
        stride, size = self.strides[level], self.sizes[level]
        out = []
        for w in range(self.wide):
            z, x = divmod(w, 2)
            digit = z // stride % size
            to = z + ((digit + step) % size - digit) * stride
            out.append((w, to * 2 + x))
        return out

    def across(self, value, way):
        out = lax.ppermute(after(value, *self.sent[:-1]), BOTH, way)
        self.sent = [*self.sent, out][-2:]
        return out

    def over_core(self, value):
        return lax.ppermute(value, "narrow", self.core)

    def along(self, shard):
        held = shard[None]
        for level, size in enumerate(self.sizes):
            got = [lax.ppermute(held, "wide", self.shift(level, step)) for step in range(1, size)]
            held = stack(self.place, level, [held, *got])
        return held

    def swap(self, a, b):
        first = self.c == 0
        return jnp.where(first, a, b), jnp.where(first, b, a)


class Gather:
    def __init__(self, net, shard, extra=0, before=()):
        self.net, self.extra = net, extra
        self.held = net.along(after(shard, *before))

    def start(self, *others):
        net, held = self.net, after(self.held, *others)
        self.one, self.two = net.across(held, net.first), net.across(held, net.second)
        return self

    def turn(self, *others):
        self.three = self.net.across(after(self.one, *others), self.net.second)
        return self

    def end(self, *others):
        net = self.net
        three = after(self.three, *others)
        out = []
        for full in assemble(net.place, self.held, self.one, self.two, three, self.extra):
            mine = full.reshape((2, -1) + full.shape[4:])
            out.append((mine, net.over_core(mine)))
        return out if self.extra else out[0]


class Reduction:
    def __init__(self, net, name, products, more=None):
        self.net, self.name, self.products, self.more = net, name, products, more
        self.got = net.over_core(self.all_rows())

    def sizes(self):
        return [r.shape[-1] // (2 if r.ndim == 3 else 4) for _, r in self.products]

    def rights(self, src, y):
        ins = []
        for (_, right), size in zip(self.products, self.sizes()):
            if right.ndim == 3:
                ins.append((right, (1, right.shape[1], size), lambda *a: (src, 0, y(a[-1]))))
            else:
                ins.append(
                    (right, (right.shape[0], size), lambda *a: (0, 2 * y(a[-1]) + (a[-1][2] ^ src)))
                )
        return ins

    def all_rows(self):
        net, sizes = self.net, self.sizes()
        cols, count = sum(sizes), len(sizes)
        rows = self.products[0][0].shape[0] // net.wide
        extra = self.more[1].shape[2] if self.more else 0
        group = max(1, min(net.wide, 256 // rows))
        ins = []
        for left, _ in self.products:
            view = left.reshape(net.wide, rows, -1)
            ins.append((view, (group,) + view.shape[1:], lambda s, at: (s, 0, 0)))
        for y in range(2):
            ins += self.rights(1, lambda at, y=y: y)
        if extra:
            ins.append((self.more[1], (2, group, extra, cols), lambda s, at: (0, s, 0, 0)))

        def body(place, *refs):
            out = refs[-1]
            start = 0
            for i, size in enumerate(sizes):
                left = refs[i][...].reshape(group * rows, -1)
                for y in range(2):
                    right = refs[count + y * count + i]
                    right = right[0] if len(right.shape) == 3 else right[...]
                    value = dot(left, right).astype(LOW).reshape(group, rows, size)
                    out[y, :, :rows, start : start + size] = value
                start += size
            if extra:
                out[:, :, rows:, :] = refs[-2][...]

        shape = (2, net.wide, rows + extra, cols)
        (out,) = net_call(
            body,
            self.name + "_other",
            net.place,
            (net.wide // group,),
            ins,
            [(shape, LOW, (2, group, rows + extra, cols), lambda s, at: (0, s, 0, 0))],
        )
        return out

    def quarter(self, names, added, cut=None):
        net, sizes = self.net, self.sizes()
        cols, count = sum(sizes), len(sizes)
        lines = net.lines
        _, _, rows, _ = self.got.shape
        extra = self.more[0].shape[2] if self.more else 0
        rows -= extra
        got = self.got.reshape(2, lines, 2, rows + extra, cols)
        ins = []
        for dy, dx in names:

            def column(at, dy=dy):
                return at[0] ^ dy(at[2])

            def row(at, dx=dx):
                return at[1] ^ dx(at[2])

            def corner(s, at, column=column, row=row):
                return (column(at), 0, row(at), 0, 0)

            for left, _ in self.products:
                view = left.reshape(lines, 2, rows, -1)
                block = (lines, 1) + view.shape[2:]
                ins.append((view, block, lambda s, at, row=row: (0, row(at), 0, 0)))
            ins += self.rights(0, column)
            ins.append((got, (1, lines, 1, rows + extra, cols), corner))
            if extra:
                view = self.more[0].reshape(2, lines, 2, extra, cols)
                ins.append((view, (1, lines, 1, extra, cols), corner))
        each = len(ins) // len(names)
        ins += [(a, a.shape, lambda *_: (0, 0, 0)) for a in added]
        scratch = []
        shape = (lines, rows + extra, cols)
        if cut is None:
            outs = [(shape, LOW, shape, lambda *_: (0, 0, 0)) for _ in names]
        else:
            piece = (lines // net.sizes[cut],) + shape[1:]
            outs = [(piece, LOW, piece, lambda *_: (0, 0, 0)) for _ in range(net.sizes[cut])]
            scratch = [pltpu.VMEM(shape, LOW)]

        def body(place, *refs):
            for q in range(len(names)):
                mine = refs[q * each : (q + 1) * each]
                to = refs[len(ins) + q] if cut is None else refs[-1]
                start = 0
                for i, size in enumerate(sizes):
                    left, right = mine[i], mine[count + i]
                    right = right[0] if len(right.shape) == 3 else right[...]
                    value = dot(left[:, 0].reshape(lines * rows, -1), right)
                    at = (slice(None), slice(0, rows), slice(start, start + size))
                    value = value.reshape(lines, rows, size)
                    value += mine[2 * count][0, :, 0, :rows, start : start + size].astype(FULL)
                    for more in refs[each * len(names) : len(ins)]:
                        value += more[at].astype(FULL)
                    to[at] = value.astype(LOW)
                    start += size
                if extra:
                    value = mine[2 * count][0, :, 0, rows:, :].astype(FULL)
                    value += mine[2 * count + 1][0, :, 0].astype(FULL)
                    for more in refs[each * len(names) : len(ins)]:
                        value += more[:, rows:, :].astype(FULL)
                    to[:, rows:, :] = value.astype(LOW)
            if cut is not None:
                size = net.sizes[cut]
                stride = lines // size
                for k in range(size):
                    digit = lax.rem(place[3 + cut] + k, size)
                    refs[len(ins) + k][...] = refs[-1][pl.ds(digit * stride, stride)]

        return net_call(body, self.name, net.place, (1,), ins, outs, scratch)

    def start(self, *others):
        net = self.net
        self.got = after(self.got, *others)
        far, half = self.quarter((FAR, HALF), ())
        self.far, self.half = net.across(far, net.second), net.across(half, net.second)
        return self

    def turn(self, *others):
        net = self.net
        (near,) = self.quarter((NEAR,), (after(self.far, *others),))
        self.near = net.across(near, net.first)
        return self

    def end(self, *others):
        net = self.net
        last = len(net.sizes) - 1
        parts = self.quarter((OWN,), (self.half, after(self.near, *others)), last)
        for level in range(last, -1, -1):
            if level < last:
                parts = deal(net.place, level, net.sizes[level], parts)
            parts = [parts[0]] + [
                lax.ppermute(part, "wide", net.shift(level, step))
                for step, part in enumerate(parts[1:], 1)
            ]
        self.parts = parts
        return self

    def result(self):
        return sum(part[0].astype(FULL) for part in self.parts)


def net_call(body, name, place, grid, ins, outs, scratch=()):
    moved = sum(math.prod(b) * a.dtype.itemsize for a, b, _ in ins) * math.prod(grid)
    return pl.pallas_call(
        body,
        grid_spec=pltpu.PrefetchScalarGridSpec(
            num_scalar_prefetch=1,
            grid=grid,
            in_specs=[pl.BlockSpec(b, m) for _, b, m in ins],
            out_specs=[pl.BlockSpec(b, m) for _, _, b, m in outs],
            scratch_shapes=list(scratch),
        ),
        out_shape=[jax.ShapeDtypeStruct(s, d) for s, d, _, _ in outs],
        compiler_params=pltpu.CompilerParams(
            dimension_semantics=("arbitrary",) * len(grid), vmem_limit_bytes=VMEM_BYTES
        ),
        cost_estimate=pl.CostEstimate(flops=moved, bytes_accessed=2 * moved, transcendentals=0),
        name=name,
    )(place, *(a for a, _, _ in ins))


def stack(place, level, pieces):
    size, shape = len(pieces), pieces[0].shape

    def body(place, *refs):
        for step in range(size):

            @pl.when(pl.program_id(0) == step)
            def _(step=step):
                refs[-1][0] = refs[step][...]

    (out,) = net_call(
        body,
        "stack",
        place,
        (size,),
        [(p, shape, lambda *_: (0, 0, 0)) for p in pieces],
        [
            (
                (size,) + shape,
                pieces[0].dtype,
                (1,) + shape,
                lambda s, at: (lax.rem(at[3 + level] - s + size, size), 0, 0, 0),
            )
        ],
    )
    return out.reshape((-1,) + shape[1:])


def assemble(place, held, one, two, three, extra):
    lines, rows, cols = held.shape
    rows = (rows - extra, extra) if extra else (rows,)

    def body(place, *refs):
        for step in range(4):

            @pl.when(pl.program_id(0) == step)
            def _(step=step):
                start = 0
                for out, count in zip(refs[4:], rows):
                    out[0, :, 0] = refs[step][:, start : start + count]
                    start += count

    def index(s, at):
        dy = jnp.where(s == 0, 0, jnp.where(s == 1, at[2], jnp.where(s == 2, 1 - at[2], 1)))
        dx = jnp.where(s == 0, 0, jnp.where(s == 1, 1 - at[2], jnp.where(s == 2, at[2], 1)))
        return (at[0] ^ dy, 0, at[1] ^ dx, 0, 0)

    return net_call(
        body,
        "assemble",
        place,
        (4,),
        [(p, p.shape, lambda *_: (0, 0, 0)) for p in (held, one, two, three)],
        [((2, lines, 2, r, cols), held.dtype, (1, lines, 1, r, cols), index) for r in rows],
    )


OWN = (lambda c: 0, lambda c: 0)
FAR = (lambda c: 1, lambda c: 1)
HALF = (lambda c: 1 - c, lambda c: c)
NEAR = (lambda c: c, lambda c: 1 - c)


def deal(place, level, size, parts):
    count, rows, cols = parts[0].shape
    stride = count // size

    def source(s, at):
        return (lax.rem(at[3 + level] + lax.div(s, stride), size) * stride + lax.rem(s, stride), 0, 0)

    def body(place, *refs):
        total = sum(ref[0].astype(FULL) for ref in refs[: len(parts)]).astype(parts[0].dtype)
        for k, out in enumerate(refs[len(parts) :]):

            @pl.when(lax.div(pl.program_id(0), stride) == k)
            def _(out=out):
                out[0] = total

    outs = []
    for k in range(size):

        def target(s, at, k=k):
            return (jnp.clip(s - k * stride, 0, stride - 1), 0, 0)

        outs.append(((stride, rows, cols), parts[0].dtype, (1, rows, cols), target))
    return net_call(
        body, "deal", place, (count,), [(p, (1, rows, cols), source) for p in parts], outs
    )


def call(body, name, which, grid, ins, outs, scratch=(), flops=0):
    moved = sum(a.size * a.dtype.itemsize for a, _, _ in ins)
    moved += sum(math.prod(s) * jnp.dtype(d).itemsize for s, d, _, _ in outs)
    return pl.pallas_call(
        body,
        grid_spec=pltpu.PrefetchScalarGridSpec(
            num_scalar_prefetch=1,
            grid=grid,
            in_specs=[pl.BlockSpec(b, m) for _, b, m in ins],
            out_specs=[pl.BlockSpec(b, m) for _, _, b, m in outs],
            scratch_shapes=list(scratch),
        ),
        out_shape=[jax.ShapeDtypeStruct(s, d) for s, d, _, _ in outs],
        compiler_params=pltpu.CompilerParams(
            dimension_semantics=("arbitrary",) * len(grid), vmem_limit_bytes=VMEM_BYTES
        ),
        cost_estimate=pl.CostEstimate(flops=flops, bytes_accessed=moved, transcendentals=0),
        name=name,
    )(which, *(a for a, _, _ in ins))


def whole(array):
    return (array, array.shape, lambda *_: (0,) * array.ndim)


def whole_out(shape, dtype):
    return (shape, dtype, shape, lambda *_: (0,) * len(shape))


def block_at(step, c):
    return 2 * lax.rem(step, 2) + (lax.div(step, 2) ^ c[0])


def mine_at(col=0, first=0):
    return lambda s, c: (jnp.clip(s - first, 0, 1), 0, col)


def other_at(col=0, first=0):
    return lambda s, c: (jnp.clip(s - first - 2, 0, 1), 0, col)


def lanes(index, size):
    return pl.ds(pl.multiple_of(index * size, 128), size)


def dot(a, b):
    return jnp.dot(a, b, preferred_element_type=FULL)


def dot_t(a, b):
    return lax.dot_general(a, b, (((1,), (1,)), ((), ())), preferred_element_type=FULL)


def t_dot(a, b):
    return lax.dot_general(a, b, (((0,), (0,)), ((), ())), preferred_element_type=FULL)


def norm_parts(z):
    centred = z - jnp.mean(z, axis=-1, keepdims=True)
    scale = lax.rsqrt(jnp.mean(centred * centred, axis=-1, keepdims=True) + EPS)
    return centred * scale, scale


def norm(z, vec, which):
    unit, _ = norm_parts(z)
    return unit * vec[GAIN + which : GAIN + which + 1] + vec[SHIFT + which : SHIFT + which + 1]


def norm_back(upstream, z, gain):
    unit, scale = norm_parts(z)
    d_gain = jnp.sum(upstream * unit, axis=0, keepdims=True)
    d_shift = jnp.sum(upstream, axis=0, keepdims=True)
    inner = upstream * gain
    mean = jnp.mean(inner, axis=-1, keepdims=True)
    along = jnp.mean(inner * unit, axis=-1, keepdims=True)
    return scale * (inner - mean - unit * along), d_gain, d_shift


def column_sum(values):
    return jnp.sum(values.astype(FULL), axis=0, keepdims=True)


def either(step, mine, other, then):
    pl.when(step < 2)(lambda: then(mine))
    pl.when(step >= 2)(lambda: then(other))


def two_heads(rows):
    low = lax.broadcasted_iota(jnp.int32, rows.shape, 1) < HD
    none = jnp.zeros_like(rows)
    return jnp.concatenate([jnp.where(low, rows, none), jnp.where(low, none, rows)], axis=0)


def one_row(stacked):
    half = stacked.shape[0] // 2
    low = lax.broadcasted_iota(jnp.int32, (half, PAIR), 1) < HD
    return jnp.where(low, stacked[:half], stacked[half:])


def softmax_rows(query, keys, allowed):
    logits = jnp.where(allowed, dot_t(two_heads(query), keys) * HD ** (-0.5), MASKED_SCORE)
    weight = jnp.exp(logits - jnp.max(logits, axis=-1, keepdims=True))
    return (weight * (1.0 / jnp.sum(weight, axis=-1, keepdims=True))).astype(LOW)


def attend_back(query, keys, values, probs, upstream):
    queries, ups = two_heads(query), two_heads(upstream)
    wide_probs = probs.astype(FULL)
    d_probs = dot_t(ups, values)
    row_dot = jnp.sum(wide_probs * d_probs, axis=-1, keepdims=True)
    d_scores = (wide_probs * (d_probs - row_dot)).astype(LOW)
    scale = HD ** (-0.5)
    return one_row(dot(d_scores, keys)) * scale, t_dot(d_scores, queries) * scale, t_dot(probs, ups)


def twice(a):
    return jnp.concatenate([a, a], axis=0)


def attend_self(seg_col, seg_row, joined, probs, mix):
    width, rows = mix.shape[1], seg_row.shape[-1]
    below = lax.broadcasted_iota(jnp.int32, (rows, rows), 0) >= lax.broadcasted_iota(
        jnp.int32, (rows, rows), 1
    )
    for p in range(mix.shape[0] // rows):
        at = pl.ds(p * rows, rows)
        allowed = twice(jnp.where((seg_col[at, :] == seg_row[p]) & below, 1, 0)) == 1
        for h in range(width // PAIR):
            q, k, v = (joined[at, pl.ds(i * width + h * PAIR, PAIR)] for i in range(3))
            low = softmax_rows(q, k, allowed)
            probs[pl.ds((p * (width // PAIR) + h) * 2 * rows, 2 * rows), :] = low
            mix[at, pl.ds(h * PAIR, PAIR)] = one_row(dot(low, v)).astype(LOW)


def self_forward(c, x, mine, other, bias, seg_col, seg_row, joined, probs, mix, x_t, mix_t):
    step = pl.program_id(0)
    at = lanes(block_at(step, c), mine.shape[-1])

    def put(w):
        joined[:, at] = (dot(x[...], w[0]) + bias[:, at]).astype(LOW)

    either(step, mine, other, put)

    @pl.when(step == 3)
    def _():
        attend_self(seg_col, seg_row, joined, probs, mix)
        x_t[...] = x[...].T
        mix_t[...] = mix[...].T


def first_half(c, mix, mine, other, x, vec, first_sum, low_t, query, first_low, acc):
    step = pl.program_id(0)
    at = lanes(block_at(lax.rem(step, 4), c), mine.shape[-1])

    def put_sum(w):
        acc[:, at] = dot(mix[...], w[0])

    def put_query(w):
        query[:, at] = (dot(first_low[...], w[0]) + vec[B_CROSS_Q : B_CROSS_Q + 1, at]).astype(LOW)

    pl.when(step < 4)(lambda: either(step, mine, other, put_sum))

    @pl.when(step == 3)
    def _():
        z = x[...].astype(FULL) + (acc[...] + vec[B_SELF_OUT : B_SELF_OUT + 1, :])
        first_sum[...] = z
        low = norm(z, vec, 0).astype(LOW)
        first_low[...] = low
        low_t[...] = low.T

    pl.when(step >= 4)(lambda: either(step - 4, mine, other, put_query))


def table_keys(c, x, mine, other, vec, out, x_t):
    half = out.shape[-1] // 2
    for src, w in enumerate((mine, other)):
        bias = vec[B_CROSS_V : B_CROSS_V + 1, lanes(c[0] ^ src, half)]
        out[src, :, :half] = dot(x[...], w[0]).astype(LOW)
        out[src, :, half:] = (dot(x[...], w[1]) + bias).astype(LOW)
    x_t[...] = x[...].T


def cross_forward(c, query, kv, table_col, table_row, mix, probs, mix_t):
    rows, half = query.shape
    allowed = twice(jnp.where(table_col[...] == table_row[0], 1, 0)) == 1
    for h in range(half // PAIR):
        at = pl.ds(h * PAIR, PAIR)
        low = softmax_rows(query[:, at], kv[0, :, at], allowed)
        probs[0, 0, pl.ds(h * 2 * rows, 2 * rows), :] = low
        mixed = one_row(dot(low, kv[0, :, pl.ds(half + h * PAIR, PAIR)])).astype(LOW)
        mix[:, at] = mixed
        mix_t[at, :] = mixed.T


def second_half(c, mix, mine, other, first_sum, vec, second_sum, second_low, low_t, acc):
    step = pl.program_id(0)
    at = lanes(block_at(step, c), mine.shape[-1])

    def put(w):
        acc[:, at] = dot(mix[...], w[0])

    either(step, mine, other, put)

    @pl.when(step == 3)
    def _():
        z = norm(first_sum[...], vec, 0) + (acc[...] + vec[B_CROSS_OUT : B_CROSS_OUT + 1, :])
        second_sum[...] = z
        low = norm(z, vec, 1).astype(LOW)
        second_low[...] = low
        low_t[...] = low.T


def feed_in(c, x, mine, other, bias, active, slope, active_t):
    def put(w):
        hidden = dot(x[...], w[0]) + bias[...]
        share = 0.5 + 0.5 * lax.erf(hidden * 2 ** (-0.5))
        low = (hidden * share).astype(LOW)
        active[...] = low
        active_t[...] = low.T
        density = jnp.exp(hidden * hidden * (-0.5)) * (2 * math.pi) ** (-0.5)
        slope[...] = (share + hidden * density).astype(LOW)

    either(pl.program_id(0), mine, other, put)


def feed_out(c, active, mine, other, second_sum, cotangent, vec, output, d_third, d_low, grads, acc):
    step = pl.program_id(0)
    at = lanes(block_at(step, c), mine.shape[-1])

    def put(w):
        acc[:, at] = dot(active[...], w[0])

    either(step, mine, other, put)

    @pl.when(step == 3)
    def _():
        z = norm(second_sum[...], vec, 1) + (acc[...] + vec[B_FC_OUT : B_FC_OUT + 1, :])
        output[...] = norm(z, vec, 2).astype(LOW)
        back, d_gain, d_shift = norm_back(cotangent[...].astype(FULL), z, vec[GAIN + 2 : GAIN + 3])
        d_third[...] = back
        low = back.astype(LOW)
        d_low[...] = low
        grads[0:1, :] = column_sum(low)
        grads[1:2, :] = d_shift
        grads[2:3, :] = d_gain


def through(c, rows, mine, other):
    cols = mine.shape[-1]
    total = 0
    for step in range(4):
        w = (mine, other)[step // 2]
        total += dot_t(rows[:, lanes(block_at(step, c), cols)], w[step % 2])
    return total


def feed_out_back(c, d_third, mine, other, slope, d_hidden, grads):
    low = (slope[...].astype(FULL) * through(c, d_third, mine, other)).astype(LOW)
    d_hidden[...] = low
    grads[...] = column_sum(low)


def feed_in_back(
    c, d_hidden, mine, other, d_third, second_sum, vec, out_mine, out_other,
    d_sum, d_low, d_mix, grads, acc,
):
    step = pl.program_id(0)

    @pl.when(step == 0)
    def _():
        acc[...] = d_third[...]

    def add(w):
        acc[...] += dot_t(d_hidden[...], w[0])

    either(step, mine, other, add)

    @pl.when(step == 3)
    def _():
        back, d_gain, d_shift = norm_back(acc[...], second_sum[...], vec[GAIN + 1 : GAIN + 2])
        d_sum[...] = back
        low = back.astype(LOW)
        d_low[...] = low
        grads[0:1, :] = column_sum(low)
        grads[1:2, :] = d_shift
        grads[2:3, :] = d_gain
        d_mix[...] = through(c, d_low, out_mine, out_other).astype(LOW)


def cross_backward(c, query, kv, probs, d_mix, d_query, d_kv, grads):
    rows, half = query.shape
    for h in range(half // PAIR):
        at, beside = pl.ds(h * PAIR, PAIR), pl.ds(half + h * PAIR, PAIR)
        dq, dk, dv = attend_back(
            query[:, at],
            kv[0, :, at],
            kv[0, :, beside],
            probs[0, 0, pl.ds(h * 2 * rows, 2 * rows), :],
            d_mix[:, at],
        )
        d_query[:, at] = dq.astype(LOW)
        d_kv[0, :, at] = dk.astype(LOW)
        low = dv.astype(LOW)
        d_kv[0, :, beside] = low
        sums = column_sum(low)
        before = jnp.where(pl.program_id(1) == 0, 0.0, grads[0, :, at])
        grads[0, :, at] = before + sums


def self_backward(
    c, d_query, q_mine, q_other, d_sum2, first_sum, vec, out_mine, out_other, joined, probs,
    d_sum, d_low, d_joined, grads,
):
    width = d_sum.shape[-1]
    upstream = d_sum2[...] + through(c, d_query, q_mine, q_other)
    back, d_gain, d_shift = norm_back(upstream, first_sum[...], vec[GAIN : GAIN + 1])
    d_sum[...] = back
    low = back.astype(LOW)
    d_low[...] = low
    d_mix = through(c, d_low, out_mine, out_other).astype(LOW)
    rows = probs.shape[-1]
    heads = width // PAIR
    for p in range(d_sum.shape[0] // rows):
        at = pl.ds(p * rows, rows)
        for h in range(heads):
            where = [pl.ds(i * width + h * PAIR, PAIR) for i in range(3)]
            q, k, v = (joined[at, w] for w in where)
            found = attend_back(
                q,
                k,
                v,
                probs[pl.ds((p * heads + h) * 2 * rows, 2 * rows), :],
                d_mix[p * rows : (p + 1) * rows, h * PAIR : (h + 1) * PAIR],
            )
            for w, value in zip(where, found):
                d_joined[at, w] = value.astype(LOW)
    grads[0:1, :] = column_sum(d_joined[:, :width])
    grads[1:2, :] = column_sum(d_joined[:, 2 * width :])
    grads[2:3, :] = column_sum(low)
    grads[3:4, :] = column_sum(d_query[...])
    grads[4:5, :] = d_shift
    grads[5:6, :] = d_gain


def input_back(c, d_joined, mine, other, d_sum, out):
    @pl.when(pl.program_id(0) == 0)
    def _():
        out[...] = d_sum[...]

    def add(w):
        out[...] += dot_t(d_joined[...], w[0])

    either(pl.program_id(0), mine, other, add)


def table_back(c, d_kv, mine, other, out):
    half = mine.shape[-1]
    total = 0
    for src, w in enumerate((mine, other)):
        for y in range(2):
            total += dot_t(d_kv[src, :, y * half : (y + 1) * half], w[y])
    out[...] = total


def segment_index(lengths, count):
    segment_ends = jnp.cumsum(lengths, axis=-1)
    position = jnp.arange(count, dtype=jnp.int32)
    passed = (position[None, :, None] >= segment_ends[:, None, :]).astype(jnp.int32)
    return jnp.sum(passed, axis=-1)


def per_device(
    inputs,
    memory,
    cotangent,
    dec_lengths,
    mem_lengths,
    seg_table,
    self_qkv,
    self_out,
    cross_q,
    cross_kv,
    cross_out,
    fc_in,
    fc_out,
    vec_bias,
    norm_gain,
    fc_in_bias,
    *,
    wide,
    narrow,
):
    net = Net(wide, narrow)
    which = net.which
    pairs, length, width = inputs.shape
    held = memory.shape[1]
    x = inputs.reshape(-1, width)
    table = memory.reshape(-1, width)
    upstream = cotangent.reshape(-1, width)
    count, quarter, half = x.shape[0], width // narrow, width // 2
    hidden = fc_out.shape[0] * wide

    segments = segment_index(dec_lengths, length)
    tables = segment_index(mem_lengths, held)
    matches = segments[:, :, None] == jnp.arange(dec_lengths.shape[-1], dtype=jnp.int32)
    query_table = jnp.sum(jnp.where(matches, seg_table[:, None, :], 0), axis=-1)
    seg_col, seg_row = segments.reshape(-1, 1), segments.reshape(pairs, 1, length)
    table_col, table_row = query_table.reshape(-1, 1), tables.reshape(pairs, 1, held)

    rows = jnp.concatenate([vec_bias, norm_gain])
    small = jnp.concatenate([rows.reshape(-1), fc_in_bias])
    extra = 16
    small_rows = jnp.zeros((extra, self_qkv.shape[1]), LOW).at[0, : small.size].set(small)
    g1 = Gather(net, jnp.concatenate([self_out, cross_q], axis=1)).start()
    g2 = Gather(net, jnp.concatenate([self_qkv, small_rows]), extra, (g1.held,))
    g1.turn(g2.held)
    w_near = g1.end()
    g2.start()
    g3 = Gather(net, jnp.concatenate([cross_kv, cross_out], axis=1), 0, (g2.held,))
    g2.turn(g3.held)
    w_qkv, vectors = g2.end()
    g3.start()
    g4 = Gather(net, fc_in, 0, (g3.held,))
    g3.turn(g4.held)
    w_far = g3.end()
    g4.start()
    g5 = Gather(net, fc_out, 0, (g4.held,))
    g4.turn(g5.held)
    w_in = g4.end()
    w_out = g5.start().turn().end()

    def by_device(pair):
        both = jnp.stack(net.swap(*pair), axis=1).reshape(narrow, wide, extra, -1)
        return jnp.swapaxes(both[:, :, 0, : small.size], 0, 1).reshape(wide * narrow, -1)

    vectors = by_device(vectors).astype(FULL)
    fc_bias = vectors[:, rows.size :].reshape(1, -1)
    vec = vectors[:, : rows.size].reshape(wide * narrow, rows.shape[0], -1)
    vec = jnp.transpose(vec, (1, 0, 2)).reshape(rows.shape[0], width)
    joined_bias = jnp.concatenate([vec[0], jnp.zeros((width,), FULL), vec[1]])[None]

    def steps(weights, col=0, block=None, first=0):
        block = block or weights[0].shape[2]
        shape = (1, weights[0].shape[1], block)
        return [
            (weights[0], shape, mine_at(col, first)),
            (weights[1], shape, other_at(col, first)),
        ]

    def all_of(weights, col, block):
        shape = (2, weights[0].shape[1], block)
        return [(w, shape, lambda *_: (0, 0, col)) for w in weights]

    heads = width // PAIR
    joined, self_probs, self_mix, x_t, self_mix_t = call(
        self_forward,
        "self_forward",
        which,
        (4,),
        [whole(x), *steps(w_qkv), whole(joined_bias), whole(seg_col), whole(seg_row)],
        [
            whole_out((count, 3 * width), LOW),
            whole_out((pairs * heads * 2 * length, length), LOW),
            whole_out((count, width), LOW),
            whole_out((width, count), LOW),
            whole_out((width, count), LOW),
        ],
        flops=2 * count * width * 3 * width,
    )

    def so_q(side):
        def index(s, c):
            low = 2 * side
            later = s >= 4
            step = jnp.where(later, s - 4, s)
            return (jnp.clip(step - low, 0, 1), 0, jnp.where(later, 1, 0))

        return index

    first_sum, first_low_t, query = call(
        first_half,
        "first_half",
        which,
        (8,),
        [
            whole(self_mix),
            *((w_near[i], (1, width, quarter), so_q(i)) for i in range(2)),
            whole(x),
            whole(vec),
        ],
        [
            whole_out((count, width), FULL),
            whole_out((width, count), LOW),
            whole_out((count, width), LOW),
        ],
        [pltpu.VMEM((count, width), LOW), pltpu.VMEM((count, width), FULL)],
        flops=4 * count * width * width,
    )
    tile = 512
    kv, table_t = call(
        table_keys,
        "table_keys",
        which,
        (table.shape[0] // tile,),
        [
            (table, (tile, width), lambda t, c: (t, 0)),
            *all_of(w_far, 0, half),
            whole(vec),
        ],
        [
            ((2, table.shape[0], width), LOW, (2, tile, width), lambda t, c: (0, t, 0)),
            ((width, table.shape[0]), LOW, (width, tile), lambda t, c: (0, t)),
        ],
        flops=4 * table.shape[0] * width * width,
    )
    core_block = ((length, half), lambda s, p, c: (p, c[0] ^ s))
    kv_block = ((1, held, width), lambda s, p, c: (s, p, 0))
    score_rows = half // PAIR * 2 * length
    probs_shape = (2, pairs, score_rows, held)
    probs_block = ((1, 1, score_rows, held), lambda s, p, c: (s, p, 0, 0))
    cross_mix, cross_probs, cross_mix_t = call(
        cross_forward,
        "cross_forward",
        which,
        (2, pairs),
        [
            (query, *core_block),
            (kv, *kv_block),
            (table_col, (length, 1), lambda s, p, c: (p, 0)),
            (table_row, (1, 1, held), lambda s, p, c: (p, 0, 0)),
        ],
        [
            ((count, width), LOW, *core_block),
            (probs_shape, LOW, *probs_block),
            ((width, count), LOW, (half, length), lambda s, p, c: (c[0] ^ s, p)),
        ],
        flops=8 * count * held * width,
    )
    second_sum, second_low, second_low_t = call(
        second_half,
        "second_half",
        which,
        (4,),
        [whole(cross_mix), *steps(w_far, 2, quarter), whole(first_sum), whole(vec)],
        [
            whole_out((count, width), FULL),
            whole_out((count, width), LOW),
            whole_out((width, count), LOW),
        ],
        [pltpu.VMEM((count, width), FULL)],
        flops=2 * count * width * width,
    )
    hidden_block = ((count, hidden // 4), lambda s, c: (0, block_at(s, c)))
    active, slope, active_t = call(
        feed_in,
        "feed_in",
        which,
        (4,),
        [
            whole(second_low),
            *steps(w_in),
            (fc_bias, (1, hidden // 4), lambda s, c: (0, block_at(s, c))),
        ],
        [
            ((count, hidden), LOW, *hidden_block),
            ((count, hidden), LOW, *hidden_block),
            ((hidden, count), LOW, (hidden // 4, count), lambda s, c: (block_at(s, c), 0)),
        ],
        flops=2 * count * width * hidden,
    )
    output, d_third, d_low3, grads3 = call(
        feed_out,
        "feed_out",
        which,
        (4,),
        [whole(active), *steps(w_out), whole(second_sum), whole(upstream), whole(vec)],
        [
            whole_out((count, width), LOW),
            whole_out((count, width), FULL),
            whole_out((count, width), LOW),
            whole_out((8, width), FULL),
        ],
        [pltpu.VMEM((count, width), FULL)],
        flops=2 * count * width * hidden,
    )

    r_out = Reduction(net, "grad_out", [(active_t, d_low3)])
    tile = hidden // 4
    d_hidden, g_fc_bias = call(
        feed_out_back,
        "feed_out_back",
        which,
        (4,),
        [
            whole(d_low3),
            *((w, (2, tile, quarter), lambda t, c: (0, t, 0)) for w in w_out),
            (slope, (count, tile), lambda t, c: (0, t)),
        ],
        [
            ((count, hidden), LOW, (count, tile), lambda t, c: (0, t)),
            ((1, hidden), FULL, (1, tile), lambda t, c: (0, t)),
        ],
        flops=2 * count * width * hidden,
    )
    r_out.start().turn().end()
    r_in = Reduction(net, "grad_in", [(second_low_t, d_hidden)]).start().turn().end()
    d_sum2, d_low2, d_mix, grads2 = call(
        feed_in_back,
        "feed_in_back",
        which,
        (4,),
        [
            (d_hidden, *hidden_block),
            *steps(w_in),
            whole(d_third),
            whole(second_sum),
            whole(vec),
            *all_of(w_far, 2, quarter),
        ],
        [
            whole_out((count, width), FULL),
            whole_out((count, width), LOW),
            whole_out((count, width), LOW),
            whole_out((8, width), FULL),
        ],
        [pltpu.VMEM((count, width), FULL)],
        flops=2 * count * width * (hidden + width),
    )
    d_query, d_kv, grads_v = call(
        cross_backward,
        "cross_backward",
        which,
        (2, pairs),
        [
            (query, *core_block),
            (kv, *kv_block),
            (cross_probs, *probs_block),
            (d_mix, *core_block),
        ],
        [
            ((count, width), LOW, *core_block),
            (kv.shape, LOW, *kv_block),
            ((2, 1, half), FULL, (1, 1, half), lambda s, p, c: (s, 0, 0)),
        ],
        flops=16 * count * held * width,
    )
    r_cross = Reduction(net, "grad_cross", [(table_t, d_kv), (cross_mix_t, d_low2)])
    r_cross.start(*r_out.parts).turn().end()
    d_sum1, d_low1, d_joined, grads1 = call(
        self_backward,
        "self_backward",
        which,
        (1,),
        [
            whole(d_query),
            *all_of(w_near, 1, quarter),
            whole(d_sum2),
            whole(first_sum),
            whole(vec),
            *all_of(w_near, 0, quarter),
            whole(joined),
            whole(self_probs),
        ],
        [
            whole_out((count, width), FULL),
            whole_out((count, width), LOW),
            whole_out((count, 3 * width), LOW),
            whole_out((8, width), FULL),
        ],
        flops=4 * count * width * width,
    )
    r_self = Reduction(net, "grad_self", [(self_mix_t, d_low1), (first_low_t, d_query)])
    r_self.start(*r_in.parts).turn().end()

    grads_v = jnp.concatenate(net.swap(grads_v[0], grads_v[1]), axis=1)
    g_rows = jnp.concatenate(
        [
            grads1[:4],
            grads_v,
            grads2[:1],
            grads3[:1],
            grads1[4:5],
            grads2[1:2],
            grads3[1:2],
            grads1[5:6],
            grads2[2:3],
            grads3[2:3],
        ]
    )
    g_rows = jnp.transpose(g_rows.reshape(rows.shape[0], wide, narrow, -1), (2, 1, 0, 3))
    g_small = jnp.transpose(g_fc_bias.reshape(wide, narrow, -1), (1, 0, 2))
    g_small = jnp.concatenate([g_rows.reshape(narrow, wide, -1), g_small], axis=2).astype(LOW)
    g_small = jnp.pad(
        g_small[:, :, None],
        ((0, 0), (0, 0), (0, extra - 1), (0, self_qkv.shape[1] - small.size)),
    )
    g_small = g_small.reshape(2, 2, wide, extra, -1)
    r_qkv = Reduction(
        net,
        "grad_qkv",
        [(x_t, d_joined)],
        net.swap(g_small[:, 0], g_small[:, 1]),
    )
    r_qkv.start(*r_cross.parts).turn().end()
    (input_grad,) = call(
        input_back,
        "input_back",
        which,
        (4,),
        [
            (d_joined, (count, 3 * quarter), lambda s, c: (0, block_at(s, c))),
            *steps(w_qkv),
            whole(d_sum1),
        ],
        [whole_out((count, width), FULL)],
        flops=2 * count * width * 3 * width,
    )
    tile = 512
    (memory_grad,) = call(
        table_back,
        "table_back",
        which,
        (table.shape[0] // tile,),
        [
            (d_kv, (2, tile, width), lambda t, c: (0, t, 0)),
            *all_of(w_far, 0, half),
        ],
        [(table.shape, FULL, (tile, width), lambda t, c: (t, 0))],
        flops=4 * table.shape[0] * width * width,
    )

    g_out, g_in, g_cross, g_self, g_qkv = (
        r.result() for r in (r_out, r_in, r_cross, r_self, r_qkv)
    )
    g_small = g_qkv[-extra, : small.size]
    g_rows, g_fc_bias = g_small[: rows.size].reshape(rows.shape), g_small[rows.size :]
    return (
        output.reshape(inputs.shape),
        input_grad.reshape(inputs.shape),
        memory_grad.reshape(memory.shape),
        g_qkv[:-extra],
        g_self[:, :quarter],
        g_self[:, quarter:],
        g_cross[:, : 2 * quarter],
        g_cross[:, 2 * quarter :],
        g_in,
        g_out,
        g_rows[:10],
        g_rows[10:],
        g_fc_bias,
    )


def solution(mesh):
    tokens = P(BOTH, None, None)
    lengths = P(BOTH, None)
    weight = P("wide", "narrow")
    vector = P(None, BOTH)
    return jax.shard_map(
        partial(per_device, wide=mesh.shape["wide"], narrow=mesh.shape["narrow"]),
        mesh=mesh,
        in_specs=(tokens,) * 3 + (lengths,) * 3 + (weight,) * 7 + (vector, vector, P(BOTH)),
        out_specs=(tokens,) * 3 + (weight,) * 7 + (vector, vector, P(BOTH)),
        check_vma=False,
    )
```

```python
import math
from functools import partial

import jax
import jax.numpy as jnp
from jax import lax
from jax.experimental import pallas as pl
from jax.experimental.pallas import tpu as pltpu
from jax.sharding import PartitionSpec as P

HD = 64
PAIR = 2 * HD
BOTH = ("wide", "narrow")
EPS = 1e-05
MASKED_SCORE = -1000000000.0
LOW = jnp.bfloat16
FULL = jnp.float32
VMEM_BYTES = 60 * 1024 * 1024
B_QUERY, B_VALUE, B_SELF_OUT, B_CROSS_Q, B_CROSS_V, B_CROSS_OUT, B_FC_OUT = range(7)
SHIFT, GAIN = 7, 10


def after(value, *others):
    return lax.optimization_barrier((value, others))[0]


class Order:
    last, soon, later = (), (), ()

    @classmethod
    def put(cls, kernel, arrays):
        first = after(arrays[0], *cls.last, *cls.soon)
        out = kernel(first, *arrays[1:])
        cls.last, cls.soon, cls.later = (out[0],), cls.later, ()
        return out

    @classmethod
    def now(cls, value, *others):
        return after(value, *cls.last, *others)

    @classmethod
    def need(cls, *arrays):
        cls.soon += arrays

    @classmethod
    def pin(cls, *arrays):
        cls.later += arrays
        return arrays


class Net:
    def __init__(self, wide, narrow):
        self.wide, self.narrow, self.lines = wide, narrow, wide // 2
        w, n = lax.axis_index("wide"), lax.axis_index("narrow")
        self.z, self.x, self.y, self.c = w // 2, w % 2, n // 2, n % 2
        self.place = jnp.stack([self.y, self.x, self.c, self.z]).astype(jnp.int32)
        both = [(i, j) for i in range(wide) for j in range(narrow)]

        def flat(i, j):
            return i * narrow + j

        def pairs(x_core):
            return [
                (flat(i, j), flat(i ^ 1, j) if j % 2 == x_core else flat(i, j ^ 2)) for i, j in both
            ]

        self.first, self.second = pairs(0), pairs(1)
        self.core = [(j, j ^ 1) for j in range(narrow)]
        self.groups = [[z * 2 + x for z in range(self.lines)] for x in range(2)]

    def across(self, value, way, *others):
        return lax.ppermute(Order.now(value, *others), BOTH, way)

    def over_core(self, value, *others):
        return lax.ppermute(Order.now(value, *others), "narrow", self.core)

    def along(self, value, step, *others):
        way = [(w, ((w // 2) ^ step) * 2 + w % 2) for w in range(self.wide)]
        return lax.ppermute(Order.now(value, *others), "wide", way)

    def swap(self, a, b):
        first = self.c == 0
        return jnp.where(first, a, b), jnp.where(first, b, a)


class Weight:
    def __init__(self, net, shard, before=()):
        self.net = net
        self.rows = shard.shape[0]
        self.shard = after(shard, *before)

    def at_once(self):
        self.held = lax.all_gather(
            self.shard, "wide", axis=0, axis_index_groups=self.net.groups
        )
        return self

    def line(self, *others):
        net = self.net
        if net.lines == 4:
            self.got = net.along(self.shard, 2, *others)
        return self

    def line_on(self):
        net = self.net
        if net.lines == 4:
            self.held = stack(net, [self.shard, self.got], 1)
            self.got = net.along(self.held, 1)
        return self

    def line_end(self):
        net = self.net
        if net.lines == 4:
            self.held = stack(net, [self.held, self.got], 0)
        else:
            self.at_once()
        return self

    def start(self):
        net = self.net
        self.one, self.two = net.across(self.held, net.first), net.across(self.held, net.second)
        return self

    def turn(self, *others):
        net = self.net
        self.three = net.across(self.one, net.second, self.two, *others)
        return self

    def copy(self, *names):
        new = [self.net.over_core(getattr(self, name)) for name in names]
        self.copies = [*getattr(self, "copies", ()), *new]
        return new

    @property
    def pieces(self):
        return [self.held, self.one, self.two, self.three, *self.copies]


def piece_place(place, index):
    side, k = divmod(index, 4)
    c = place[2] ^ side
    dy, dx = ((0, 0), (c, 1 - c), (1 - c, c), (1, 1))[k]
    return place[0] ^ dy, place[1] ^ dx, side


class Loaded:
    def __init__(self, place, pieces, buffer, sems, rows, col):
        self.buffer = buffer
        size = buffer.shape[-1]
        self.copies = []
        for i, piece in enumerate(pieces):
            y, x, side = piece_place(place, i)
            self.copies.append(
                pltpu.make_async_copy(
                    piece.at[:, pl.ds(0, rows), pl.ds(col, size)],
                    buffer.at[side, y, :, x],
                    sems.at[i],
                )
            )

    def start(self):
        for copy in self.copies:
            copy.start()

    def wait(self, side):
        for copy in self.copies[4 * side : 4 * side + 4]:
            copy.wait()

    def part(self, side, y):
        return self.buffer[side, y].reshape(-1, self.buffer.shape[-1])


class Reduction:
    def __init__(self, net, name, products, more=None, time=8):
        self.net = net
        self.pair, self.near, self.own = quarter_grads(net, name, products, more, time)

    def start(self, *others):
        self.pair = self.net.across(self.pair, self.net.second, *others)
        return self

    def turn(self):
        pair = Order.now(self.pair)
        ready = (self.near.astype(FULL) + pair[0].astype(FULL)).astype(LOW)
        Order.need(ready)
        self.near = self.net.across(ready, self.net.first)
        return self

    def line(self):
        net = self.net
        near = Order.now(self.near)
        total = self.own.astype(FULL) + self.pair[1].astype(FULL) + near.astype(FULL)
        self.total = total.astype(LOW)
        Order.need(self.total)
        self.step = net.along(self.total[total.shape[0] // 2 :], 1)
        return self

    def line_on(self):
        net = self.net
        half, step = self.total.shape[0] // 2, 2
        total = self.total[:half].astype(FULL) + Order.now(self.step).astype(FULL)
        while half > 2:
            half //= 2
            low = total.astype(LOW)
            got = net.along(low[half:], step)
            total = low[:half].astype(FULL) + got.astype(FULL)
            step *= 2
        self.total = total.astype(LOW)
        Order.need(self.total)
        if half > 1:
            self.step = net.along(self.total[1:], step)
        return self

    def line_end(self):
        total = self.total[0].astype(FULL)
        if self.total.shape[0] > 1:
            total += Order.now(self.step)[0].astype(FULL)
        self.total = total
        return self


def call(body, name, net, grid, ins, outs, scratch=(), weights=(), time=5):
    operands, specs, buffers = [], [], []
    for weight, _, size in weights:
        operands += weight.pieces
        specs += [pl.BlockSpec(memory_space=pl.ANY)] * 8
        shape = (2, 2, net.lines, 2, weight.rows, size)
        buffers += [pltpu.VMEM(shape, LOW), pltpu.SemaphoreType.DMA((8,))]
    plain = len(ins) + len(outs)

    def run(place, *refs):
        pieces, rest = refs[: len(operands)], refs[len(operands) :]
        held = rest[plain : plain + len(buffers)]
        rest = rest[:plain] + rest[plain + len(buffers) :]
        loaded = [
            Loaded(
                place,
                pieces[8 * i : 8 * i + 8],
                held[2 * i],
                held[2 * i + 1],
                weight.rows,
                col,
            )
            for i, (weight, col, _) in enumerate(weights)
        ]

        def start():
            for weight in loaded:
                weight.start()

        if grid == (1,):
            start()
        elif loaded:
            pl.when(pl.program_id(0) == 0)(start)
        body(place, *loaded, *rest)

    kernel = pl.pallas_call(
        run,
        grid_spec=pltpu.PrefetchScalarGridSpec(
            num_scalar_prefetch=1,
            grid=grid,
            in_specs=specs + [pl.BlockSpec(b, m) for _, b, m in ins],
            out_specs=[pl.BlockSpec(b, m) for _, _, b, m in outs],
            scratch_shapes=[*buffers, *scratch],
        ),
        out_shape=[jax.ShapeDtypeStruct(s, d) for s, d, _, _ in outs],
        compiler_params=pltpu.CompilerParams(
            dimension_semantics=("arbitrary",) * len(grid), vmem_limit_bytes=VMEM_BYTES
        ),
        cost_estimate=pl.CostEstimate(
            flops=time * 10**9, bytes_accessed=3 * time * 10**6, transcendentals=0
        ),
        name=name,
    )
    return Order.put(partial(kernel, net.place), [*operands, *(a for a, _, _ in ins)])


def stack(net, pieces, bit):
    rows, cols = pieces[0].shape[-2:]

    def body(place, *refs):
        for i in range(2):

            @pl.when(pl.program_id(0) == i)
            def _(i=i):
                refs[-1][:, 0] = refs[i][...].reshape(-1, rows, cols)

    lead = pieces[0].size // (rows * cols)
    shape = (lead, 2, rows, cols)
    (out,) = call(
        body,
        "stack",
        net,
        (2,),
        [whole(p) for p in pieces],
        [(shape, LOW, (lead, 1, rows, cols), lambda s, at: (0, ((at[3] >> bit) & 1) ^ s, 0, 0))],
        time=3,
    )
    return out.reshape(2 * lead, rows, cols)


def whole(array):
    return (array, array.shape, lambda *_: (0,) * array.ndim)


def whole_out(shape, dtype):
    return (shape, dtype, shape, lambda *_: (0,) * len(shape))


def lanes(index, size):
    return pl.ds(pl.multiple_of(index * size, 128), size)


def block_of(place, side, y):
    return 2 * y + (place[2] ^ side)


def each_block(place, weight, wait=True):
    for side in range(2):
        if wait:
            weight.wait(side)
        for y in range(2):
            yield side, y, block_of(place, side, y)


def dot(a, b):
    return jnp.dot(a, b, preferred_element_type=FULL)


def dot_t(a, b):
    return lax.dot_general(a, b, (((1,), (1,)), ((), ())), preferred_element_type=FULL)


def t_dot(a, b):
    return lax.dot_general(a, b, (((0,), (0,)), ((), ())), preferred_element_type=FULL)


def norm_parts(z):
    centred = z - jnp.mean(z, axis=-1, keepdims=True)
    scale = lax.rsqrt(jnp.mean(centred * centred, axis=-1, keepdims=True) + EPS)
    return centred * scale, scale


def norm(z, vec, which):
    unit, _ = norm_parts(z)
    return unit * vec[GAIN + which : GAIN + which + 1] + vec[SHIFT + which : SHIFT + which + 1]


def norm_back(upstream, z, gain):
    unit, scale = norm_parts(z)
    d_gain = jnp.sum(upstream * unit, axis=0, keepdims=True)
    d_shift = jnp.sum(upstream, axis=0, keepdims=True)
    inner = upstream * gain
    mean = jnp.mean(inner, axis=-1, keepdims=True)
    along = jnp.mean(inner * unit, axis=-1, keepdims=True)
    return scale * (inner - mean - unit * along), d_gain, d_shift


def column_sum(values):
    return jnp.sum(values.astype(FULL), axis=0, keepdims=True)


def two_heads(rows):
    low = lax.broadcasted_iota(jnp.int32, rows.shape, 1) < HD
    none = jnp.zeros_like(rows)
    return jnp.concatenate([jnp.where(low, rows, none), jnp.where(low, none, rows)], axis=0)


def one_row(stacked):
    half = stacked.shape[0] // 2
    low = lax.broadcasted_iota(jnp.int32, (half, PAIR), 1) < HD
    return jnp.where(low, stacked[:half], stacked[half:])


def softmax_rows(query, keys, allowed):
    logits = jnp.where(allowed, dot_t(two_heads(query), keys) * HD ** (-0.5), MASKED_SCORE)
    weight = jnp.exp(logits - jnp.max(logits, axis=-1, keepdims=True))
    return (weight * (1.0 / jnp.sum(weight, axis=-1, keepdims=True))).astype(LOW)


def attend_back(query, keys, values, probs, upstream):
    queries, ups = two_heads(query), two_heads(upstream)
    wide_probs = probs.astype(FULL)
    d_probs = dot_t(ups, values)
    row_dot = jnp.sum(wide_probs * d_probs, axis=-1, keepdims=True)
    d_scores = (wide_probs * (d_probs - row_dot)).astype(LOW)
    scale = HD ** (-0.5)
    return one_row(dot(d_scores, keys)) * scale, t_dot(d_scores, queries) * scale, t_dot(probs, ups)


def twice(mask):
    wide = jnp.where(mask, 1, 0)
    return jnp.concatenate([wide, wide], axis=0) == 1


def self_forward(
    place, weight, x, x2, bias, seg_col, seg_row, joined, probs, mix, x_t, x_t2, mix_t
):
    x_t[...] = x[...].T
    x_t2[...] = x2[...].T
    for side, y, n in each_block(place, weight):
        w = weight.part(side, y)
        at = lanes(n, w.shape[-1])
        joined[:, at] = (dot(x[...], w) + bias[:, at]).astype(LOW)
    width, rows = mix.shape[1], seg_row.shape[-1]
    below = lax.broadcasted_iota(jnp.int32, (rows, rows), 0) >= lax.broadcasted_iota(
        jnp.int32, (rows, rows), 1
    )
    for p in range(mix.shape[0] // rows):
        at = pl.ds(p * rows, rows)
        allowed = twice((seg_col[at, :] == seg_row[p]) & below)
        for h in range(width // PAIR):
            q, k, v = (joined[at, pl.ds(i * width + h * PAIR, PAIR)] for i in range(3))
            low = softmax_rows(q, k, allowed)
            probs[pl.ds((p * (width // PAIR) + h) * 2 * rows, 2 * rows), :] = low
            mix[at, pl.ds(h * PAIR, PAIR)] = one_row(dot(low, v)).astype(LOW)
    mix_t[...] = mix[...].T


def first_half(place, w_out, w_query, mix, x, vec, first_sum, low_t, query, acc):
    for side, y, n in each_block(place, w_out):
        w = w_out.part(side, y)
        acc[:, lanes(n, w.shape[-1])] = dot(mix[...], w)
    z = x[...].astype(FULL) + (acc[...] + vec[B_SELF_OUT : B_SELF_OUT + 1, :])
    first_sum[...] = z
    low = norm(z, vec, 0).astype(LOW)
    low_t[...] = low.T
    for side, y, n in each_block(place, w_query):
        w = w_query.part(side, y)
        at = lanes(n, w.shape[-1])
        query[:, at] = (dot(low, w) + vec[B_CROSS_Q : B_CROSS_Q + 1, at]).astype(LOW)


def table_keys(place, weight, x, x2, vec, out, x_t, x_t2):
    half = out.shape[-1] // 2

    @pl.when(pl.program_id(0) == 0)
    def _():
        weight.wait(0)
        weight.wait(1)

    for side in range(2):
        bias = vec[B_CROSS_V : B_CROSS_V + 1, lanes(place[2] ^ side, half)]
        out[side, :, :half] = dot(x[...], weight.part(side, 0)).astype(LOW)
        out[side, :, half:] = (dot(x[...], weight.part(side, 1)) + bias).astype(LOW)
    x_t[...] = x[...].T
    x_t2[...] = x2[...].T


def cross_forward(place, query, kv, table_col, table_row, mix, probs, mix_t):
    rows, half = query.shape
    allowed = twice(table_col[...] == table_row[0])
    for h in range(half // PAIR):
        at = pl.ds(h * PAIR, PAIR)
        low = softmax_rows(query[:, at], kv[0, :, at], allowed)
        probs[0, 0, pl.ds(h * 2 * rows, 2 * rows), :] = low
        mixed = one_row(dot(low, kv[0, :, pl.ds(half + h * PAIR, PAIR)])).astype(LOW)
        mix[:, at] = mixed
        mix_t[at, :] = mixed.T


def second_half(place, weight, mix, first_sum, vec, second_sum, second_low, low_t, acc):
    for side, y, n in each_block(place, weight):
        w = weight.part(side, y)
        acc[:, lanes(n, w.shape[-1])] = dot(mix[...], w)
    z = norm(first_sum[...], vec, 0) + (acc[...] + vec[B_CROSS_OUT : B_CROSS_OUT + 1, :])
    second_sum[...] = z
    low = norm(z, vec, 1).astype(LOW)
    second_low[...] = low
    low_t[...] = low.T


def feed_in(place, weight, x, bias, active, slope, active_t):
    for side, y, n in each_block(place, weight):
        w = weight.part(side, y)
        cols = w.shape[-1]
        at = lanes(n, cols)
        hidden = dot(x[...], w) + bias[:, at]
        share = 0.5 + 0.5 * lax.erf(hidden * 2 ** (-0.5))
        low = (hidden * share).astype(LOW)
        active[:, at] = low
        active_t[pl.ds(pl.multiple_of(n * cols, 128), cols), :] = low.T
        density = jnp.exp(hidden * hidden * (-0.5)) * (2 * math.pi) ** (-0.5)
        slope[:, at] = (share + hidden * density).astype(LOW)


def give(place, send, rows, first=0):
    cols = rows.shape[-1] // 4
    for y in range(2):
        send[y, :, first : first + cols] = rows[:, lanes(block_of(place, 1, y), cols)]


def feed_out(
    place, weight, active, second_sum, cotangent, vec, output, d_third, d_low, grads, send, acc
):
    for side, y, n in each_block(place, weight):
        w = weight.part(side, y)
        acc[:, lanes(n, w.shape[-1])] = dot(active[...], w)
    z = norm(second_sum[...], vec, 1) + (acc[...] + vec[B_FC_OUT : B_FC_OUT + 1, :])
    output[...] = norm(z, vec, 2).astype(LOW)
    back, d_gain, d_shift = norm_back(cotangent[...].astype(FULL), z, vec[GAIN + 2 : GAIN + 3])
    d_third[...] = back
    low = back.astype(LOW)
    d_low[...] = low
    grads[0:1, :] = column_sum(low)
    grads[1:2, :] = d_shift
    grads[2:3, :] = d_gain
    give(place, send, d_low)


def through(place, rows, weight):
    total = 0
    for side, y, n in each_block(place, weight):
        w = weight.part(side, y)
        total += dot_t(rows[:, lanes(n, w.shape[-1])], w)
    return total


def feed_out_back(place, weight, d_third, slope, d_hidden, grads, send):
    _, _, lines, _, rows, cols = weight.buffer.shape
    weight.wait(0)
    weight.wait(1)
    step = max(1, min(lines, 1024 // (2 * rows)))
    for z in range(0, lines, step):
        total = 0
        for side, y, n in each_block(place, weight, wait=False):
            w = weight.buffer[side, y, z : z + step].reshape(-1, cols)
            total += dot_t(d_third[:, lanes(n, cols)], w)
        at = pl.ds(z * 2 * rows, step * 2 * rows)
        low = (slope[:, at].astype(FULL) * total).astype(LOW)
        d_hidden[:, at] = low
        grads[:, at] = column_sum(low)
    give(place, send, d_hidden)


def feed_in_back(
    place, w_in, w_out, d_hidden, d_third, second_sum, vec, d_sum, d_low, d_mix, grads, send
):
    upstream = d_third[...] + through(place, d_hidden, w_in)
    back, d_gain, d_shift = norm_back(upstream, second_sum[...], vec[GAIN + 1 : GAIN + 2])
    d_sum[...] = back
    low = back.astype(LOW)
    d_low[...] = low
    grads[0:1, :] = column_sum(low)
    grads[1:2, :] = d_shift
    grads[2:3, :] = d_gain
    d_mix[...] = through(place, d_low, w_out).astype(LOW)
    give(place, send, d_low)


def cross_backward(place, query, kv, probs, d_mix, d_query, d_other, d_mine, grads):
    rows, half = query.shape
    for h in range(half // PAIR):
        at, beside = pl.ds(h * PAIR, PAIR), pl.ds(half + h * PAIR, PAIR)
        dq, dk, dv = attend_back(
            query[:, at],
            kv[0, :, at],
            kv[0, :, beside],
            probs[0, 0, pl.ds(h * 2 * rows, 2 * rows), :],
            d_mix[:, at],
        )
        d_query[:, at] = dq.astype(LOW)
        low = dv.astype(LOW)

        @pl.when(pl.program_id(0) == 0)
        def _(at=at, beside=beside, dk=dk, low=low):
            d_other[:, at] = dk.astype(LOW)
            d_other[:, beside] = low

        @pl.when(pl.program_id(0) == 1)
        def _(at=at, beside=beside, dk=dk, low=low):
            d_mine[:, at] = dk.astype(LOW)
            d_mine[:, beside] = low

        sums = column_sum(low)
        before = jnp.where(pl.program_id(1) == 0, 0.0, grads[0, :, at])
        grads[0, :, at] = before + sums


def self_backward(
    place, w_query, w_out, d_query, d_sum2, first_sum, vec, joined, probs,
    d_sum, d_low, d_joined, grads, send,
):
    width = d_sum.shape[-1]
    upstream = d_sum2[...] + through(place, d_query, w_query)
    back, d_gain, d_shift = norm_back(upstream, first_sum[...], vec[GAIN : GAIN + 1])
    d_sum[...] = back
    low = back.astype(LOW)
    d_low[...] = low
    d_mix = through(place, d_low, w_out).astype(LOW)
    rows = probs.shape[-1]
    heads = width // PAIR
    for p in range(d_sum.shape[0] // rows):
        at = pl.ds(p * rows, rows)
        for h in range(heads):
            where = [pl.ds(i * width + h * PAIR, PAIR) for i in range(3)]
            q, k, v = (joined[at, w] for w in where)
            found = attend_back(
                q,
                k,
                v,
                probs[pl.ds((p * heads + h) * 2 * rows, 2 * rows), :],
                d_mix[p * rows : (p + 1) * rows, h * PAIR : (h + 1) * PAIR],
            )
            for w, value in zip(where, found):
                d_joined[at, w] = value.astype(LOW)
    grads[0:1, :] = column_sum(d_joined[:, :width])
    grads[1:2, :] = column_sum(d_joined[:, 2 * width :])
    grads[2:3, :] = column_sum(low)
    grads[3:4, :] = column_sum(d_query[...])
    grads[4:5, :] = d_shift
    grads[5:6, :] = d_gain
    give(place, send, d_joined)
    give(place, send, d_low, 3 * width // 4)
    give(place, send, d_query, width)


def input_back(place, weight, d_joined, d_sum, out):
    out[...] = d_sum[...] + through(place, d_joined, weight)


def table_back(place, weight, d_mine, d_other, out):
    @pl.when(pl.program_id(0) == 0)
    def _():
        weight.wait(0)
        weight.wait(1)

    half = d_mine.shape[-1] // 2
    total = 0
    for side, d in enumerate((d_mine, d_other)):
        for y in range(2):
            total += dot_t(d[:, y * half : (y + 1) * half], weight.part(side, y))
    out[...] = total


def quarter_place(step, place):
    c = place[2]
    dy = jnp.where(step == 0, 1, jnp.where(step == 1, 1 - c, jnp.where(step == 2, c, 0)))
    dx = jnp.where(step == 0, 1, jnp.where(step == 1, c, jnp.where(step == 2, 1 - c, 0)))
    return place[0] ^ dy, place[1] ^ dx


def quarter_grads(net, name, products, more, time):
    lines = net.lines
    ins = []
    for left, left2, right, right2, size, first in products:
        for a in (left, left2):
            view = a.reshape(lines, 2, -1, a.shape[-1])
            block = (lines, 1) + view.shape[2:]
            ins.append((view, block, lambda s, at: (0, quarter_place(s, at)[1], 0, 0)))
        if first is None:
            for a in (right, right2):
                ins.append(
                    (a, (a.shape[0], size), lambda s, at: (0, quarter_place(s, at)[0]))
                )
        else:
            ins.append(
                (
                    right,
                    (right.shape[0], size),
                    lambda s, at: (0, 2 * quarter_place(s, at)[0] + at[2]),
                )
            )
            ins.append(
                (
                    right2,
                    (1, right2.shape[1], size),
                    lambda s, at, first=first: (quarter_place(s, at)[0], 0, first),
                )
            )
    rows = products[0][0].shape[0] // net.wide
    cols = sum(p[4] for p in products)
    extra = more[0].shape[3] if more else 0
    for a in more or ():

        def corner(s, at):
            y, x = quarter_place(s, at)
            return (y, 0, x, 0, 0)

        ins.append((a, (1, lines, 1, extra, cols), corner))

    def body(place, *refs):
        outs = refs[len(ins) :]
        quarters = []
        start = 0
        for i, (_, _, _, _, size, first) in enumerate(products):
            left, left2, right, right2 = refs[4 * i : 4 * i + 4]
            l, l2 = (a[:, 0].reshape(lines * rows, -1) for a in (left, left2))
            r2 = right2[...] if first is None else right2[0]
            value = dot(l, right[...]) + dot(l2, r2)
            quarters.append((start, size, value.astype(LOW).reshape(lines, rows, size)))
            start += size

        def put(out):
            for z in range(lines):
                differs = place[3] ^ z
                to = sum(
                    ((differs >> bit) & 1) * (lines >> (bit + 1))
                    for bit in range(lines.bit_length() - 1)
                )
                for start, size, value in quarters:
                    out[to, :rows, start : start + size] = value[z]
                if extra:
                    a, b = refs[4 * len(products) : len(ins)]
                    value = a[0, z, 0].astype(FULL) + b[0, z, 0].astype(FULL)
                    out[to, rows:, :] = value.astype(LOW)

        step = pl.program_id(0)
        pl.when(step < 2)(lambda: put(outs[0].at[0]))
        pl.when(step == 2)(lambda: put(outs[1]))
        pl.when(step == 3)(lambda: put(outs[2]))

    shape = (lines, rows + extra, cols)
    return call(
        body,
        name,
        net,
        (4,),
        ins,
        [
            ((2,) + shape, LOW, (1,) + shape, lambda s, at: (jnp.minimum(s, 1), 0, 0, 0)),
            whole_out(shape, LOW),
            whole_out(shape, LOW),
        ],
        time=time,
    )


def segment_index(lengths, count):
    segment_ends = jnp.cumsum(lengths, axis=-1)
    position = jnp.arange(count, dtype=jnp.int32)
    passed = (position[None, :, None] >= segment_ends[:, None, :]).astype(jnp.int32)
    return jnp.sum(passed, axis=-1)


def per_device(
    inputs,
    memory,
    cotangent,
    dec_lengths,
    mem_lengths,
    seg_table,
    self_qkv,
    self_out,
    cross_q,
    cross_kv,
    cross_out,
    fc_in,
    fc_out,
    vec_bias,
    norm_gain,
    fc_in_bias,
    *,
    wide,
    narrow,
):
    net = Net(wide, narrow)
    Order.last = Order.soon = Order.later = ()
    pairs, length, width = inputs.shape
    held = memory.shape[1]
    x = inputs.reshape(-1, width)
    table = memory.reshape(-1, width)
    upstream = cotangent.reshape(-1, width)
    count, quarter, half = x.shape[0], width // narrow, width // 2
    hidden = fc_out.shape[0] * wide

    rows = jnp.concatenate([vec_bias, norm_gain])
    small = jnp.concatenate([rows.reshape(-1), fc_in_bias])
    extra = 16
    small_rows = jnp.zeros((extra, self_qkv.shape[1]), LOW).at[0, : small.size].set(small)
    x2, table2 = net.over_core(x), net.over_core(table)
    g2 = Weight(net, jnp.concatenate([self_qkv, small_rows])).at_once()
    g2.rows = self_qkv.shape[0]
    shards = jnp.concatenate([cross_kv, cross_out, self_out, cross_q], axis=1)
    g3, g4, g5 = Weight(net, shards), Weight(net, fc_in), Weight(net, fc_out)
    g2.start()
    g3.line(g2.held)
    Order.need(x2, table2, *g2.copy("held"))
    g3.line_on()
    g2.turn()
    Order.need(*g2.copy("one", "two"))
    g3.line_end()
    g3.start()
    g4.line()
    g2.copy("three")

    segments = segment_index(dec_lengths, length)
    tables = segment_index(mem_lengths, held)
    matches = segments[:, :, None] == jnp.arange(dec_lengths.shape[-1], dtype=jnp.int32)
    query_table = jnp.sum(jnp.where(matches, seg_table[:, None, :], 0), axis=-1)
    seg_col, seg_row = segments.reshape(-1, 1), segments.reshape(pairs, 1, length)
    table_col, table_row = query_table.reshape(-1, 1), tables.reshape(pairs, 1, held)

    def in_place(pieces):
        sides = []
        for side, (same, one, two, three) in enumerate((pieces[:4], pieces[4:])):
            first = (net.c ^ side) == 0
            by_x = jnp.where(first, one, two)
            by_y = jnp.where(first, two, one)
            sides.append(jnp.stack([jnp.stack([same, by_x]), jnp.stack([by_y, three])]))
        out = jnp.stack(net.swap(*sides))
        out = jnp.where(net.y == 0, out, out[:, ::-1])
        out = jnp.where(net.x == 0, out, out[:, :, ::-1])
        return jnp.transpose(out, (3, 2, 1, 0, 4)).reshape(wide, narrow, -1)

    vectors = in_place([p[:, self_qkv.shape[0], : small.size] for p in g2.pieces]).astype(FULL)
    fc_bias = vectors[:, :, rows.size :].reshape(1, -1)
    vec = vectors[:, :, : rows.size].reshape(wide * narrow, rows.shape[0], -1)
    vec = jnp.transpose(vec, (1, 0, 2)).reshape(rows.shape[0], width)
    joined_bias = jnp.concatenate([vec[0], jnp.zeros((width,), FULL), vec[1]])[None]

    heads = width // PAIR
    joined, self_probs, self_mix, x_t, x_t2, self_mix_t = call(
        self_forward,
        "self_forward",
        net,
        (1,),
        [whole(x), whole(x2), whole(joined_bias), whole(seg_col), whole(seg_row)],
        [
            whole_out((count, 3 * width), LOW),
            whole_out((pairs * heads * 2 * length, length), LOW),
            whole_out((count, width), LOW),
            whole_out((width, count), LOW),
            whole_out((width, count), LOW),
            whole_out((width, count), LOW),
        ],
        weights=[(g2, 0, 3 * quarter)],
        time=9,
    )
    g4.line_on()
    g3.turn()
    Order.need(*g3.copy("held", "one", "two"))
    g4.line_end()
    g4.start()
    g5.line()
    g3.copy("three")
    first_sum, first_low_t, query = call(
        first_half,
        "first_half",
        net,
        (1,),
        [whole(self_mix), whole(x), whole(vec)],
        [
            whole_out((count, width), FULL),
            whole_out((width, count), LOW),
            whole_out((count, width), LOW),
        ],
        [pltpu.VMEM((count, width), FULL)],
        weights=[(g3, 3 * quarter, quarter), (g3, 4 * quarter, quarter)],
        time=6,
    )
    g5.line_on()
    g4.turn()
    Order.pin(*g4.copy("held", "one", "two"))
    tile = 512
    kv, table_t, table_t2 = call(
        table_keys,
        "table_keys",
        net,
        (table.shape[0] // tile,),
        [
            (table, (tile, width), lambda t, at: (t, 0)),
            (table2, (tile, width), lambda t, at: (t, 0)),
            whole(vec),
        ],
        [
            ((2, table.shape[0], width), LOW, (2, tile, width), lambda t, at: (0, t, 0)),
            ((width, table.shape[0]), LOW, (width, tile), lambda t, at: (0, t)),
            ((width, table.shape[0]), LOW, (width, tile), lambda t, at: (0, t)),
        ],
        weights=[(g3, 0, half)],
        time=15,
    )
    g5.line_end()
    g5.start()
    Order.pin(*g4.copy("three"))
    score_rows = half // PAIR * 2 * length
    core_block = ((length, half), lambda s, p, at: (p, at[2] ^ s))
    cross_mix, cross_probs, cross_mix_t = call(
        cross_forward,
        "cross_forward",
        net,
        (2, pairs),
        [
            (query, *core_block),
            (kv, (1, held, width), lambda s, p, at: (s, p, 0)),
            (table_col, (length, 1), lambda s, p, at: (p, 0)),
            (table_row, (1, 1, held), lambda s, p, at: (p, 0, 0)),
        ],
        [
            ((count, width), LOW, *core_block),
            (
                (2, pairs, score_rows, held),
                LOW,
                (1, 1, score_rows, held),
                lambda s, p, at: (s, p, 0, 0),
            ),
            ((width, count), LOW, (half, length), lambda s, p, at: (at[2] ^ s, p)),
        ],
        time=15,
    )
    second_sum, second_low, second_low_t = call(
        second_half,
        "second_half",
        net,
        (1,),
        [whole(cross_mix), whole(first_sum), whole(vec)],
        [
            whole_out((count, width), FULL),
            whole_out((count, width), LOW),
            whole_out((width, count), LOW),
        ],
        [pltpu.VMEM((count, width), FULL)],
        weights=[(g3, half, quarter)],
        time=6,
    )
    g5.turn()
    g5.copy("held", "one", "two")
    active, slope, active_t = call(
        feed_in,
        "feed_in",
        net,
        (1,),
        [whole(second_low), whole(fc_bias)],
        [
            whole_out((count, hidden), LOW),
            whole_out((count, hidden), LOW),
            whole_out((hidden, count), LOW),
        ],
        weights=[(g4, 0, hidden // 4)],
        time=11,
    )
    g5.copy("three")
    active_t2, second_low_t2 = net.over_core(active_t), net.over_core(second_low_t)
    output, d_third, d_low3, grads3, send3 = call(
        feed_out,
        "feed_out",
        net,
        (1,),
        [whole(active), whole(second_sum), whole(upstream), whole(vec)],
        [
            whole_out((count, width), LOW),
            whole_out((count, width), FULL),
            whole_out((count, width), LOW),
            whole_out((8, width), FULL),
            whole_out((2, count, quarter), LOW),
        ],
        [pltpu.VMEM((count, width), FULL)],
        weights=[(g5, 0, quarter)],
        time=10,
    )

    got3 = net.over_core(send3)
    first_low_t2, self_mix_t2, cross_mix_t2 = Order.pin(
        *(net.over_core(a) for a in (first_low_t, self_mix_t, cross_mix_t))
    )
    r_out = Reduction(net, "grad_out", [(active_t, active_t2, d_low3, got3, quarter, 0)]).start()
    d_hidden, g_fc_bias, send_hidden = call(
        feed_out_back,
        "feed_out_back",
        net,
        (1,),
        [whole(d_low3), whole(slope)],
        [
            whole_out((count, hidden), LOW),
            whole_out((1, hidden), FULL),
            whole_out((2, count, hidden // 4), LOW),
        ],
        weights=[(g5, 0, quarter)],
        time=10,
    )
    got_hidden = net.over_core(send_hidden)
    d_sum2, d_low2, d_mix, grads2, send2 = call(
        feed_in_back,
        "feed_in_back",
        net,
        (1,),
        [whole(d_hidden), whole(d_third), whole(second_sum), whole(vec)],
        [
            whole_out((count, width), FULL),
            whole_out((count, width), LOW),
            whole_out((count, width), LOW),
            whole_out((8, width), FULL),
            whole_out((2, count, quarter), LOW),
        ],
        weights=[(g4, 0, hidden // 4), (g3, half, quarter)],
        time=10,
    )
    got2 = net.over_core(send2)
    Order.need(got2)
    r_in = Reduction(
        net, "grad_in", [(second_low_t, second_low_t2, d_hidden, got_hidden, hidden // 4, 0)]
    ).start()
    r_out.turn()
    back_block = ((length, half), lambda s, p, at: (p, at[2] ^ 1 ^ s))
    d_query, d_other, d_mine, grads_v = call(
        cross_backward,
        "cross_backward",
        net,
        (2, pairs),
        [
            (query, *back_block),
            (kv, (1, held, width), lambda s, p, at: (1 - s, p, 0)),
            (cross_probs, (1, 1, score_rows, held), lambda s, p, at: (1 - s, p, 0, 0)),
            (d_mix, *back_block),
        ],
        [
            ((count, width), LOW, *back_block),
            (
                table.shape,
                LOW,
                (held, width),
                lambda s, p, at: (jnp.where(s == 0, p, pairs - 1), 0),
            ),
            (table.shape, LOW, (held, width), lambda s, p, at: (jnp.where(s == 0, 0, p), 0)),
            ((2, 1, half), FULL, (1, 1, half), lambda s, p, at: (1 - s, 0, 0)),
        ],
        time=23,
    )
    d_sum1, d_low1, d_joined, grads1, send1 = call(
        self_backward,
        "self_backward",
        net,
        (1,),
        [
            whole(d_query),
            whole(d_sum2),
            whole(first_sum),
            whole(vec),
            whole(joined),
            whole(self_probs),
        ],
        [
            whole_out((count, width), FULL),
            whole_out((count, width), LOW),
            whole_out((count, 3 * width), LOW),
            whole_out((8, width), FULL),
            whole_out((2, count, 5 * quarter), LOW),
        ],
        weights=[(g3, 4 * quarter, quarter), (g3, 3 * quarter, quarter)],
        time=13,
    )
    got1, got_table = net.over_core(send1), net.over_core(d_other)
    r_out.line()
    r_in.turn()
    r_qkv = Reduction(
        net,
        "grad_qkv",
        [(x_t, x_t2, d_joined, got1, 3 * quarter, 0)],
    ).start(r_in.near, r_out.step)
    grads_v = jnp.concatenate(net.swap(grads_v[0], grads_v[1]), axis=1)
    g_rows = jnp.concatenate(
        [
            grads1[:4],
            grads_v,
            grads2[:1],
            grads3[:1],
            grads1[4:5],
            grads2[1:2],
            grads3[1:2],
            grads1[5:6],
            grads2[2:3],
            grads3[2:3],
        ]
    )
    g_rows = jnp.transpose(g_rows.reshape(rows.shape[0], wide, narrow, -1), (2, 1, 0, 3))
    g_small = jnp.transpose(g_fc_bias.reshape(wide, narrow, -1), (1, 0, 2))
    g_small = jnp.concatenate([g_rows.reshape(narrow, wide, -1), g_small], axis=2).astype(LOW)
    room = extra * 2 * quarter - small.size
    g_small = jnp.pad(g_small, ((0, 0), (0, 0), (0, room)))
    g_small = g_small.reshape(2, 2, wide // 2, 2, extra, -1)
    small_mine, small_other = net.swap(g_small[:, 0], g_small[:, 1])
    small_got = net.over_core(small_other)
    r_out.line_on()
    r_in.line()
    r_self = Reduction(
        net,
        "grad_self",
        [
            (self_mix_t, self_mix_t2, d_low1, got1, quarter, 3),
            (first_low_t, first_low_t2, d_query, got1, quarter, 4),
        ],
        (small_mine, small_got),
    ).start()
    r_cross = Reduction(
        net,
        "grad_cross",
        [
            (table_t, table_t2, d_mine, got_table, half, None),
            (cross_mix_t, cross_mix_t2, d_low2, got2, quarter, 0),
        ],
        time=17,
    ).start(r_qkv.pair, r_self.pair)
    r_qkv.turn()
    r_self.turn()
    r_out.line_end()
    r_in.line_on()
    tile = 512
    (memory_grad,) = call(
        table_back,
        "table_back",
        net,
        (table.shape[0] // tile,),
        [(d, (tile, width), lambda t, at: (t, 0)) for d in (d_mine, d_other)],
        [(table.shape, FULL, (tile, width), lambda t, at: (t, 0))],
        weights=[(g3, 0, half)],
        time=15,
    )
    r_qkv.line()
    r_self.line()
    r_in.line_end()
    (input_grad,) = call(
        input_back,
        "input_back",
        net,
        (1,),
        [whole(d_joined), whole(d_sum1)],
        [whole_out((count, width), FULL)],
        weights=[(g2, 0, 3 * quarter)],
        time=7,
    )
    r_cross.turn()
    r_qkv.line_on()
    r_self.line_on()
    r_cross.line().line_on()
    r_qkv.line_end()
    r_self.line_end()
    r_cross.line_end()

    g_out, g_in, g_cross, g_self, g_qkv = (
        r.total for r in (r_out, r_in, r_cross, r_self, r_qkv)
    )
    g_small = g_self[-extra:].reshape(-1)[: small.size]
    g_rows, g_fc_bias = g_small[: rows.size].reshape(rows.shape), g_small[rows.size :]
    return (
        output.reshape(inputs.shape),
        input_grad.reshape(inputs.shape),
        memory_grad.reshape(memory.shape),
        g_qkv,
        g_self[:-extra, :quarter],
        g_self[:-extra, quarter:],
        g_cross[:, : 2 * quarter],
        g_cross[:, 2 * quarter :],
        g_in,
        g_out,
        g_rows[:10],
        g_rows[10:],
        g_fc_bias,
    )


def solution(mesh):
    tokens = P(BOTH, None, None)
    lengths = P(BOTH, None)
    weight = P("wide", "narrow")
    vector = P(None, BOTH)
    return jax.shard_map(
        partial(per_device, wide=mesh.shape["wide"], narrow=mesh.shape["narrow"]),
        mesh=mesh,
        in_specs=(tokens,) * 3 + (lengths,) * 3 + (weight,) * 7 + (vector, vector, P(BOTH)),
        out_specs=(tokens,) * 3 + (weight,) * 7 + (vector, vector, P(BOTH)),
        check_vma=False,
    )
```

```python
import math
from functools import partial

import jax
import jax.numpy as jnp
from jax import lax
from jax.experimental import pallas as pl
from jax.experimental.pallas import tpu as pltpu
from jax.sharding import PartitionSpec as P

HD = 64
PAIR = 2 * HD
BOTH = ("wide", "narrow")
EPS = 1e-05
MASKED_SCORE = -1000000000.0
LOW = jnp.bfloat16
FULL = jnp.float32
VMEM_BYTES = 60 * 1024 * 1024
B_QUERY, B_VALUE, B_SELF_OUT, B_CROSS_Q, B_CROSS_V, B_CROSS_OUT, B_FC_OUT = range(7)
SHIFT, GAIN = 7, 10


def after(value, *others):
    return lax.optimization_barrier((value, others))[0]


class Order:
    last, soon, later = (), (), ()

    @classmethod
    def put(cls, kernel, arrays):
        first = after(arrays[0], *cls.last, *cls.soon)
        out = kernel(first, *arrays[1:])
        cls.last, cls.soon, cls.later = (out[0],), cls.later, ()
        return out

    @classmethod
    def now(cls, value, *others):
        return after(value, *cls.last, *others)

    @classmethod
    def need(cls, *arrays):
        cls.soon += arrays

    @classmethod
    def pin(cls, *arrays):
        cls.later += arrays
        return arrays


class Net:
    def __init__(self, wide, narrow):
        self.wide, self.narrow, self.lines = wide, narrow, wide // 2
        w, n = lax.axis_index("wide"), lax.axis_index("narrow")
        self.z, self.x, self.y, self.c = w // 2, w % 2, n // 2, n % 2
        self.place = jnp.stack([self.y, self.x, self.c, self.z]).astype(jnp.int32)
        both = [(i, j) for i in range(wide) for j in range(narrow)]

        def flat(i, j):
            return i * narrow + j

        def pairs(x_core):
            return [
                (flat(i, j), flat(i ^ 1, j) if j % 2 == x_core else flat(i, j ^ 2)) for i, j in both
            ]

        self.first, self.second = pairs(0), pairs(1)
        self.core = [(j, j ^ 1) for j in range(narrow)]
        self.groups = [[z * 2 + x for z in range(self.lines)] for x in range(2)]

    def across(self, value, way, *others):
        return lax.ppermute(Order.now(value, *others), BOTH, way)

    def over_core(self, value, *others):
        return lax.ppermute(Order.now(value, *others), "narrow", self.core)

    def along(self, value, step, *others):
        way = [(w, ((w // 2) ^ step) * 2 + w % 2) for w in range(self.wide)]
        return lax.ppermute(Order.now(value, *others), "wide", way)

    def swap(self, a, b):
        first = self.c == 0
        return jnp.where(first, a, b), jnp.where(first, b, a)


class Weight:
    def __init__(self, net, shard, before=()):
        self.net = net
        self.rows = shard.shape[0]
        self.shard = after(shard, *before)

    def at_once(self):
        self.held = lax.all_gather(
            self.shard, "wide", axis=0, axis_index_groups=self.net.groups
        )
        return self

    def line(self, *others):
        net = self.net
        if net.lines == 4:
            self.got = net.along(self.shard, 2, *others)
        return self

    def line_on(self):
        net = self.net
        if net.lines == 4:
            self.held = stack(net, [self.shard, self.got], 1)
            self.got = net.along(self.held, 1)
        return self

    def line_end(self):
        net = self.net
        if net.lines == 4:
            self.held = stack(net, [self.held, self.got], 0)
        else:
            self.at_once()
        return self

    def start(self, *others):
        net = self.net
        self.one = net.across(self.held, net.first, *others)
        self.two = net.across(self.held, net.second, *others)
        return self

    def turn(self, *others):
        net = self.net
        self.three = net.across(self.one, net.second, self.two, *others)
        return self

    def copy(self, *names, after=None):
        others = () if after is None else (after,)
        new = [self.net.over_core(getattr(self, name), *others) for name in names]
        self.copies = [*getattr(self, "copies", ()), *new]
        return new

    def arrays(self):
        return [self.held, self.one, self.two, self.three, *self.copies]

    def spots(self):
        return [(i, 0) for i in range(8)]


class PairedWeight(Weight):
    def begin(self, *others):
        self.mate = self.net.across(self.shard, self.net.first, *others)
        return self

    def pair(self):
        self.single = self.rows
        self.shard = jnp.concatenate([self.shard, self.mate])
        return self

    def turn(self, *others):
        self.far = self.net.across(self.held, self.net.second, *others)
        return self

    def arrays(self):
        return [self.held, self.far, *self.copies]

    def spots(self):
        return [(2 * side + k // 2, k % 2 * self.rows) for side in range(2) for k in range(4)]


def piece_place(place, index):
    side, k = divmod(index, 4)
    c = place[2] ^ side
    dy, dx = ((0, 0), (c, 1 - c), (1 - c, c), (1, 1))[k]
    return place[0] ^ dy, place[1] ^ dx, side


class Loaded:
    def __init__(self, place, arrays, spots, buffer, sems, rows, col):
        self.buffer = buffer
        size = buffer.shape[-1]
        self.copies = []
        for i, (array, first) in enumerate(spots):
            y, x, side = piece_place(place, i)
            self.copies.append(
                pltpu.make_async_copy(
                    arrays[array].at[:, pl.ds(first, rows), pl.ds(col, size)],
                    buffer.at[side, y, :, x],
                    sems.at[i],
                )
            )

    def start(self):
        for copy in self.copies:
            copy.start()

    def wait(self, side):
        for copy in self.copies[4 * side : 4 * side + 4]:
            copy.wait()

    def part(self, side, y):
        return self.buffer[side, y].reshape(-1, self.buffer.shape[-1])


class Reduction:
    def __init__(self, net, name, products, more=None):
        self.net = net
        self.pair, self.near, self.own = quarter_grads(net, name, products, more)

    def start(self, *others):
        self.pair = self.net.across(self.pair, self.net.second, *others)
        return self

    def turn(self, *others):
        pair = Order.now(self.pair, *others)
        self.ready = (self.near.astype(FULL) + pair[0].astype(FULL)).astype(LOW)
        Order.need(self.ready)
        self.near = self.net.across(self.ready, self.net.first)
        return self

    def line(self, *others):
        net = self.net
        near = Order.now(self.near, *others)
        total = self.own.astype(FULL) + self.pair[1].astype(FULL) + near.astype(FULL)
        self.total = total.astype(LOW)
        Order.need(self.total)
        self.step = net.along(self.total[total.shape[0] // 2 :], 1)
        return self

    def line_on(self):
        net = self.net
        half, step = self.total.shape[0] // 2, 2
        total = self.total[:half].astype(FULL) + Order.now(self.step).astype(FULL)
        while half > 2:
            half //= 2
            low = total.astype(LOW)
            got = net.along(low[half:], step)
            total = low[:half].astype(FULL) + got.astype(FULL)
            step *= 2
        self.total = total.astype(LOW)
        Order.need(self.total)
        if half > 1:
            self.step = net.along(self.total[1:], step)
        return self

    def line_end(self):
        total = self.total[0].astype(FULL)
        if self.total.shape[0] > 1:
            total += Order.now(self.step)[0].astype(FULL)
        self.total = total
        return self


def call(body, name, net, grid, ins, outs, scratch=(), weights=(), into=()):
    operands, buffers, first = [], [], []
    for weight, _, size in weights:
        first.append(len(operands))
        operands += weight.arrays()
        shape = (2, 2, net.lines, 2, weight.rows, size)
        buffers += [pltpu.VMEM(shape, LOW), pltpu.SemaphoreType.DMA((8,))]
    plain = len(ins) + len(outs)
    fixed = len(operands)
    operands += into
    specs = [pl.BlockSpec(memory_space=pl.ANY)] * len(operands)

    def run(place, *refs):
        pieces, rest = refs[:fixed], refs[len(operands) :]
        held = rest[plain : plain + len(buffers)]
        rest = rest[:plain] + rest[plain + len(buffers) :]
        loaded = [
            Loaded(
                place,
                pieces[first[i] :],
                weight.spots(),
                held[2 * i],
                held[2 * i + 1],
                weight.rows,
                col,
            )
            for i, (weight, col, _) in enumerate(weights)
        ]

        def start():
            for weight in loaded:
                weight.start()

        if grid == (1,):
            start()
        elif loaded:
            pl.when(pl.program_id(0) == 0)(start)
        body(place, *loaded, *rest)

    kernel = pl.pallas_call(
        run,
        grid_spec=pltpu.PrefetchScalarGridSpec(
            num_scalar_prefetch=1,
            grid=grid,
            in_specs=specs + [pl.BlockSpec(b, m) for _, b, m in ins],
            out_specs=[pl.BlockSpec(b, m) for _, _, b, m in outs],
            scratch_shapes=[*buffers, *scratch],
        ),
        out_shape=[jax.ShapeDtypeStruct(s, d) for s, d, _, _ in outs],
        compiler_params=pltpu.CompilerParams(
            dimension_semantics=("arbitrary",) * len(grid), vmem_limit_bytes=VMEM_BYTES
        ),
        cost_estimate=pl.CostEstimate(flops=1000, bytes_accessed=1000, transcendentals=0),
        input_output_aliases={1 + fixed + i: i for i in range(len(into))},
        name=name,
    )
    return Order.put(partial(kernel, net.place), [*operands, *(a for a, _, _ in ins)])


def stack(net, pieces, bit):
    rows, cols = pieces[0].shape[-2:]

    def body(place, *refs):
        for i in range(2):

            @pl.when(pl.program_id(0) == i)
            def _(i=i):
                refs[-1][:, 0] = refs[i][...].reshape(-1, rows, cols)

    lead = pieces[0].size // (rows * cols)
    shape = (lead, 2, rows, cols)
    (out,) = call(
        body,
        "stack",
        net,
        (2,),
        [whole(p) for p in pieces],
        [(shape, LOW, (lead, 1, rows, cols), lambda s, at: (0, ((at[3] >> bit) & 1) ^ s, 0, 0))],
    )
    return out.reshape(2 * lead, rows, cols)


def whole(array):
    return (array, array.shape, lambda *_: (0,) * array.ndim)


def whole_out(shape, dtype):
    return (shape, dtype, shape, lambda *_: (0,) * len(shape))


def lanes(index, size):
    return pl.ds(pl.multiple_of(index * size, 128), size)


def block_of(place, side, y):
    return 2 * y + (place[2] ^ side)


def each_block(place, weight, wait=True):
    for side in range(2):
        if wait:
            weight.wait(side)
        for y in range(2):
            yield side, y, block_of(place, side, y)


def dot(a, b):
    return jnp.dot(a, b, preferred_element_type=FULL)


def dot_t(a, b):
    return lax.dot_general(a, b, (((1,), (1,)), ((), ())), preferred_element_type=FULL)


def t_dot(a, b):
    return lax.dot_general(a, b, (((0,), (0,)), ((), ())), preferred_element_type=FULL)


def norm_parts(z):
    centred = z - jnp.mean(z, axis=-1, keepdims=True)
    scale = lax.rsqrt(jnp.mean(centred * centred, axis=-1, keepdims=True) + EPS)
    return centred * scale, scale


def norm(z, vec, which):
    unit, _ = norm_parts(z)
    return unit * vec[GAIN + which : GAIN + which + 1] + vec[SHIFT + which : SHIFT + which + 1]


def norm_back(upstream, z, gain):
    unit, scale = norm_parts(z)
    d_gain = jnp.sum(upstream * unit, axis=0, keepdims=True)
    d_shift = jnp.sum(upstream, axis=0, keepdims=True)
    inner = upstream * gain
    mean = jnp.mean(inner, axis=-1, keepdims=True)
    along = jnp.mean(inner * unit, axis=-1, keepdims=True)
    return scale * (inner - mean - unit * along), d_gain, d_shift


def column_sum(values):
    return jnp.sum(values.astype(FULL), axis=0, keepdims=True)


def two_heads(rows):
    low = lax.broadcasted_iota(jnp.int32, rows.shape, 1) < HD
    none = jnp.zeros_like(rows)
    return jnp.concatenate([jnp.where(low, rows, none), jnp.where(low, none, rows)], axis=0)


def one_row(stacked):
    half = stacked.shape[0] // 2
    low = lax.broadcasted_iota(jnp.int32, (half, PAIR), 1) < HD
    return jnp.where(low, stacked[:half], stacked[half:])


def softmax_rows(query, keys, allowed):
    logits = jnp.where(allowed, dot_t(two_heads(query), keys) * HD ** (-0.5), MASKED_SCORE)
    weight = jnp.exp(logits - jnp.max(logits, axis=-1, keepdims=True))
    return (weight * (1.0 / jnp.sum(weight, axis=-1, keepdims=True))).astype(LOW)


def attend_back(query, keys, values, probs, upstream):
    queries, ups = two_heads(query), two_heads(upstream)
    wide_probs = probs.astype(FULL)
    d_probs = dot_t(ups, values)
    row_dot = jnp.sum(wide_probs * d_probs, axis=-1, keepdims=True)
    d_scores = (wide_probs * (d_probs - row_dot)).astype(LOW)
    scale = HD ** (-0.5)
    return one_row(dot(d_scores, keys)) * scale, t_dot(d_scores, queries) * scale, t_dot(probs, ups)


def twice(mask):
    wide = jnp.where(mask, 1, 0)
    return jnp.concatenate([wide, wide], axis=0) == 1


def self_forward(
    place, weight, x, bias, seg_col, seg_row, joined, probs, mix, x_t, mix_t
):
    x_t[...] = x[...].T
    for side, y, n in each_block(place, weight):
        w = weight.part(side, y)
        at = lanes(n, w.shape[-1])
        joined[:, at] = (dot(x[...], w) + bias[:, at]).astype(LOW)
    width, rows = mix.shape[1], seg_row.shape[-1]
    below = lax.broadcasted_iota(jnp.int32, (rows, rows), 0) >= lax.broadcasted_iota(
        jnp.int32, (rows, rows), 1
    )
    for p in range(mix.shape[0] // rows):
        at = pl.ds(p * rows, rows)
        allowed = twice((seg_col[at, :] == seg_row[p]) & below)
        for h in range(width // PAIR):
            q, k, v = (joined[at, pl.ds(i * width + h * PAIR, PAIR)] for i in range(3))
            low = softmax_rows(q, k, allowed)
            probs[pl.ds((p * (width // PAIR) + h) * 2 * rows, 2 * rows), :] = low
            mix[at, pl.ds(h * PAIR, PAIR)] = one_row(dot(low, v)).astype(LOW)
    mix_t[...] = mix[...].T


def first_half(place, w_out, w_query, mix, x, vec, first_sum, low_t, query, acc):
    for side, y, n in each_block(place, w_out):
        w = w_out.part(side, y)
        acc[:, lanes(n, w.shape[-1])] = dot(mix[...], w)
    z = x[...].astype(FULL) + (acc[...] + vec[B_SELF_OUT : B_SELF_OUT + 1, :])
    first_sum[...] = z
    low = norm(z, vec, 0).astype(LOW)
    low_t[...] = low.T
    for side, y, n in each_block(place, w_query):
        w = w_query.part(side, y)
        at = lanes(n, w.shape[-1])
        query[:, at] = (dot(low, w) + vec[B_CROSS_Q : B_CROSS_Q + 1, at]).astype(LOW)


def table_keys(place, weight, x, x2, vec, out, x_t, x_t2):
    half = out.shape[-1] // 2

    @pl.when(pl.program_id(0) == 0)
    def _():
        weight.wait(0)
        weight.wait(1)

    for side in range(2):
        bias = vec[B_CROSS_V : B_CROSS_V + 1, lanes(place[2] ^ side, half)]
        out[side, :, :half] = dot(x[...], weight.part(side, 0)).astype(LOW)
        out[side, :, half:] = (dot(x[...], weight.part(side, 1)) + bias).astype(LOW)
    x_t[...] = x[...].T
    x_t2[...] = x2[...].T


def cross_forward(place, query, kv, table_col, table_row, mix, probs, mix_t):
    rows, half = query.shape
    allowed = twice(table_col[...] == table_row[0])
    for h in range(half // PAIR):
        at = pl.ds(h * PAIR, PAIR)
        low = softmax_rows(query[:, at], kv[0, :, at], allowed)
        probs[0, 0, pl.ds(h * 2 * rows, 2 * rows), :] = low
        mixed = one_row(dot(low, kv[0, :, pl.ds(half + h * PAIR, PAIR)])).astype(LOW)
        mix[:, at] = mixed
        mix_t[at, :] = mixed.T


def second_half(place, weight, mix, first_sum, vec, second_sum, second_low, low_t, acc):
    for side, y, n in each_block(place, weight):
        w = weight.part(side, y)
        acc[:, lanes(n, w.shape[-1])] = dot(mix[...], w)
    z = norm(first_sum[...], vec, 0) + (acc[...] + vec[B_CROSS_OUT : B_CROSS_OUT + 1, :])
    second_sum[...] = z
    low = norm(z, vec, 1).astype(LOW)
    second_low[...] = low
    low_t[...] = low.T


def feed_in(place, weight, x, bias, active, slope, active_t):
    for side, y, n in each_block(place, weight):
        w = weight.part(side, y)
        cols = w.shape[-1]
        at = lanes(n, cols)
        hidden = dot(x[...], w) + bias[:, at]
        share = 0.5 + 0.5 * lax.erf(hidden * 2 ** (-0.5))
        low = (hidden * share).astype(LOW)
        active[:, at] = low
        active_t[pl.ds(pl.multiple_of(n * cols, 128), cols), :] = low.T
        density = jnp.exp(hidden * hidden * (-0.5)) * (2 * math.pi) ** (-0.5)
        slope[:, at] = (share + hidden * density).astype(LOW)


def give(place, send, rows, first=0):
    cols = rows.shape[-1] // 4
    for y in range(2):
        send[y, :, first : first + cols] = rows[:, lanes(block_of(place, 1, y), cols)]


def feed_out(
    place, weight, active, second_sum, cotangent, vec, output, d_third, d_low, grads, send, acc
):
    for side, y, n in each_block(place, weight):
        w = weight.part(side, y)
        acc[:, lanes(n, w.shape[-1])] = dot(active[...], w)
    z = norm(second_sum[...], vec, 1) + (acc[...] + vec[B_FC_OUT : B_FC_OUT + 1, :])
    output[...] = norm(z, vec, 2).astype(LOW)
    back, d_gain, d_shift = norm_back(cotangent[...].astype(FULL), z, vec[GAIN + 2 : GAIN + 3])
    d_third[...] = back
    low = back.astype(LOW)
    d_low[...] = low
    grads[0:1, :] = column_sum(low)
    grads[1:2, :] = d_shift
    grads[2:3, :] = d_gain
    give(place, send, d_low)


def through(place, rows, weight):
    total = 0
    for side, y, n in each_block(place, weight):
        w = weight.part(side, y)
        total += dot_t(rows[:, lanes(n, w.shape[-1])], w)
    return total


def feed_out_back(place, weight, d_third, slope, d_hidden, grads, send):
    _, _, lines, _, rows, cols = weight.buffer.shape
    weight.wait(0)
    weight.wait(1)
    step = max(1, min(lines, 1024 // (2 * rows)))
    for z in range(0, lines, step):
        total = 0
        for side, y, n in each_block(place, weight, wait=False):
            w = weight.buffer[side, y, z : z + step].reshape(-1, cols)
            total += dot_t(d_third[:, lanes(n, cols)], w)
        at = pl.ds(z * 2 * rows, step * 2 * rows)
        low = (slope[:, at].astype(FULL) * total).astype(LOW)
        d_hidden[:, at] = low
        grads[:, at] = column_sum(low)
    give(place, send, d_hidden)


def feed_in_back(
    place, w_in, w_out, d_hidden, d_third, second_sum, vec, d_sum, d_low, d_mix, grads, send
):
    upstream = d_third[...] + through(place, d_hidden, w_in)
    back, d_gain, d_shift = norm_back(upstream, second_sum[...], vec[GAIN + 1 : GAIN + 2])
    d_sum[...] = back
    low = back.astype(LOW)
    d_low[...] = low
    grads[0:1, :] = column_sum(low)
    grads[1:2, :] = d_shift
    grads[2:3, :] = d_gain
    d_mix[...] = through(place, d_low, w_out).astype(LOW)
    give(place, send, d_low)


def cross_backward(place, query, kv, probs, d_mix, d_query, d_other, d_mine, grads):
    rows, half = query.shape
    for h in range(half // PAIR):
        at, beside = pl.ds(h * PAIR, PAIR), pl.ds(half + h * PAIR, PAIR)
        dq, dk, dv = attend_back(
            query[:, at],
            kv[0, :, at],
            kv[0, :, beside],
            probs[0, 0, pl.ds(h * 2 * rows, 2 * rows), :],
            d_mix[:, at],
        )
        d_query[:, at] = dq.astype(LOW)
        low = dv.astype(LOW)

        @pl.when(pl.program_id(0) == 0)
        def _(at=at, beside=beside, dk=dk, low=low):
            d_other[:, at] = dk.astype(LOW)
            d_other[:, beside] = low

        @pl.when(pl.program_id(0) == 1)
        def _(at=at, beside=beside, dk=dk, low=low):
            d_mine[:, at] = dk.astype(LOW)
            d_mine[:, beside] = low

        sums = column_sum(low)
        before = jnp.where(pl.program_id(1) == 0, 0.0, grads[0, :, at])
        grads[0, :, at] = before + sums


def self_backward(
    place, w_query, w_out, d_query, d_sum2, first_sum, vec, joined, probs,
    d_sum, d_low, d_joined, grads, send,
):
    width = d_sum.shape[-1]
    upstream = d_sum2[...] + through(place, d_query, w_query)
    back, d_gain, d_shift = norm_back(upstream, first_sum[...], vec[GAIN : GAIN + 1])
    d_sum[...] = back
    low = back.astype(LOW)
    d_low[...] = low
    d_mix = through(place, d_low, w_out).astype(LOW)
    rows = probs.shape[-1]
    heads = width // PAIR
    for p in range(d_sum.shape[0] // rows):
        at = pl.ds(p * rows, rows)
        for h in range(heads):
            where = [pl.ds(i * width + h * PAIR, PAIR) for i in range(3)]
            q, k, v = (joined[at, w] for w in where)
            found = attend_back(
                q,
                k,
                v,
                probs[pl.ds((p * heads + h) * 2 * rows, 2 * rows), :],
                d_mix[p * rows : (p + 1) * rows, h * PAIR : (h + 1) * PAIR],
            )
            for w, value in zip(where, found):
                d_joined[at, w] = value.astype(LOW)
    grads[0:1, :] = column_sum(d_joined[:, :width])
    grads[1:2, :] = column_sum(d_joined[:, 2 * width :])
    grads[2:3, :] = column_sum(low)
    grads[3:4, :] = column_sum(d_query[...])
    grads[4:5, :] = d_shift
    grads[5:6, :] = d_gain
    give(place, send, d_joined)
    give(place, send, d_low, 3 * width // 4)
    give(place, send, d_query, width)


def input_back(place, weight, d_joined, d_sum, out):
    out[...] = d_sum[...] + through(place, d_joined, weight)


def table_back(place, weight, d_mine, d_other, out):
    @pl.when(pl.program_id(0) == 0)
    def _():
        weight.wait(0)
        weight.wait(1)

    half = d_mine.shape[-1] // 2
    total = 0
    for side, d in enumerate((d_mine, d_other)):
        for y in range(2):
            total += dot_t(d[:, y * half : (y + 1) * half], weight.part(side, y))
    out[...] = total


def quarter_place(step, place):
    c = place[2]
    dy = jnp.where(step == 0, 1, jnp.where(step == 1, 1 - c, jnp.where(step == 2, c, 0)))
    dx = jnp.where(step == 0, 1, jnp.where(step == 1, c, jnp.where(step == 2, 1 - c, 0)))
    return place[0] ^ dy, place[1] ^ dx


def quarter_grads(net, name, products, more):
    lines = net.lines
    ins = []
    for left, left2, right, right2, size, first in products:
        for a in (left, left2):
            view = a.reshape(lines, 2, -1, a.shape[-1])
            block = (lines, 1) + view.shape[2:]
            ins.append((view, block, lambda s, at: (0, quarter_place(s, at)[1], 0, 0)))
        if first is None:
            for a in (right, right2):
                ins.append(
                    (a, (a.shape[0], size), lambda s, at: (0, quarter_place(s, at)[0]))
                )
        else:
            ins.append(
                (
                    right,
                    (right.shape[0], size),
                    lambda s, at: (0, 2 * quarter_place(s, at)[0] + at[2]),
                )
            )
            ins.append(
                (
                    right2,
                    (1, right2.shape[1], size),
                    lambda s, at, first=first: (quarter_place(s, at)[0], 0, first),
                )
            )
    rows = products[0][0].shape[0] // net.wide
    cols = sum(p[4] for p in products)
    extra = more[0].shape[3] if more else 0
    for a in more or ():

        def corner(s, at):
            y, x = quarter_place(s, at)
            return (y, 0, x, 0, 0)

        ins.append((a, (1, lines, 1, extra, cols), corner))

    def body(place, *refs):
        outs = refs[len(ins) :]
        quarters = []
        start = 0
        for i, (_, _, _, _, size, first) in enumerate(products):
            left, left2, right, right2 = refs[4 * i : 4 * i + 4]
            l, l2 = (a[:, 0].reshape(lines * rows, -1) for a in (left, left2))
            r2 = right2[...] if first is None else right2[0]
            value = dot(l, right[...]) + dot(l2, r2)
            quarters.append((start, size, value.astype(LOW).reshape(lines, rows, size)))
            start += size

        def put(out):
            for z in range(lines):
                differs = place[3] ^ z
                to = sum(
                    ((differs >> bit) & 1) * (lines >> (bit + 1))
                    for bit in range(lines.bit_length() - 1)
                )
                for start, size, value in quarters:
                    out[to, :rows, start : start + size] = value[z]
                if extra:
                    a, b = refs[4 * len(products) : len(ins)]
                    value = a[0, z, 0].astype(FULL) + b[0, z, 0].astype(FULL)
                    out[to, rows:, :] = value.astype(LOW)

        step = pl.program_id(0)
        pl.when(step < 2)(lambda: put(outs[0].at[0]))
        pl.when(step == 2)(lambda: put(outs[1]))
        pl.when(step == 3)(lambda: put(outs[2]))

    shape = (lines, rows + extra, cols)
    return call(
        body,
        name,
        net,
        (4,),
        ins,
        [
            ((2,) + shape, LOW, (1,) + shape, lambda s, at: (jnp.minimum(s, 1), 0, 0, 0)),
            whole_out(shape, LOW),
            whole_out(shape, LOW),
        ],
    )


def segment_index(lengths, count):
    segment_ends = jnp.cumsum(lengths, axis=-1)
    position = jnp.arange(count, dtype=jnp.int32)
    passed = (position[None, :, None] >= segment_ends[:, None, :]).astype(jnp.int32)
    return jnp.sum(passed, axis=-1)


def per_device(
    inputs,
    memory,
    cotangent,
    dec_lengths,
    mem_lengths,
    seg_table,
    self_qkv,
    self_out,
    cross_q,
    cross_kv,
    cross_out,
    fc_in,
    fc_out,
    vec_bias,
    norm_gain,
    fc_in_bias,
    *,
    wide,
    narrow,
):
    net = Net(wide, narrow)
    Order.last = Order.soon = Order.later = ()
    pairs, length, width = inputs.shape
    held = memory.shape[1]
    x = inputs.reshape(-1, width)
    table = memory.reshape(-1, width)
    upstream = cotangent.reshape(-1, width)
    count, quarter, half = x.shape[0], width // narrow, width // 2
    hidden = fc_out.shape[0] * wide

    rows = jnp.concatenate([vec_bias, norm_gain])
    small = jnp.concatenate([rows.reshape(-1), fc_in_bias])
    extra = 16
    small_rows = jnp.zeros((extra, self_qkv.shape[1]), LOW).at[0, : small.size].set(small)
    table2 = net.over_core(table)
    g2 = Weight(net, jnp.concatenate([self_qkv, small_rows])).at_once()
    g2.rows = self_qkv.shape[0]
    shards = jnp.concatenate([cross_kv, cross_out, self_out, cross_q], axis=1)
    g3, g4, g5 = Weight(net, shards), Weight(net, fc_in), PairedWeight(net, fc_out).begin()
    g2.start(g5.mate)
    g3.line(g2.held, g5.mate)
    Order.need(table2, *g2.copy("held", after=g5.mate))
    g3.line_on()
    g4.line()
    g2.turn()
    Order.need(*g2.copy("one", "two"))
    if net.lines == 4:
        Order.need(g4.got)
    g3.line_end()
    g3.start()
    g4.line_on()
    g5.pair().line()
    g2.copy("three")

    segments = segment_index(dec_lengths, length)
    tables = segment_index(mem_lengths, held)
    matches = segments[:, :, None] == jnp.arange(dec_lengths.shape[-1], dtype=jnp.int32)
    query_table = jnp.sum(jnp.where(matches, seg_table[:, None, :], 0), axis=-1)
    seg_col, seg_row = segments.reshape(-1, 1), segments.reshape(pairs, 1, length)
    table_col, table_row = query_table.reshape(-1, 1), tables.reshape(pairs, 1, held)

    def in_place(pieces):
        sides = []
        for side, (same, one, two, three) in enumerate((pieces[:4], pieces[4:])):
            first = (net.c ^ side) == 0
            by_x = jnp.where(first, one, two)
            by_y = jnp.where(first, two, one)
            sides.append(jnp.stack([jnp.stack([same, by_x]), jnp.stack([by_y, three])]))
        out = jnp.stack(net.swap(*sides))
        out = jnp.where(net.y == 0, out, out[:, ::-1])
        out = jnp.where(net.x == 0, out, out[:, :, ::-1])
        return jnp.transpose(out, (3, 2, 1, 0, 4)).reshape(wide, narrow, -1)

    vectors = in_place([p[:, self_qkv.shape[0], : small.size] for p in g2.arrays()]).astype(FULL)
    fc_bias = vectors[:, :, rows.size :].reshape(1, -1)
    vec = vectors[:, :, : rows.size].reshape(wide * narrow, rows.shape[0], -1)
    vec = jnp.transpose(vec, (1, 0, 2)).reshape(rows.shape[0], width)
    joined_bias = jnp.concatenate([vec[0], jnp.zeros((width,), FULL), vec[1]])[None]

    heads = width // PAIR
    joined, self_probs, self_mix, x_t, self_mix_t = call(
        self_forward,
        "self_forward",
        net,
        (1,),
        [whole(x), whole(joined_bias), whole(seg_col), whole(seg_row)],
        [
            whole_out((count, 3 * width), LOW),
            whole_out((pairs * heads * 2 * length, length), LOW),
            whole_out((count, width), LOW),
            whole_out((width, count), LOW),
            whole_out((width, count), LOW),
        ],
        weights=[(g2, 0, 3 * quarter)],
    )
    g4.line_end()
    g5.line_on()
    g3.turn()
    copies = g3.copy("held", "one", "two")
    g4.start(*copies)
    g3.copy("three")
    first_sum, first_low_t, query = call(
        first_half,
        "first_half",
        net,
        (1,),
        [whole(self_mix), whole(x), whole(vec)],
        [
            whole_out((count, width), FULL),
            whole_out((width, count), LOW),
            whole_out((count, width), LOW),
        ],
        [pltpu.VMEM((count, width), FULL)],
        weights=[(g3, 3 * quarter, quarter), (g3, 4 * quarter, quarter)],
    )
    tile = 512
    kv, table_t, table_t2 = call(
        table_keys,
        "table_keys",
        net,
        (table.shape[0] // tile,),
        [
            (table, (tile, width), lambda t, at: (t, 0)),
            (table2, (tile, width), lambda t, at: (t, 0)),
            whole(vec),
        ],
        [
            ((2, table.shape[0], width), LOW, (2, tile, width), lambda t, at: (0, t, 0)),
            ((width, table.shape[0]), LOW, (width, tile), lambda t, at: (0, t)),
            ((width, table.shape[0]), LOW, (width, tile), lambda t, at: (0, t)),
        ],
        weights=[(g3, 0, half)],
    )
    g4.turn()
    g4.copy("held", "one")
    g5.line_end()
    g5.turn()
    g5.copy("held")
    score_rows = half // PAIR * 2 * length
    core_block = ((length, half), lambda s, p, at: (p, at[2] ^ s))
    cross_mix, cross_probs, cross_mix_t = call(
        cross_forward,
        "cross_forward",
        net,
        (2, pairs),
        [
            (query, *core_block),
            (kv, (1, held, width), lambda s, p, at: (s, p, 0)),
            (table_col, (length, 1), lambda s, p, at: (p, 0)),
            (table_row, (1, 1, held), lambda s, p, at: (p, 0, 0)),
        ],
        [
            ((count, width), LOW, *core_block),
            (
                (2, pairs, score_rows, held),
                LOW,
                (1, 1, score_rows, held),
                lambda s, p, at: (s, p, 0, 0),
            ),
            ((width, count), LOW, (half, length), lambda s, p, at: (at[2] ^ s, p)),
        ],
    )
    g4.copy("two", "three")
    second_sum, second_low, second_low_t = call(
        second_half,
        "second_half",
        net,
        (1,),
        [whole(cross_mix), whole(first_sum), whole(vec)],
        [
            whole_out((count, width), FULL),
            whole_out((count, width), LOW),
            whole_out((width, count), LOW),
        ],
        [pltpu.VMEM((count, width), FULL)],
        weights=[(g3, half, quarter)],
    )
    active, slope, active_t = call(
        feed_in,
        "feed_in",
        net,
        (1,),
        [whole(second_low), whole(fc_bias)],
        [
            whole_out((count, hidden), LOW),
            whole_out((count, hidden), LOW),
            whole_out((hidden, count), LOW),
        ],
        weights=[(g4, 0, hidden // 4)],
    )
    g5.copy("far")
    active_t2, second_low_t2 = (net.over_core(a, g5.far) for a in (active_t, second_low_t))
    output, d_third, d_low3, grads3, send3 = call(
        feed_out,
        "feed_out",
        net,
        (1,),
        [whole(active), whole(second_sum), whole(upstream), whole(vec)],
        [
            whole_out((count, width), LOW),
            whole_out((count, width), FULL),
            whole_out((count, width), LOW),
            whole_out((8, width), FULL),
            whole_out((2, count, quarter), LOW),
        ],
        [pltpu.VMEM((count, width), FULL)],
        weights=[(g5, 0, quarter)],
    )

    got3 = net.over_core(send3)
    first_low_t2, self_mix_t2, cross_mix_t2, x_t2 = Order.pin(
        *(net.over_core(a) for a in (first_low_t, self_mix_t, cross_mix_t, x_t))
    )
    r_out = Reduction(net, "grad_out", [(active_t, active_t2, d_low3, got3, quarter, 0)]).start()
    d_hidden, g_fc_bias, send_hidden = call(
        feed_out_back,
        "feed_out_back",
        net,
        (1,),
        [whole(d_low3), whole(slope)],
        [
            whole_out((count, hidden), LOW),
            whole_out((1, hidden), FULL),
            whole_out((2, count, hidden // 4), LOW),
        ],
        weights=[(g5, 0, quarter)],
    )
    got_hidden = net.over_core(send_hidden)
    d_sum2, d_low2, d_mix, grads2, send2 = call(
        feed_in_back,
        "feed_in_back",
        net,
        (1,),
        [whole(d_hidden), whole(d_third), whole(second_sum), whole(vec)],
        [
            whole_out((count, width), FULL),
            whole_out((count, width), LOW),
            whole_out((count, width), LOW),
            whole_out((8, width), FULL),
            whole_out((2, count, quarter), LOW),
        ],
        weights=[(g4, 0, hidden // 4), (g3, half, quarter)],
    )
    got2 = net.over_core(send2)
    Order.need(got2)
    r_in = Reduction(
        net, "grad_in", [(second_low_t, second_low_t2, d_hidden, got_hidden, hidden // 4, 0)]
    ).start()
    r_out.turn()
    back_block = ((length, half), lambda s, p, at: (p, at[2] ^ 1 ^ s))
    d_query, d_other, d_mine, grads_v = call(
        cross_backward,
        "cross_backward",
        net,
        (2, pairs),
        [
            (query, *back_block),
            (kv, (1, held, width), lambda s, p, at: (1 - s, p, 0)),
            (cross_probs, (1, 1, score_rows, held), lambda s, p, at: (1 - s, p, 0, 0)),
            (d_mix, *back_block),
        ],
        [
            ((count, width), LOW, *back_block),
            (
                table.shape,
                LOW,
                (held, width),
                lambda s, p, at: (jnp.where(s == 0, p, pairs - 1), 0),
            ),
            (table.shape, LOW, (held, width), lambda s, p, at: (jnp.where(s == 0, 0, p), 0)),
            ((2, 1, half), FULL, (1, 1, half), lambda s, p, at: (1 - s, 0, 0)),
        ],
    )
    d_sum1, d_low1, d_joined, grads1, send1 = call(
        self_backward,
        "self_backward",
        net,
        (1,),
        [
            whole(d_query),
            whole(d_sum2),
            whole(first_sum),
            whole(vec),
            whole(joined),
            whole(self_probs),
        ],
        [
            whole_out((count, width), FULL),
            whole_out((count, width), LOW),
            whole_out((count, 3 * width), LOW),
            whole_out((8, width), FULL),
            whole_out((2, count, 5 * quarter), LOW),
        ],
        weights=[(g3, 4 * quarter, quarter), (g3, 3 * quarter, quarter)],
    )
    waits = (r_out.near, r_in.pair)
    got1, got_table = net.over_core(send1, *waits), net.over_core(d_other, *waits)
    r_out.line()
    r_in.turn()
    r_self = Reduction(
        net,
        "grad_self",
        [
            (x_t, x_t2, d_joined, got1, 3 * quarter, 0),
            (self_mix_t, self_mix_t2, d_low1, got1, quarter, 3),
            (first_low_t, first_low_t2, d_query, got1, quarter, 4),
        ],
    ).start(r_in.near, r_out.step, got_table)
    grads_v = jnp.concatenate(net.swap(grads_v[0], grads_v[1]), axis=1)
    g_rows = jnp.concatenate(
        [
            grads1[:4],
            grads_v,
            grads2[:1],
            grads3[:1],
            grads1[4:5],
            grads2[1:2],
            grads3[1:2],
            grads1[5:6],
            grads2[2:3],
            grads3[2:3],
        ]
    )
    g_rows = jnp.transpose(g_rows.reshape(rows.shape[0], wide, narrow, -1), (2, 1, 0, 3))
    g_small = jnp.transpose(g_fc_bias.reshape(wide, narrow, -1), (1, 0, 2))
    g_small = jnp.concatenate([g_rows.reshape(narrow, wide, -1), g_small], axis=2).astype(LOW)
    room = extra * 3 * quarter - small.size
    g_small = jnp.pad(g_small, ((0, 0), (0, 0), (0, room)))
    g_small = g_small.reshape(2, 2, wide // 2, 2, extra, -1)
    small_mine, small_other = net.swap(g_small[:, 0], g_small[:, 1])
    small_got = net.over_core(small_other)
    r_out.line_on()
    r_in.line()
    r_cross = Reduction(
        net,
        "grad_cross",
        [
            (table_t, table_t2, d_mine, got_table, half, None),
            (cross_mix_t, cross_mix_t2, d_low2, got2, quarter, 0),
        ],
        (small_mine, small_got),
    ).start()
    r_out.line_end()
    r_in.line_on()
    (input_grad,) = call(
        input_back,
        "input_back",
        net,
        (1,),
        [whole(d_joined), whole(d_sum1)],
        [whole_out((count, width), FULL)],
        weights=[(g2, 0, 3 * quarter)],
    )
    r_in.line_end()
    r_self.turn(r_in.total, r_out.total)
    tile = 512
    (memory_grad,) = call(
        table_back,
        "table_back",
        net,
        (table.shape[0] // tile,),
        [(d, (tile, width), lambda t, at: (t, 0)) for d in (d_mine, d_other)],
        [(table.shape, FULL, (tile, width), lambda t, at: (t, 0))],
        weights=[(g3, 0, half)],
    )
    r_cross.turn(r_self.near)
    r_self.line(r_cross.ready)
    r_self.line_on()
    r_cross.line()
    r_self.line_end()
    r_cross.line_on().line_end()

    g_out, g_in, g_cross, g_self = (r.total for r in (r_out, r_in, r_cross, r_self))
    g_small = g_cross[-extra:].reshape(-1)[: small.size]
    g_rows, g_fc_bias = g_small[: rows.size].reshape(rows.shape), g_small[rows.size :]
    return (
        output.reshape(inputs.shape),
        input_grad.reshape(inputs.shape),
        memory_grad.reshape(memory.shape),
        g_self[:, : 3 * quarter],
        g_self[:, 3 * quarter : 4 * quarter],
        g_self[:, 4 * quarter :],
        g_cross[:-extra, : 2 * quarter],
        g_cross[:-extra, 2 * quarter :],
        g_in,
        g_out,
        g_rows[:10],
        g_rows[10:],
        g_fc_bias,
    )


def solution(mesh):
    tokens = P(BOTH, None, None)
    lengths = P(BOTH, None)
    weight = P("wide", "narrow")
    vector = P(None, BOTH)
    return jax.shard_map(
        partial(per_device, wide=mesh.shape["wide"], narrow=mesh.shape["narrow"]),
        mesh=mesh,
        in_specs=(tokens,) * 3 + (lengths,) * 3 + (weight,) * 7 + (vector, vector, P(BOTH)),
        out_specs=(tokens,) * 3 + (weight,) * 7 + (vector, vector, P(BOTH)),
        check_vma=False,
    )
```

```python
import math
from functools import partial

import jax
import jax.numpy as jnp
from jax import lax
from jax.experimental import pallas as pl
from jax.experimental.pallas import tpu as pltpu
from jax.sharding import PartitionSpec as P

HD = 64
PAIR = 2 * HD
BOTH = ("wide", "narrow")
EPS = 1e-05
MASKED_SCORE = -1000000000.0
LOW = jnp.bfloat16
FULL = jnp.float32
VMEM_BYTES = 60 * 1024 * 1024
B_QUERY, B_VALUE, B_SELF_OUT, B_CROSS_Q, B_CROSS_V, B_CROSS_OUT, B_FC_OUT = range(7)
SHIFT, GAIN = 7, 10


def after(value, *others):
    return lax.optimization_barrier((value, others))[0]


class Order:
    last, soon, later = (), (), ()

    @classmethod
    def put(cls, kernel, arrays):
        first = after(arrays[0], *cls.last, *cls.soon)
        out = kernel(first, *arrays[1:])
        cls.last, cls.soon, cls.later = (out[0],), cls.later, ()
        return out

    @classmethod
    def now(cls, value, *others):
        return after(value, *cls.last, *others)

    @classmethod
    def need(cls, *arrays):
        cls.soon += arrays

    @classmethod
    def pin(cls, *arrays):
        cls.later += arrays
        return arrays


class Net:
    def __init__(self, wide, narrow):
        self.wide, self.narrow, self.lines = wide, narrow, wide // 2
        w, n = lax.axis_index("wide"), lax.axis_index("narrow")
        self.z, self.x, self.y, self.c = w // 2, w % 2, n // 2, n % 2
        self.place = jnp.stack([self.y, self.x, self.c, self.z]).astype(jnp.int32)
        both = [(i, j) for i in range(wide) for j in range(narrow)]

        def flat(i, j):
            return i * narrow + j

        def pairs(x_core):
            return [
                (flat(i, j), flat(i ^ 1, j) if j % 2 == x_core else flat(i, j ^ 2)) for i, j in both
            ]

        self.first, self.second = pairs(0), pairs(1)
        self.core = [(j, j ^ 1) for j in range(narrow)]
        self.groups = [[z * 2 + x for z in range(self.lines)] for x in range(2)]

    def across(self, value, way, *others):
        return lax.ppermute(Order.now(value, *others), BOTH, way)

    def over_core(self, value, *others):
        return lax.ppermute(Order.now(value, *others), "narrow", self.core)

    def along(self, value, step, *others):
        way = [(w, ((w // 2) ^ step) * 2 + w % 2) for w in range(self.wide)]
        return lax.ppermute(Order.now(value, *others), "wide", way)

    def swap(self, a, b):
        first = self.c == 0
        return jnp.where(first, a, b), jnp.where(first, b, a)


class Weight:
    def __init__(self, net, shard, before=()):
        self.net = net
        self.rows = shard.shape[0]
        self.shard = after(shard, *before)

    def at_once(self):
        self.held = lax.all_gather(
            self.shard, "wide", axis=0, axis_index_groups=self.net.groups
        )
        return self

    def line(self, *others):
        net = self.net
        if net.lines == 4:
            self.got = net.along(self.shard, 2, *others)
        return self

    def line_on(self):
        net = self.net
        if net.lines == 4:
            self.held = stack(net, [self.shard, self.got], 1)
            self.got = net.along(self.held, 1)
        return self

    def line_end(self):
        net = self.net
        if net.lines == 4:
            self.held = stack(net, [self.held, self.got], 0)
        else:
            self.at_once()
        return self

    def start(self, *others):
        net = self.net
        self.one = net.across(self.held, net.first, *others)
        self.two = net.across(self.held, net.second, *others)
        return self

    def turn(self, *others):
        net = self.net
        self.three = net.across(self.one, net.second, self.two, *others)
        return self

    def copy(self, *names, after=None):
        others = () if after is None else (after,)
        new = [self.net.over_core(getattr(self, name), *others) for name in names]
        self.copies = [*getattr(self, "copies", ()), *new]
        return new

    def arrays(self):
        return [self.held, self.one, self.two, self.three, *self.copies]

    def spots(self):
        return [(i, 0) for i in range(8)]


class PairedWeight(Weight):
    def begin(self, *others):
        self.mate = self.net.across(self.shard, self.net.first, *others)
        return self

    def pair(self):
        self.single = self.rows
        self.shard = jnp.concatenate([self.shard, self.mate])
        return self

    def turn(self, *others):
        self.far = self.net.across(self.held, self.net.second, *others)
        return self

    def arrays(self):
        return [self.held, self.far, *self.copies]

    def spots(self):
        return [(2 * side + k // 2, k % 2 * self.rows) for side in range(2) for k in range(4)]


def piece_place(place, index):
    side, k = divmod(index, 4)
    c = place[2] ^ side
    dy, dx = ((0, 0), (c, 1 - c), (1 - c, c), (1, 1))[k]
    return place[0] ^ dy, place[1] ^ dx, side


class Loaded:
    def __init__(self, place, arrays, spots, buffer, sems, rows, col):
        self.buffer = buffer
        size = buffer.shape[-1]
        self.copies = []
        for i, (array, first) in enumerate(spots):
            y, x, side = piece_place(place, i)
            self.copies.append(
                pltpu.make_async_copy(
                    arrays[array].at[:, pl.ds(first, rows), pl.ds(col, size)],
                    buffer.at[side, y, :, x],
                    sems.at[i],
                )
            )

    def start(self):
        for copy in self.copies:
            copy.start()

    def wait(self, side):
        for copy in self.copies[4 * side : 4 * side + 4]:
            copy.wait()

    def part(self, side, y):
        return self.buffer[side, y].reshape(-1, self.buffer.shape[-1])


class Reduction:
    def __init__(self, net, name, products, more=None):
        self.net = net
        self.pair, self.near, self.own = quarter_grads(net, name, products, more)

    def start(self, *others):
        self.pair = self.net.across(self.pair, self.net.second, *others)
        return self

    def turn(self, *others):
        pair = Order.now(self.pair, *others)
        self.ready = (self.near.astype(FULL) + pair[0].astype(FULL)).astype(LOW)
        Order.need(self.ready)
        self.near = self.net.across(self.ready, self.net.first)
        return self

    def line(self, *others):
        net = self.net
        near = Order.now(self.near, *others)
        total = self.own.astype(FULL) + self.pair[1].astype(FULL) + near.astype(FULL)
        self.total = total.astype(LOW)
        Order.need(self.total)
        self.step = net.along(self.total[total.shape[0] // 2 :], 1)
        return self

    def line_on(self):
        net = self.net
        half, step = self.total.shape[0] // 2, 2
        total = self.total[:half].astype(FULL) + Order.now(self.step).astype(FULL)
        while half > 2:
            half //= 2
            low = total.astype(LOW)
            got = net.along(low[half:], step)
            total = low[:half].astype(FULL) + got.astype(FULL)
            step *= 2
        self.total = total.astype(LOW)
        Order.need(self.total)
        if half > 1:
            self.step = net.along(self.total[1:], step)
        return self

    def line_end(self):
        total = self.total[0].astype(FULL)
        if self.total.shape[0] > 1:
            total += Order.now(self.step)[0].astype(FULL)
        self.total = total
        return self


def call(body, name, net, grid, ins, outs, scratch=(), weights=(), into=()):
    operands, buffers, first = [], [], []
    for weight, _, size in weights:
        first.append(len(operands))
        operands += weight.arrays()
        shape = (2, 2, net.lines, 2, weight.rows, size)
        buffers += [pltpu.VMEM(shape, LOW), pltpu.SemaphoreType.DMA((8,))]
    plain = len(ins) + len(outs)
    fixed = len(operands)
    operands += into
    specs = [pl.BlockSpec(memory_space=pl.ANY)] * len(operands)

    def run(place, *refs):
        pieces, rest = refs[:fixed], refs[len(operands) :]
        held = rest[plain : plain + len(buffers)]
        rest = rest[:plain] + rest[plain + len(buffers) :]
        loaded = [
            Loaded(
                place,
                pieces[first[i] :],
                weight.spots(),
                held[2 * i],
                held[2 * i + 1],
                weight.rows,
                col,
            )
            for i, (weight, col, _) in enumerate(weights)
        ]

        def start():
            for weight in loaded:
                weight.start()

        if grid == (1,):
            start()
        elif loaded:
            pl.when(pl.program_id(0) == 0)(start)
        body(place, *loaded, *rest)

    kernel = pl.pallas_call(
        run,
        grid_spec=pltpu.PrefetchScalarGridSpec(
            num_scalar_prefetch=1,
            grid=grid,
            in_specs=specs + [pl.BlockSpec(b, m) for _, b, m in ins],
            out_specs=[pl.BlockSpec(b, m) for _, _, b, m in outs],
            scratch_shapes=[*buffers, *scratch],
        ),
        out_shape=[jax.ShapeDtypeStruct(s, d) for s, d, _, _ in outs],
        compiler_params=pltpu.CompilerParams(
            dimension_semantics=("arbitrary",) * len(grid), vmem_limit_bytes=VMEM_BYTES
        ),
        cost_estimate=pl.CostEstimate(flops=1000, bytes_accessed=1000, transcendentals=0),
        input_output_aliases={1 + fixed + i: i for i in range(len(into))},
        name=name,
    )
    return Order.put(partial(kernel, net.place), [*operands, *(a for a, _, _ in ins)])


def stack(net, pieces, bit):
    rows, cols = pieces[0].shape[-2:]

    def body(place, *refs):
        for i in range(2):

            @pl.when(pl.program_id(0) == i)
            def _(i=i):
                refs[-1][:, 0] = refs[i][...].reshape(-1, rows, cols)

    lead = pieces[0].size // (rows * cols)
    shape = (lead, 2, rows, cols)
    (out,) = call(
        body,
        "stack",
        net,
        (2,),
        [whole(p) for p in pieces],
        [(shape, LOW, (lead, 1, rows, cols), lambda s, at: (0, ((at[3] >> bit) & 1) ^ s, 0, 0))],
    )
    return out.reshape(2 * lead, rows, cols)


def whole(array):
    return (array, array.shape, lambda *_: (0,) * array.ndim)


def whole_out(shape, dtype):
    return (shape, dtype, shape, lambda *_: (0,) * len(shape))


def lanes(index, size):
    return pl.ds(pl.multiple_of(index * size, 128), size)


def block_of(place, side, y):
    return 2 * y + (place[2] ^ side)


def each_block(place, weight, wait=True):
    for side in range(2):
        if wait:
            weight.wait(side)
        for y in range(2):
            yield side, y, block_of(place, side, y)


def dot(a, b):
    return jnp.dot(a, b, preferred_element_type=FULL)


def dot_t(a, b):
    return lax.dot_general(a, b, (((1,), (1,)), ((), ())), preferred_element_type=FULL)


def t_dot(a, b):
    return lax.dot_general(a, b, (((0,), (0,)), ((), ())), preferred_element_type=FULL)


def norm_parts(z):
    centred = z - jnp.mean(z, axis=-1, keepdims=True)
    scale = lax.rsqrt(jnp.mean(centred * centred, axis=-1, keepdims=True) + EPS)
    return centred * scale, scale


def norm(z, vec, which):
    unit, _ = norm_parts(z)
    return unit * vec[GAIN + which : GAIN + which + 1] + vec[SHIFT + which : SHIFT + which + 1]


def norm_back(upstream, z, gain):
    unit, scale = norm_parts(z)
    d_gain = jnp.sum(upstream * unit, axis=0, keepdims=True)
    d_shift = jnp.sum(upstream, axis=0, keepdims=True)
    inner = upstream * gain
    mean = jnp.mean(inner, axis=-1, keepdims=True)
    along = jnp.mean(inner * unit, axis=-1, keepdims=True)
    return scale * (inner - mean - unit * along), d_gain, d_shift


def column_sum(values):
    return jnp.sum(values.astype(FULL), axis=0, keepdims=True)


def two_heads(rows):
    low = lax.broadcasted_iota(jnp.int32, rows.shape, 1) < HD
    none = jnp.zeros_like(rows)
    return jnp.concatenate([jnp.where(low, rows, none), jnp.where(low, none, rows)], axis=0)


def one_row(stacked):
    half = stacked.shape[0] // 2
    low = lax.broadcasted_iota(jnp.int32, (half, PAIR), 1) < HD
    return jnp.where(low, stacked[:half], stacked[half:])


def one_side(stacked):
    half = stacked.shape[1] // 2
    low = lax.broadcasted_iota(jnp.int32, (PAIR, half), 0) < HD
    return jnp.where(low, stacked[:, :half], stacked[:, half:])


def softmax_sides(query, keys, allowed):
    logits = jnp.where(allowed, dot_t(keys, two_heads(query)) * HD ** (-0.5), MASKED_SCORE)
    weight = jnp.exp(logits - jnp.max(logits, axis=0, keepdims=True))
    return (weight * (1.0 / jnp.sum(weight, axis=0, keepdims=True))).astype(LOW)


def softmax_rows(query, keys, allowed):
    logits = jnp.where(allowed, dot_t(two_heads(query), keys) * HD ** (-0.5), MASKED_SCORE)
    weight = jnp.exp(logits - jnp.max(logits, axis=-1, keepdims=True))
    return (weight * (1.0 / jnp.sum(weight, axis=-1, keepdims=True))).astype(LOW)


def attend_back_rows(query, keys, values, probs, upstream, mix):
    queries, ups = two_heads(query), two_heads(upstream)
    product = two_heads(upstream.astype(FULL) * mix.astype(FULL))
    row_dot = jnp.sum(product, axis=1, keepdims=True)
    d_scores = (probs.astype(FULL) * (dot_t(ups, values) - row_dot)).astype(LOW)
    scale = HD ** (-0.5)
    return one_row(dot(d_scores, keys)) * scale, t_dot(d_scores, queries) * scale, t_dot(probs, ups)


def row_dots(mix, upstream):
    product = (mix.astype(FULL) * upstream.astype(FULL)).T
    sums = [
        jnp.sum(product[i : i + HD], axis=0, keepdims=True) for i in range(0, product.shape[0], HD)
    ]
    return [jnp.concatenate(sums[i : i + 2], axis=1) for i in range(0, len(sums), 2)]


def attend_back_sides(query, keys, values, probs, upstream, row_dot):
    queries, ups = two_heads(query), two_heads(upstream)
    scale = HD ** (-0.5)
    d_scores = (probs.astype(FULL) * (dot_t(values, ups) - row_dot)).astype(LOW)
    d_query = one_side(t_dot(keys, d_scores)).T * scale
    return d_query, dot(d_scores, queries) * scale, dot(probs, ups)


def twice(mask, axis):
    wide = jnp.where(mask, 1, 0)
    return jnp.concatenate([wide, wide], axis=axis) == 1


def self_forward(
    place, weight, x, bias, seg_col, seg_row, joined, probs, mix, x_t, mix_t
):
    x_t[...] = x[...].T
    for side, y, n in each_block(place, weight):
        w = weight.part(side, y)
        at = lanes(n, w.shape[-1])
        joined[:, at] = (dot(x[...], w) + bias[:, at]).astype(LOW)
    width, rows = mix.shape[1], seg_row.shape[-1]
    above = lax.broadcasted_iota(jnp.int32, (rows, rows), 0) <= lax.broadcasted_iota(
        jnp.int32, (rows, rows), 1
    )
    for p in range(mix.shape[0] // rows):
        at = pl.ds(p * rows, rows)
        allowed = twice((seg_col[at, :] == seg_row[p]) & above, 1)
        for h in range(width // PAIR):
            q, k, v = (joined[at, pl.ds(i * width + h * PAIR, PAIR)] for i in range(3))
            low = softmax_sides(q, k, allowed)
            probs[pl.ds((p * (width // PAIR) + h) * rows, rows), :] = low
            mixed = one_side(t_dot(v, low)).astype(LOW)
            mix_t[pl.ds(h * PAIR, PAIR), at] = mixed
            mix[at, pl.ds(h * PAIR, PAIR)] = mixed.T


def first_half(place, w_out, w_query, mix, x, vec, first_sum, low_t, query, acc):
    for side, y, n in each_block(place, w_out):
        w = w_out.part(side, y)
        acc[:, lanes(n, w.shape[-1])] = dot(mix[...], w)
    z = x[...].astype(FULL) + (acc[...] + vec[B_SELF_OUT : B_SELF_OUT + 1, :])
    first_sum[...] = z
    low = norm(z, vec, 0).astype(LOW)
    low_t[...] = low.T
    for side, y, n in each_block(place, w_query):
        w = w_query.part(side, y)
        at = lanes(n, w.shape[-1])
        query[:, at] = (dot(low, w) + vec[B_CROSS_Q : B_CROSS_Q + 1, at]).astype(LOW)


def table_keys(place, weight, x, x2, vec, out, x_t, x_t2):
    half = out.shape[-1] // 2

    @pl.when(pl.program_id(0) == 0)
    def _():
        weight.wait(0)
        weight.wait(1)

    for side in range(2):
        bias = vec[B_CROSS_V : B_CROSS_V + 1, lanes(place[2] ^ side, half)]
        out[side, :, :half] = dot(x[...], weight.part(side, 0)).astype(LOW)
        out[side, :, half:] = (dot(x[...], weight.part(side, 1)) + bias).astype(LOW)
    x_t[...] = x[...].T
    x_t2[...] = x2[...].T


def cross_forward(place, query, kv, table_col, table_row, mix, probs, mix_t):
    rows, half = query.shape
    allowed = twice(table_col[...] == table_row[0], 0)
    for h in range(half // PAIR):
        at = pl.ds(h * PAIR, PAIR)
        low = softmax_rows(query[:, at], kv[0, :, at], allowed)
        probs[0, 0, pl.ds(h * 2 * rows, 2 * rows), :] = low
        mixed = one_row(dot(low, kv[0, :, pl.ds(half + h * PAIR, PAIR)])).astype(LOW)
        mix[:, at] = mixed
        mix_t[at, :] = mixed.T


def second_half(place, weight, mix, first_sum, vec, second_sum, second_low, low_t, acc):
    for side, y, n in each_block(place, weight):
        w = weight.part(side, y)
        acc[:, lanes(n, w.shape[-1])] = dot(mix[...], w)
    z = norm(first_sum[...], vec, 0) + (acc[...] + vec[B_CROSS_OUT : B_CROSS_OUT + 1, :])
    second_sum[...] = z
    low = norm(z, vec, 1).astype(LOW)
    second_low[...] = low
    low_t[...] = low.T


def feed_in(place, weight, x, bias, active, slope, active_t):
    for side, y, n in each_block(place, weight):
        w = weight.part(side, y)
        cols = w.shape[-1]
        at = lanes(n, cols)
        hidden = dot(x[...], w) + bias[:, at]
        share = 0.5 + 0.5 * lax.erf(hidden * 2 ** (-0.5))
        low = (hidden * share).astype(LOW)
        active[:, at] = low
        active_t[pl.ds(pl.multiple_of(n * cols, 128), cols), :] = low.T
        density = jnp.exp(hidden * hidden * (-0.5)) * (2 * math.pi) ** (-0.5)
        slope[:, at] = (share + hidden * density).astype(LOW)


def give(place, send, rows, first=0):
    cols = rows.shape[-1] // 4
    for y in range(2):
        send[y, :, first : first + cols] = rows[:, lanes(block_of(place, 1, y), cols)]


def feed_out(
    place, weight, active, second_sum, cotangent, vec, output, d_third, d_low, grads, send, acc
):
    for side, y, n in each_block(place, weight):
        w = weight.part(side, y)
        acc[:, lanes(n, w.shape[-1])] = dot(active[...], w)
    z = norm(second_sum[...], vec, 1) + (acc[...] + vec[B_FC_OUT : B_FC_OUT + 1, :])
    output[...] = norm(z, vec, 2).astype(LOW)
    back, d_gain, d_shift = norm_back(cotangent[...].astype(FULL), z, vec[GAIN + 2 : GAIN + 3])
    d_third[...] = back
    low = back.astype(LOW)
    d_low[...] = low
    grads[0:1, :] = column_sum(low)
    grads[1:2, :] = d_shift
    grads[2:3, :] = d_gain
    give(place, send, d_low)


def through(place, rows, weight):
    total = 0
    for side, y, n in each_block(place, weight):
        w = weight.part(side, y)
        total += dot_t(rows[:, lanes(n, w.shape[-1])], w)
    return total


def feed_out_back(place, weight, d_third, slope, d_hidden, grads, send):
    _, _, lines, _, rows, cols = weight.buffer.shape
    weight.wait(0)
    weight.wait(1)
    step = max(1, min(lines, 1024 // (2 * rows)))
    for z in range(0, lines, step):
        total = 0
        for side, y, n in each_block(place, weight, wait=False):
            w = weight.buffer[side, y, z : z + step].reshape(-1, cols)
            total += dot_t(d_third[:, lanes(n, cols)], w)
        at = pl.ds(z * 2 * rows, step * 2 * rows)
        low = (slope[:, at].astype(FULL) * total).astype(LOW)
        d_hidden[:, at] = low
        grads[:, at] = column_sum(low)
    give(place, send, d_hidden)


def feed_in_back(
    place, w_in, w_out, d_hidden, d_third, second_sum, vec, d_sum, d_low, d_mix, grads, send
):
    upstream = d_third[...] + through(place, d_hidden, w_in)
    back, d_gain, d_shift = norm_back(upstream, second_sum[...], vec[GAIN + 1 : GAIN + 2])
    d_sum[...] = back
    low = back.astype(LOW)
    d_low[...] = low
    grads[0:1, :] = column_sum(low)
    grads[1:2, :] = d_shift
    grads[2:3, :] = d_gain
    d_mix[...] = through(place, d_low, w_out).astype(LOW)
    give(place, send, d_low)


def cross_backward(place, query, kv, probs, d_mix, mix, d_query, d_kv, grads):
    rows, half = query.shape
    for h in range(half // PAIR):
        at, beside = pl.ds(h * PAIR, PAIR), pl.ds(half + h * PAIR, PAIR)
        dq, dk, dv = attend_back_rows(
            query[:, at],
            kv[0, :, at],
            kv[0, :, beside],
            probs[0, 0, pl.ds(h * 2 * rows, 2 * rows), :],
            d_mix[:, at],
            mix[:, at],
        )
        d_query[:, at] = dq.astype(LOW)
        d_kv[:, at] = dk.astype(LOW)
        low = dv.astype(LOW)
        d_kv[:, beside] = low
        before = jnp.where(pl.program_id(0) == 0, 0.0, grads[:, at])
        grads[:, at] = before + column_sum(low)


def self_backward(
    place, w_query, w_out, d_query, d_sum2, first_sum, vec, joined, probs, mix,
    d_sum, d_low, d_joined, grads, send,
):
    width = d_sum.shape[-1]
    upstream = d_sum2[...] + through(place, d_query, w_query)
    back, d_gain, d_shift = norm_back(upstream, first_sum[...], vec[GAIN : GAIN + 1])
    d_sum[...] = back
    low = back.astype(LOW)
    d_low[...] = low
    d_mix = through(place, d_low, w_out).astype(LOW)
    rows = probs.shape[-1] // 2
    heads = width // PAIR
    for p in range(d_sum.shape[0] // rows):
        at = pl.ds(p * rows, rows)
        ups = d_mix[p * rows : (p + 1) * rows]
        dots = row_dots(mix[at, :], ups)
        for h in range(heads):
            where = [pl.ds(i * width + h * PAIR, PAIR) for i in range(3)]
            q, k, v = (joined[at, w] for w in where)
            found = attend_back_sides(
                q,
                k,
                v,
                probs[pl.ds((p * heads + h) * rows, rows), :],
                ups[:, h * PAIR : (h + 1) * PAIR],
                dots[h],
            )
            for w, value in zip(where, found):
                d_joined[at, w] = value.astype(LOW)
    grads[0:1, :] = column_sum(d_joined[:, :width])
    grads[1:2, :] = column_sum(d_joined[:, 2 * width :])
    grads[2:3, :] = column_sum(low)
    grads[3:4, :] = column_sum(d_query[...])
    grads[4:5, :] = d_shift
    grads[5:6, :] = d_gain
    give(place, send, d_joined)
    give(place, send, d_low, 3 * width // 4)
    give(place, send, d_query, width)


def input_back(place, weight, d_joined, d_sum, out):
    out[...] = d_sum[...] + through(place, d_joined, weight)


def table_back(place, weight, d_mine, d_other, out):
    @pl.when(pl.program_id(0) == 0)
    def _():
        weight.wait(0)
        weight.wait(1)

    half = d_mine.shape[-1] // 2
    total = 0
    for side, d in enumerate((d_mine, d_other)):
        for y in range(2):
            total += dot_t(d[:, y * half : (y + 1) * half], weight.part(side, y))
    out[...] = total


def quarter_place(step, place):
    c = place[2]
    dy = jnp.where(step == 0, 1, jnp.where(step == 1, 1 - c, jnp.where(step == 2, c, 0)))
    dx = jnp.where(step == 0, 1, jnp.where(step == 1, c, jnp.where(step == 2, 1 - c, 0)))
    return place[0] ^ dy, place[1] ^ dx


def quarter_grads(net, name, products, more):
    lines = net.lines
    ins = []
    for left, left2, right, right2, size, first in products:
        for a in (left, left2):
            view = a.reshape(lines, 2, -1, a.shape[-1])
            block = (lines, 1) + view.shape[2:]
            ins.append((view, block, lambda s, at: (0, quarter_place(s, at)[1], 0, 0)))
        if first is None:
            for a in (right, right2):
                ins.append(
                    (a, (a.shape[0], size), lambda s, at: (0, quarter_place(s, at)[0]))
                )
        else:
            ins.append(
                (
                    right,
                    (right.shape[0], size),
                    lambda s, at: (0, 2 * quarter_place(s, at)[0] + at[2]),
                )
            )
            ins.append(
                (
                    right2,
                    (1, right2.shape[1], size),
                    lambda s, at, first=first: (quarter_place(s, at)[0], 0, first),
                )
            )
    rows = products[0][0].shape[0] // net.wide
    cols = sum(p[4] for p in products)
    extra = more[0].shape[3] if more else 0
    for a in more or ():

        def corner(s, at):
            y, x = quarter_place(s, at)
            return (y, 0, x, 0, 0)

        ins.append((a, (1, lines, 1, extra, cols), corner))

    def body(place, *refs):
        outs = refs[len(ins) :]
        quarters = []
        start = 0
        for i, (_, _, _, _, size, first) in enumerate(products):
            left, left2, right, right2 = refs[4 * i : 4 * i + 4]
            l, l2 = (a[:, 0].reshape(lines * rows, -1) for a in (left, left2))
            r2 = right2[...] if first is None else right2[0]
            value = dot(l, right[...]) + dot(l2, r2)
            quarters.append((start, size, value.astype(LOW).reshape(lines, rows, size)))
            start += size

        def put(out):
            for z in range(lines):
                differs = place[3] ^ z
                to = sum(
                    ((differs >> bit) & 1) * (lines >> (bit + 1))
                    for bit in range(lines.bit_length() - 1)
                )
                for start, size, value in quarters:
                    out[to, :rows, start : start + size] = value[z]
                if extra:
                    a, b = refs[4 * len(products) : len(ins)]
                    value = a[0, z, 0].astype(FULL) + b[0, z, 0].astype(FULL)
                    out[to, rows:, :] = value.astype(LOW)

        step = pl.program_id(0)
        pl.when(step < 2)(lambda: put(outs[0].at[0]))
        pl.when(step == 2)(lambda: put(outs[1]))
        pl.when(step == 3)(lambda: put(outs[2]))

    shape = (lines, rows + extra, cols)
    return call(
        body,
        name,
        net,
        (4,),
        ins,
        [
            ((2,) + shape, LOW, (1,) + shape, lambda s, at: (jnp.minimum(s, 1), 0, 0, 0)),
            whole_out(shape, LOW),
            whole_out(shape, LOW),
        ],
    )


def segment_index(lengths, count):
    segment_ends = jnp.cumsum(lengths, axis=-1)
    position = jnp.arange(count, dtype=jnp.int32)
    passed = (position[None, :, None] >= segment_ends[:, None, :]).astype(jnp.int32)
    return jnp.sum(passed, axis=-1)


def per_device(
    inputs,
    memory,
    cotangent,
    dec_lengths,
    mem_lengths,
    seg_table,
    self_qkv,
    self_out,
    cross_q,
    cross_kv,
    cross_out,
    fc_in,
    fc_out,
    vec_bias,
    norm_gain,
    fc_in_bias,
    *,
    wide,
    narrow,
):
    net = Net(wide, narrow)
    Order.last = Order.soon = Order.later = ()
    pairs, length, width = inputs.shape
    held = memory.shape[1]
    x = inputs.reshape(-1, width)
    table = memory.reshape(-1, width)
    upstream = cotangent.reshape(-1, width)
    count, quarter, half = x.shape[0], width // narrow, width // 2
    hidden = fc_out.shape[0] * wide

    rows = jnp.concatenate([vec_bias, norm_gain])
    small = jnp.concatenate([rows.reshape(-1), fc_in_bias])
    extra = 16
    small_rows = jnp.zeros((extra, self_qkv.shape[1]), LOW).at[0, : small.size].set(small)
    table2 = net.over_core(table)
    g2 = Weight(net, jnp.concatenate([self_qkv, small_rows])).at_once()
    g2.rows = self_qkv.shape[0]
    shards = jnp.concatenate([cross_kv, cross_out, self_out, cross_q], axis=1)
    g3, g4, g5 = Weight(net, shards), Weight(net, fc_in), PairedWeight(net, fc_out).begin()
    g2.start(g5.mate)
    g3.line(g2.held, g5.mate)
    Order.need(table2, *g2.copy("held", after=g5.mate))
    g3.line_on()
    g4.line()
    g2.turn()
    Order.need(*g2.copy("one", "two"))
    if net.lines == 4:
        Order.need(g4.got)
    g3.line_end()
    g3.start()
    g4.line_on()
    g5.pair().line()
    g2.copy("three")

    segments = segment_index(dec_lengths, length)
    tables = segment_index(mem_lengths, held)
    matches = segments[:, :, None] == jnp.arange(dec_lengths.shape[-1], dtype=jnp.int32)
    query_table = jnp.sum(jnp.where(matches, seg_table[:, None, :], 0), axis=-1)
    seg_col, seg_row = segments.reshape(-1, 1), segments.reshape(pairs, 1, length)
    table_col, table_row = query_table.reshape(-1, 1), tables.reshape(pairs, 1, held)

    def in_place(pieces):
        sides = []
        for side, (same, one, two, three) in enumerate((pieces[:4], pieces[4:])):
            first = (net.c ^ side) == 0
            by_x = jnp.where(first, one, two)
            by_y = jnp.where(first, two, one)
            sides.append(jnp.stack([jnp.stack([same, by_x]), jnp.stack([by_y, three])]))
        out = jnp.stack(net.swap(*sides))
        out = jnp.where(net.y == 0, out, out[:, ::-1])
        out = jnp.where(net.x == 0, out, out[:, :, ::-1])
        return jnp.transpose(out, (3, 2, 1, 0, 4)).reshape(wide, narrow, -1)

    vectors = in_place([p[:, self_qkv.shape[0], : small.size] for p in g2.arrays()]).astype(FULL)
    fc_bias = vectors[:, :, rows.size :].reshape(1, -1)
    vec = vectors[:, :, : rows.size].reshape(wide * narrow, rows.shape[0], -1)
    vec = jnp.transpose(vec, (1, 0, 2)).reshape(rows.shape[0], width)
    joined_bias = jnp.concatenate([vec[0], jnp.zeros((width,), FULL), vec[1]])[None]

    heads = width // PAIR
    joined, self_probs, self_mix, x_t, self_mix_t = call(
        self_forward,
        "self_forward",
        net,
        (1,),
        [whole(x), whole(joined_bias), whole(seg_col), whole(seg_row)],
        [
            whole_out((count, 3 * width), LOW),
            whole_out((pairs * heads * length, 2 * length), LOW),
            whole_out((count, width), LOW),
            whole_out((width, count), LOW),
            whole_out((width, count), LOW),
        ],
        weights=[(g2, 0, 3 * quarter)],
    )
    g4.line_end()
    g5.line_on()
    g3.turn()
    copies = g3.copy("held", "one", "two")
    g4.start(*copies)
    g3.copy("three")
    first_sum, first_low_t, query = call(
        first_half,
        "first_half",
        net,
        (1,),
        [whole(self_mix), whole(x), whole(vec)],
        [
            whole_out((count, width), FULL),
            whole_out((width, count), LOW),
            whole_out((count, width), LOW),
        ],
        [pltpu.VMEM((count, width), FULL)],
        weights=[(g3, 3 * quarter, quarter), (g3, 4 * quarter, quarter)],
    )
    tile = 512
    kv, table_t, table_t2 = call(
        table_keys,
        "table_keys",
        net,
        (table.shape[0] // tile,),
        [
            (table, (tile, width), lambda t, at: (t, 0)),
            (table2, (tile, width), lambda t, at: (t, 0)),
            whole(vec),
        ],
        [
            ((2, table.shape[0], width), LOW, (2, tile, width), lambda t, at: (0, t, 0)),
            ((width, table.shape[0]), LOW, (width, tile), lambda t, at: (0, t)),
            ((width, table.shape[0]), LOW, (width, tile), lambda t, at: (0, t)),
        ],
        weights=[(g3, 0, half)],
    )
    g4.turn()
    g4.copy("held", "one")
    g5.line_end()
    g5.turn()
    g5.copy("held")
    score_rows = half // PAIR * 2 * length
    core_block = ((length, half), lambda s, p, at: (p, at[2] ^ s))
    cross_mix, cross_probs, cross_mix_t = call(
        cross_forward,
        "cross_forward",
        net,
        (2, pairs),
        [
            (query, *core_block),
            (kv, (1, held, width), lambda s, p, at: (s, p, 0)),
            (table_col, (length, 1), lambda s, p, at: (p, 0)),
            (table_row, (1, 1, held), lambda s, p, at: (p, 0, 0)),
        ],
        [
            ((count, width), LOW, *core_block),
            (
                (2, pairs, score_rows, held),
                LOW,
                (1, 1, score_rows, held),
                lambda s, p, at: (s, p, 0, 0),
            ),
            ((width, count), LOW, (half, length), lambda s, p, at: (at[2] ^ s, p)),
        ],
    )
    g4.copy("two", "three")
    second_sum, second_low, second_low_t = call(
        second_half,
        "second_half",
        net,
        (1,),
        [whole(cross_mix), whole(first_sum), whole(vec)],
        [
            whole_out((count, width), FULL),
            whole_out((count, width), LOW),
            whole_out((width, count), LOW),
        ],
        [pltpu.VMEM((count, width), FULL)],
        weights=[(g3, half, quarter)],
    )
    active, slope, active_t = call(
        feed_in,
        "feed_in",
        net,
        (1,),
        [whole(second_low), whole(fc_bias)],
        [
            whole_out((count, hidden), LOW),
            whole_out((count, hidden), LOW),
            whole_out((hidden, count), LOW),
        ],
        weights=[(g4, 0, hidden // 4)],
    )
    g5.copy("far")
    active_t2, second_low_t2 = (net.over_core(a, g5.far) for a in (active_t, second_low_t))
    output, d_third, d_low3, grads3, send3 = call(
        feed_out,
        "feed_out",
        net,
        (1,),
        [whole(active), whole(second_sum), whole(upstream), whole(vec)],
        [
            whole_out((count, width), LOW),
            whole_out((count, width), FULL),
            whole_out((count, width), LOW),
            whole_out((8, width), FULL),
            whole_out((2, count, quarter), LOW),
        ],
        [pltpu.VMEM((count, width), FULL)],
        weights=[(g5, 0, quarter)],
    )

    got3 = net.over_core(send3)
    first_low_t2, self_mix_t2, cross_mix_t2, x_t2 = Order.pin(
        *(net.over_core(a) for a in (first_low_t, self_mix_t, cross_mix_t, x_t))
    )
    r_out = Reduction(net, "grad_out", [(active_t, active_t2, d_low3, got3, quarter, 0)]).start()
    d_hidden, g_fc_bias, send_hidden = call(
        feed_out_back,
        "feed_out_back",
        net,
        (1,),
        [whole(d_low3), whole(slope)],
        [
            whole_out((count, hidden), LOW),
            whole_out((1, hidden), FULL),
            whole_out((2, count, hidden // 4), LOW),
        ],
        weights=[(g5, 0, quarter)],
    )
    got_hidden = net.over_core(send_hidden)
    r_in = Reduction(
        net, "grad_in", [(second_low_t, second_low_t2, d_hidden, got_hidden, hidden // 4, 0)]
    ).start()
    d_sum2, d_low2, d_mix, grads2, send2 = call(
        feed_in_back,
        "feed_in_back",
        net,
        (1,),
        [whole(d_hidden), whole(d_third), whole(second_sum), whole(vec)],
        [
            whole_out((count, width), FULL),
            whole_out((count, width), LOW),
            whole_out((count, width), LOW),
            whole_out((8, width), FULL),
            whole_out((2, count, quarter), LOW),
        ],
        weights=[(g4, 0, hidden // 4), (g3, half, quarter)],
    )
    r_out.turn()
    def tables_back(side, into=()):
        block = ((length, half), lambda p, at: (p, at[2] ^ side))
        return call(
            cross_backward,
            "cross_backward",
            net,
            (pairs,),
            [
                (query, *block),
                (kv, (1, held, width), lambda p, at: (side, p, 0)),
                (cross_probs, (1, 1, score_rows, held), lambda p, at: (side, p, 0, 0)),
                (d_mix, *block),
                (cross_mix, *block),
            ],
            [
                ((count, width), LOW, *block),
                (table.shape, LOW, (held, width), lambda p, at: (p, 0)),
                whole_out((1, half), FULL),
            ],
            into=into,
        )

    d_query, d_other, grads_other = tables_back(1)
    d_query, d_mine, grads_mine = tables_back(0, (d_query,))
    d_sum1, d_low1, d_joined, grads1, send1 = call(
        self_backward,
        "self_backward",
        net,
        (1,),
        [
            whole(d_query),
            whole(d_sum2),
            whole(first_sum),
            whole(vec),
            whole(joined),
            whole(self_probs),
            whole(self_mix),
        ],
        [
            whole_out((count, width), FULL),
            whole_out((count, width), LOW),
            whole_out((count, 3 * width), LOW),
            whole_out((8, width), FULL),
            whole_out((2, count, 5 * quarter), LOW),
        ],
        weights=[(g3, 4 * quarter, quarter), (g3, 3 * quarter, quarter)],
    )
    waits = (r_out.near, r_in.pair)
    got1, got_table = net.over_core(send1, *waits), net.over_core(d_other, *waits)
    r_out.line()
    r_in.turn()
    r_self = Reduction(
        net,
        "grad_self",
        [
            (x_t, x_t2, d_joined, got1, 3 * quarter, 0),
            (self_mix_t, self_mix_t2, d_low1, got1, quarter, 3),
            (first_low_t, first_low_t2, d_query, got1, quarter, 4),
        ],
    ).start(r_in.near, r_out.step, got_table)
    grads_v = jnp.concatenate(net.swap(grads_mine, grads_other), axis=1)
    g_rows = jnp.concatenate(
        [
            grads1[:4],
            grads_v,
            grads2[:1],
            grads3[:1],
            grads1[4:5],
            grads2[1:2],
            grads3[1:2],
            grads1[5:6],
            grads2[2:3],
            grads3[2:3],
        ]
    )
    g_rows = jnp.transpose(g_rows.reshape(rows.shape[0], wide, narrow, -1), (2, 1, 0, 3))
    g_small = jnp.transpose(g_fc_bias.reshape(wide, narrow, -1), (1, 0, 2))
    g_small = jnp.concatenate([g_rows.reshape(narrow, wide, -1), g_small], axis=2).astype(LOW)
    room = extra * 3 * quarter - small.size
    g_small = jnp.pad(g_small, ((0, 0), (0, 0), (0, room)))
    g_small = g_small.reshape(2, 2, wide // 2, 2, extra, -1)
    small_mine, small_other = net.swap(g_small[:, 0], g_small[:, 1])
    small_got, got2 = net.over_core(small_other), net.over_core(send2)
    r_out.line_on()
    r_in.line()
    r_cross = Reduction(
        net,
        "grad_cross",
        [
            (table_t, table_t2, d_mine, got_table, half, None),
            (cross_mix_t, cross_mix_t2, d_low2, got2, quarter, 0),
        ],
        (small_mine, small_got),
    ).start()
    r_out.line_end()
    r_in.line_on()
    (input_grad,) = call(
        input_back,
        "input_back",
        net,
        (1,),
        [whole(d_joined), whole(d_sum1)],
        [whole_out((count, width), FULL)],
        weights=[(g2, 0, 3 * quarter)],
    )
    r_in.line_end()
    r_self.turn(r_in.total, r_out.total)
    tile = 512
    (memory_grad,) = call(
        table_back,
        "table_back",
        net,
        (table.shape[0] // tile,),
        [(d, (tile, width), lambda t, at: (t, 0)) for d in (d_mine, d_other)],
        [(table.shape, FULL, (tile, width), lambda t, at: (t, 0))],
        weights=[(g3, 0, half)],
    )
    r_cross.turn(r_self.near)
    r_self.line(r_cross.ready)
    r_self.line_on()
    r_cross.line()
    r_self.line_end()
    r_cross.line_on().line_end()

    g_out, g_in, g_cross, g_self = (r.total for r in (r_out, r_in, r_cross, r_self))
    g_small = g_cross[-extra:].reshape(-1)[: small.size]
    g_rows, g_fc_bias = g_small[: rows.size].reshape(rows.shape), g_small[rows.size :]
    return (
        output.reshape(inputs.shape),
        input_grad.reshape(inputs.shape),
        memory_grad.reshape(memory.shape),
        g_self[:, : 3 * quarter],
        g_self[:, 3 * quarter : 4 * quarter],
        g_self[:, 4 * quarter :],
        g_cross[:-extra, : 2 * quarter],
        g_cross[:-extra, 2 * quarter :],
        g_in,
        g_out,
        g_rows[:10],
        g_rows[10:],
        g_fc_bias,
    )


def solution(mesh):
    tokens = P(BOTH, None, None)
    lengths = P(BOTH, None)
    weight = P("wide", "narrow")
    vector = P(None, BOTH)
    return jax.shard_map(
        partial(per_device, wide=mesh.shape["wide"], narrow=mesh.shape["narrow"]),
        mesh=mesh,
        in_specs=(tokens,) * 3 + (lengths,) * 3 + (weight,) * 7 + (vector, vector, P(BOTH)),
        out_specs=(tokens,) * 3 + (weight,) * 7 + (vector, vector, P(BOTH)),
        check_vma=False,
    )
```

```python
import math
from functools import partial

import jax
import jax.numpy as jnp
from jax import lax
from jax.experimental import pallas as pl
from jax.experimental.pallas import tpu as pltpu
from jax.sharding import PartitionSpec as P

HD = 64
PAIR = 2 * HD
BOTH = ("wide", "narrow")
EPS = 1e-05
MASKED_SCORE = -1000000000.0
LOW = jnp.bfloat16
FULL = jnp.float32
VMEM_BYTES = 52 * 1024 * 1024
B_QUERY, B_VALUE, B_SELF_OUT, B_CROSS_Q, B_CROSS_V, B_CROSS_OUT, B_FC_OUT = range(7)
SHIFT, GAIN = 7, 10


def after(value, *others):
    return lax.optimization_barrier((value, others))[0]


class Order:
    last, soon, later = (), (), ()

    @classmethod
    def put(cls, kernel, arrays):
        first = after(arrays[0], *cls.last, *cls.soon)
        out = kernel(first, *arrays[1:])
        cls.last, cls.soon, cls.later = (out[0],), cls.later, ()
        return out

    @classmethod
    def now(cls, value, *others):
        return after(value, *cls.last, *others)

    @classmethod
    def need(cls, *arrays):
        cls.soon += arrays

    @classmethod
    def pin(cls, *arrays):
        cls.later += arrays
        return arrays


class Net:
    def __init__(self, wide, narrow):
        self.wide, self.narrow, self.lines = wide, narrow, wide // 2
        w, n = lax.axis_index("wide"), lax.axis_index("narrow")
        self.z, self.x, self.y, self.c = w // 2, w % 2, n // 2, n % 2
        self.place = jnp.stack([self.y, self.x, self.c, self.z]).astype(jnp.int32)
        both = [(i, j) for i in range(wide) for j in range(narrow)]

        def flat(i, j):
            return i * narrow + j

        def pairs(x_core):
            return [
                (flat(i, j), flat(i ^ 1, j) if j % 2 == x_core else flat(i, j ^ 2)) for i, j in both
            ]

        self.first, self.second = pairs(0), pairs(1)
        self.core = [(j, j ^ 1) for j in range(narrow)]
        self.groups = [[z * 2 + x for z in range(self.lines)] for x in range(2)]

    def across(self, value, way, *others):
        return lax.ppermute(Order.now(value, *others), BOTH, way)

    def over_core(self, value, *others):
        return lax.ppermute(Order.now(value, *others), "narrow", self.core)

    def along(self, value, step, *others):
        way = [(w, ((w // 2) ^ step) * 2 + w % 2) for w in range(self.wide)]
        return lax.ppermute(Order.now(value, *others), "wide", way)

    def swap(self, a, b):
        first = self.c == 0
        return jnp.where(first, a, b), jnp.where(first, b, a)


class Weight:
    def __init__(self, net, shard, before=()):
        self.net = net
        self.rows = shard.shape[0]
        self.shard = after(shard, *before)

    def at_once(self):
        self.held = lax.all_gather(
            self.shard, "wide", axis=0, axis_index_groups=self.net.groups
        )
        return self

    def line(self, *others):
        net = self.net
        if net.lines == 4:
            self.got = net.along(self.shard, 2, *others)
        return self

    def line_on(self):
        net = self.net
        if net.lines == 4:
            self.held = stack(net, [self.shard, self.got], 1)
            self.got = net.along(self.held, 1)
        return self

    def line_end(self):
        net = self.net
        if net.lines == 4:
            self.held = stack(net, [self.held, self.got], 0)
        else:
            self.at_once()
        return self

    def start(self, *others):
        net = self.net
        self.one = net.across(self.held, net.first, *others)
        self.two = net.across(self.held, net.second, *others)
        return self

    def turn(self, *others):
        net = self.net
        self.three = net.across(self.one, net.second, self.two, *others)
        return self

    def copy(self, *names, after=None):
        others = () if after is None else (after,)
        new = [self.net.over_core(getattr(self, name), *others) for name in names]
        self.copies = [*getattr(self, "copies", ()), *new]
        return new

    def arrays(self):
        return [self.held, self.one, self.two, self.three, *self.copies]

    def spots(self):
        return [(i, 0) for i in range(8)]


class PairedWeight(Weight):
    def begin(self, *others):
        self.mate = self.net.across(self.shard, self.net.first, *others)
        return self

    def pair(self):
        self.single = self.rows
        self.shard = jnp.concatenate([self.shard, self.mate])
        return self

    def turn(self, *others):
        self.far = self.net.across(self.held, self.net.second, *others)
        return self

    def arrays(self):
        return [self.held, self.far, *self.copies]

    def spots(self):
        return [(2 * side + k // 2, k % 2 * self.rows) for side in range(2) for k in range(4)]


def piece_place(place, index):
    side, k = divmod(index, 4)
    c = place[2] ^ side
    dy, dx = ((0, 0), (c, 1 - c), (1 - c, c), (1, 1))[k]
    return place[0] ^ dy, place[1] ^ dx, side


class Loaded:
    def __init__(self, place, arrays, spots, buffer, sems, rows, col):
        self.buffer = buffer
        size = buffer.shape[-1]
        self.copies = []
        for i, (array, first) in enumerate(spots):
            y, x, side = piece_place(place, i)
            self.copies.append(
                pltpu.make_async_copy(
                    arrays[array].at[:, pl.ds(first, rows), pl.ds(col, size)],
                    buffer.at[side, y, :, x],
                    sems.at[i],
                )
            )

    def start(self):
        for copy in self.copies:
            copy.start()

    def wait(self, side):
        for copy in self.copies[4 * side : 4 * side + 4]:
            copy.wait()

    def part(self, side, y):
        return self.buffer[side, y].reshape(-1, self.buffer.shape[-1])


class Reduction:
    def __init__(self, net, name, products, more=None):
        self.net = net
        self.pair, self.near, self.own = quarter_grads(net, name, products, more)

    def start(self, *others):
        self.pair = self.net.across(self.pair, self.net.second, *others)
        return self

    def turn(self, *others):
        pair = Order.now(self.pair, *others)
        self.ready = (self.near.astype(FULL) + pair[0].astype(FULL)).astype(LOW)
        Order.need(self.ready)
        self.near = self.net.across(self.ready, self.net.first)
        return self

    def line(self, *others):
        net = self.net
        near = Order.now(self.near, *others)
        total = self.own.astype(FULL) + self.pair[1].astype(FULL) + near.astype(FULL)
        self.total = total.astype(LOW)
        Order.need(self.total)
        self.step = net.along(self.total[total.shape[0] // 2 :], 1)
        return self

    def line_on(self):
        net = self.net
        half, step = self.total.shape[0] // 2, 2
        total = self.total[:half].astype(FULL) + Order.now(self.step).astype(FULL)
        while half > 2:
            half //= 2
            low = total.astype(LOW)
            got = net.along(low[half:], step)
            total = low[:half].astype(FULL) + got.astype(FULL)
            step *= 2
        self.total = total.astype(LOW)
        Order.need(self.total)
        if half > 1:
            self.step = net.along(self.total[1:], step)
        return self

    def line_end(self):
        total = self.total[0].astype(FULL)
        if self.total.shape[0] > 1:
            total += Order.now(self.step)[0].astype(FULL)
        self.total = total
        return self


def call(body, name, net, grid, ins, outs, scratch=(), weights=(), into=()):
    operands, buffers, first = [], [], []
    for weight, _, size in weights:
        first.append(len(operands))
        operands += weight.arrays()
        shape = (2, 2, net.lines, 2, weight.rows, size)
        buffers += [pltpu.VMEM(shape, LOW), pltpu.SemaphoreType.DMA((8,))]
    plain = len(ins) + len(outs)
    fixed = len(operands)
    operands += into
    specs = [pl.BlockSpec(memory_space=pl.ANY)] * len(operands)

    def run(place, *refs):
        pieces, rest = refs[:fixed], refs[len(operands) :]
        held = rest[plain : plain + len(buffers)]
        rest = rest[:plain] + rest[plain + len(buffers) :]
        loaded = [
            Loaded(
                place,
                pieces[first[i] :],
                weight.spots(),
                held[2 * i],
                held[2 * i + 1],
                weight.rows,
                col,
            )
            for i, (weight, col, _) in enumerate(weights)
        ]

        def start():
            for weight in loaded:
                weight.start()

        if grid == (1,):
            start()
        elif loaded:
            pl.when(pl.program_id(0) == 0)(start)
        body(place, *loaded, *rest)

    kernel = pl.pallas_call(
        run,
        grid_spec=pltpu.PrefetchScalarGridSpec(
            num_scalar_prefetch=1,
            grid=grid,
            in_specs=specs + [pl.BlockSpec(b, m) for _, b, m in ins],
            out_specs=[pl.BlockSpec(b, m) for _, _, b, m in outs],
            scratch_shapes=[*buffers, *scratch],
        ),
        out_shape=[jax.ShapeDtypeStruct(s, d) for s, d, _, _ in outs],
        compiler_params=pltpu.CompilerParams(
            dimension_semantics=("arbitrary",) * len(grid), vmem_limit_bytes=VMEM_BYTES
        ),
        cost_estimate=pl.CostEstimate(flops=1000, bytes_accessed=1000, transcendentals=0),
        input_output_aliases={1 + fixed + i: i for i in range(len(into))},
        name=name,
    )
    return Order.put(partial(kernel, net.place), [*operands, *(a for a, _, _ in ins)])


def stack(net, pieces, bit):
    rows, cols = pieces[0].shape[-2:]

    def body(place, *refs):
        for i in range(2):

            @pl.when(pl.program_id(0) == i)
            def _(i=i):
                refs[-1][:, 0] = refs[i][...].reshape(-1, rows, cols)

    lead = pieces[0].size // (rows * cols)
    shape = (lead, 2, rows, cols)
    (out,) = call(
        body,
        "stack",
        net,
        (2,),
        [whole(p) for p in pieces],
        [(shape, LOW, (lead, 1, rows, cols), lambda s, at: (0, ((at[3] >> bit) & 1) ^ s, 0, 0))],
    )
    return out.reshape(2 * lead, rows, cols)


def whole(array):
    return (array, array.shape, lambda *_: (0,) * array.ndim)


def whole_out(shape, dtype):
    return (shape, dtype, shape, lambda *_: (0,) * len(shape))


def lanes(index, size):
    return pl.ds(pl.multiple_of(index * size, 128), size)


def block_of(place, side, y):
    return 2 * y + (place[2] ^ side)


def each_block(place, weight, wait=True):
    for side in range(2):
        if wait:
            weight.wait(side)
        for y in range(2):
            yield side, y, block_of(place, side, y)


def dot(a, b):
    return jnp.dot(a, b, preferred_element_type=FULL)


def dot_t(a, b):
    return lax.dot_general(a, b, (((1,), (1,)), ((), ())), preferred_element_type=FULL)


def t_dot(a, b):
    return lax.dot_general(a, b, (((0,), (0,)), ((), ())), preferred_element_type=FULL)


def norm_parts(z):
    centred = z - jnp.mean(z, axis=-1, keepdims=True)
    scale = lax.rsqrt(jnp.mean(centred * centred, axis=-1, keepdims=True) + EPS)
    return centred * scale, scale


def norm(z, vec, which):
    unit, _ = norm_parts(z)
    return unit * vec[GAIN + which : GAIN + which + 1] + vec[SHIFT + which : SHIFT + which + 1]


def norm_back(upstream, z, gain):
    unit, scale = norm_parts(z)
    d_gain = jnp.sum(upstream * unit, axis=0, keepdims=True)
    d_shift = jnp.sum(upstream, axis=0, keepdims=True)
    inner = upstream * gain
    mean = jnp.mean(inner, axis=-1, keepdims=True)
    along = jnp.mean(inner * unit, axis=-1, keepdims=True)
    return scale * (inner - mean - unit * along), d_gain, d_shift


def column_sum(values):
    return jnp.sum(values.astype(FULL), axis=0, keepdims=True)


def two_heads(rows):
    low = lax.broadcasted_iota(jnp.int32, rows.shape, 1) < HD
    none = jnp.zeros_like(rows)
    return jnp.concatenate([jnp.where(low, rows, none), jnp.where(low, none, rows)], axis=0)


def one_row(stacked):
    half = stacked.shape[0] // 2
    low = lax.broadcasted_iota(jnp.int32, (half, PAIR), 1) < HD
    return jnp.where(low, stacked[:half], stacked[half:])


def one_side(stacked):
    half = stacked.shape[1] // 2
    low = lax.broadcasted_iota(jnp.int32, (PAIR, half), 0) < HD
    return jnp.where(low, stacked[:, :half], stacked[:, half:])


def softmax_sides(query, keys, allowed):
    logits = jnp.where(allowed, dot_t(keys, two_heads(query)) * HD ** (-0.5), MASKED_SCORE)
    weight = jnp.exp(logits - jnp.max(logits, axis=0, keepdims=True))
    return (weight * (1.0 / jnp.sum(weight, axis=0, keepdims=True))).astype(LOW)


def softmax_rows(query, keys, allowed):
    logits = jnp.where(allowed, dot_t(two_heads(query), keys) * HD ** (-0.5), MASKED_SCORE)
    weight = jnp.exp(logits - jnp.max(logits, axis=-1, keepdims=True))
    return (weight * (1.0 / jnp.sum(weight, axis=-1, keepdims=True))).astype(LOW)


def attend_back_rows(query, keys, values, probs, upstream, mix):
    queries, ups = two_heads(query), two_heads(upstream)
    product = two_heads(upstream.astype(FULL) * mix.astype(FULL))
    row_dot = jnp.sum(product, axis=1, keepdims=True)
    d_scores = (probs.astype(FULL) * (dot_t(ups, values) - row_dot)).astype(LOW)
    scale = HD ** (-0.5)
    return one_row(dot(d_scores, keys)) * scale, t_dot(d_scores, queries) * scale, t_dot(probs, ups)


def row_dots(mix, upstream):
    product = (mix.astype(FULL) * upstream.astype(FULL)).T
    sums = [
        jnp.sum(product[i : i + HD], axis=0, keepdims=True) for i in range(0, product.shape[0], HD)
    ]
    return [jnp.concatenate(sums[i : i + 2], axis=1) for i in range(0, len(sums), 2)]


def attend_back_sides(query, keys, values, probs, upstream, row_dot):
    queries, ups = two_heads(query), two_heads(upstream)
    scale = HD ** (-0.5)
    d_scores = (probs.astype(FULL) * (dot_t(values, ups) - row_dot)).astype(LOW)
    d_query = one_side(t_dot(keys, d_scores)).T * scale
    return d_query, dot(d_scores, queries) * scale, dot(probs, ups)


def twice(mask, axis):
    wide = jnp.where(mask, 1, 0)
    return jnp.concatenate([wide, wide], axis=axis) == 1


def self_forward(
    place, weight, x, bias, seg_col, seg_row, joined, probs, mix, x_t, mix_t
):
    x_t[...] = x[...].T
    for side, y, n in each_block(place, weight):
        w = weight.part(side, y)
        at = lanes(n, w.shape[-1])
        joined[:, at] = (dot(x[...], w) + bias[:, at]).astype(LOW)
    width, rows = mix.shape[1], seg_row.shape[-1]
    above = lax.broadcasted_iota(jnp.int32, (rows, rows), 0) <= lax.broadcasted_iota(
        jnp.int32, (rows, rows), 1
    )
    for p in range(mix.shape[0] // rows):
        at = pl.ds(p * rows, rows)
        allowed = twice((seg_col[at, :] == seg_row[p]) & above, 1)
        for h in range(width // PAIR):
            q, k, v = (joined[at, pl.ds(i * width + h * PAIR, PAIR)] for i in range(3))
            low = softmax_sides(q, k, allowed)
            probs[pl.ds((p * (width // PAIR) + h) * rows, rows), :] = low
            mixed = one_side(t_dot(v, low)).astype(LOW)
            mix_t[pl.ds(h * PAIR, PAIR), at] = mixed
            mix[at, pl.ds(h * PAIR, PAIR)] = mixed.T


def first_half(place, w_out, w_query, mix, x, vec, first_sum, low_t, query, acc):
    for side, y, n in each_block(place, w_out):
        w = w_out.part(side, y)
        acc[:, lanes(n, w.shape[-1])] = dot(mix[...], w)
    z = x[...].astype(FULL) + (acc[...] + vec[B_SELF_OUT : B_SELF_OUT + 1, :])
    first_sum[...] = z
    low = norm(z, vec, 0).astype(LOW)
    low_t[...] = low.T
    for side, y, n in each_block(place, w_query):
        w = w_query.part(side, y)
        at = lanes(n, w.shape[-1])
        query[:, at] = (dot(low, w) + vec[B_CROSS_Q : B_CROSS_Q + 1, at]).astype(LOW)


def table_keys(place, weight, x, x2, vec, out, x_t, x_t2):
    half = out.shape[-1] // 2

    @pl.when(pl.program_id(0) == 0)
    def _():
        weight.wait(0)
        weight.wait(1)

    for side in range(2):
        bias = vec[B_CROSS_V : B_CROSS_V + 1, lanes(place[2] ^ side, half)]
        out[side, :, :half] = dot(x[...], weight.part(side, 0)).astype(LOW)
        out[side, :, half:] = (dot(x[...], weight.part(side, 1)) + bias).astype(LOW)
    x_t[...] = x[...].T
    x_t2[...] = x2[...].T


def cross_forward(place, query, kv, table_col, table_row, mix, probs, mix_t):
    rows, half = query.shape
    allowed = twice(table_col[...] == table_row[0], 0)
    for h in range(half // PAIR):
        at = pl.ds(h * PAIR, PAIR)
        low = softmax_rows(query[:, at], kv[0, :, at], allowed)
        probs[0, 0, pl.ds(h * 2 * rows, 2 * rows), :] = low
        mixed = one_row(dot(low, kv[0, :, pl.ds(half + h * PAIR, PAIR)])).astype(LOW)
        mix[:, at] = mixed
        mix_t[at, :] = mixed.T


def second_half(place, weight, mix, first_sum, vec, second_sum, second_low, low_t, acc):
    for side, y, n in each_block(place, weight):
        w = weight.part(side, y)
        acc[:, lanes(n, w.shape[-1])] = dot(mix[...], w)
    z = norm(first_sum[...], vec, 0) + (acc[...] + vec[B_CROSS_OUT : B_CROSS_OUT + 1, :])
    second_sum[...] = z
    low = norm(z, vec, 1).astype(LOW)
    second_low[...] = low
    low_t[...] = low.T


def feed_in(place, weight, x, bias, active, slope, active_t):
    for side, y, n in each_block(place, weight):
        w = weight.part(side, y)
        cols = w.shape[-1]
        at = lanes(n, cols)
        hidden = dot(x[...], w) + bias[:, at]
        share = 0.5 + 0.5 * lax.erf(hidden * 2 ** (-0.5))
        low = (hidden * share).astype(LOW)
        active[:, at] = low
        active_t[pl.ds(pl.multiple_of(n * cols, 128), cols), :] = low.T
        density = jnp.exp(hidden * hidden * (-0.5)) * (2 * math.pi) ** (-0.5)
        slope[:, at] = (share + hidden * density).astype(LOW)


def give(place, send, rows, first=0):
    cols = rows.shape[-1] // 4
    for y in range(2):
        send[y, :, first : first + cols] = rows[:, lanes(block_of(place, 1, y), cols)]


def feed_out(
    place, weight, active, second_sum, cotangent, vec, output, d_third, d_low, grads, send, acc
):
    for side, y, n in each_block(place, weight):
        w = weight.part(side, y)
        acc[:, lanes(n, w.shape[-1])] = dot(active[...], w)
    z = norm(second_sum[...], vec, 1) + (acc[...] + vec[B_FC_OUT : B_FC_OUT + 1, :])
    output[...] = norm(z, vec, 2).astype(LOW)
    back, d_gain, d_shift = norm_back(cotangent[...].astype(FULL), z, vec[GAIN + 2 : GAIN + 3])
    d_third[...] = back
    low = back.astype(LOW)
    d_low[...] = low
    grads[0:1, :] = column_sum(low)
    grads[1:2, :] = d_shift
    grads[2:3, :] = d_gain
    give(place, send, d_low)


def through(place, rows, weight):
    total = 0
    for side, y, n in each_block(place, weight):
        w = weight.part(side, y)
        total += dot_t(rows[:, lanes(n, w.shape[-1])], w)
    return total


def feed_out_back(place, weight, d_third, slope, d_hidden, grads, send):
    _, _, lines, _, rows, cols = weight.buffer.shape
    weight.wait(0)
    weight.wait(1)
    step = max(1, min(lines, 1024 // (2 * rows)))
    for z in range(0, lines, step):
        total = 0
        for side, y, n in each_block(place, weight, wait=False):
            w = weight.buffer[side, y, z : z + step].reshape(-1, cols)
            total += dot_t(d_third[:, lanes(n, cols)], w)
        at = pl.ds(z * 2 * rows, step * 2 * rows)
        low = (slope[:, at].astype(FULL) * total).astype(LOW)
        d_hidden[:, at] = low
        grads[:, at] = column_sum(low)
    give(place, send, d_hidden)


def feed_in_back(
    place, w_in, w_out, d_hidden, d_third, second_sum, vec, d_sum, d_low, d_mix, grads, send
):
    upstream = d_third[...] + through(place, d_hidden, w_in)
    back, d_gain, d_shift = norm_back(upstream, second_sum[...], vec[GAIN + 1 : GAIN + 2])
    d_sum[...] = back
    low = back.astype(LOW)
    d_low[...] = low
    grads[0:1, :] = column_sum(low)
    grads[1:2, :] = d_shift
    grads[2:3, :] = d_gain
    d_mix[...] = through(place, d_low, w_out).astype(LOW)
    give(place, send, d_low)


def cross_backward(place, query, kv, probs, d_mix, mix, d_query, d_kv, grads):
    rows, half = query.shape
    for h in range(half // PAIR):
        at, beside = pl.ds(h * PAIR, PAIR), pl.ds(half + h * PAIR, PAIR)
        dq, dk, dv = attend_back_rows(
            query[:, at],
            kv[0, :, at],
            kv[0, :, beside],
            probs[0, 0, pl.ds(h * 2 * rows, 2 * rows), :],
            d_mix[:, at],
            mix[:, at],
        )
        d_query[:, at] = dq.astype(LOW)
        d_kv[:, at] = dk.astype(LOW)
        low = dv.astype(LOW)
        d_kv[:, beside] = low
        before = jnp.where(pl.program_id(0) == 0, 0.0, grads[:, at])
        grads[:, at] = before + column_sum(low)


def self_backward(
    place, w_query, w_out, d_query, d_sum2, first_sum, vec, joined, probs, mix,
    d_sum, d_low, d_joined, grads, send,
):
    width = d_sum.shape[-1]
    upstream = d_sum2[...] + through(place, d_query, w_query)
    back, d_gain, d_shift = norm_back(upstream, first_sum[...], vec[GAIN : GAIN + 1])
    d_sum[...] = back
    low = back.astype(LOW)
    d_low[...] = low
    d_mix = through(place, d_low, w_out).astype(LOW)
    rows = probs.shape[-1] // 2
    heads = width // PAIR
    for p in range(d_sum.shape[0] // rows):
        at = pl.ds(p * rows, rows)
        ups = d_mix[p * rows : (p + 1) * rows]
        dots = row_dots(mix[at, :], ups)
        for h in range(heads):
            where = [pl.ds(i * width + h * PAIR, PAIR) for i in range(3)]
            q, k, v = (joined[at, w] for w in where)
            found = attend_back_sides(
                q,
                k,
                v,
                probs[pl.ds((p * heads + h) * rows, rows), :],
                ups[:, h * PAIR : (h + 1) * PAIR],
                dots[h],
            )
            for w, value in zip(where, found):
                d_joined[at, w] = value.astype(LOW)
    grads[0:1, :] = column_sum(d_joined[:, :width])
    grads[1:2, :] = column_sum(d_joined[:, 2 * width :])
    grads[2:3, :] = column_sum(low)
    grads[3:4, :] = column_sum(d_query[...])
    grads[4:5, :] = d_shift
    grads[5:6, :] = d_gain
    give(place, send, d_joined)
    give(place, send, d_low, 3 * width // 4)
    give(place, send, d_query, width)


def input_back(place, weight, d_joined, d_sum, out):
    out[...] = d_sum[...] + through(place, d_joined, weight)


def table_back(place, weight, d_mine, d_other, out):
    @pl.when(pl.program_id(0) == 0)
    def _():
        weight.wait(0)
        weight.wait(1)

    half = d_mine.shape[-1] // 2
    total = 0
    for side, d in enumerate((d_mine, d_other)):
        for y in range(2):
            total += dot_t(d[:, y * half : (y + 1) * half], weight.part(side, y))
    out[...] = total


def quarter_place(step, place):
    c = place[2]
    dy = jnp.where(step == 0, 1, jnp.where(step == 1, 1 - c, jnp.where(step == 2, c, 0)))
    dx = jnp.where(step == 0, 1, jnp.where(step == 1, c, jnp.where(step == 2, 1 - c, 0)))
    return place[0] ^ dy, place[1] ^ dx


def quarter_grads(net, name, products, more):
    lines = net.lines
    ins = []
    for left, left2, right, right2, size, first in products:
        for a in (left, left2):
            view = a.reshape(lines, 2, -1, a.shape[-1])
            block = (lines, 1) + view.shape[2:]
            ins.append((view, block, lambda s, at: (0, quarter_place(s, at)[1], 0, 0)))
        if first is None:
            for a in (right, right2):
                ins.append(
                    (a, (a.shape[0], size), lambda s, at: (0, quarter_place(s, at)[0]))
                )
        else:
            ins.append(
                (
                    right,
                    (right.shape[0], size),
                    lambda s, at: (0, 2 * quarter_place(s, at)[0] + at[2]),
                )
            )
            ins.append(
                (
                    right2,
                    (1, right2.shape[1], size),
                    lambda s, at, first=first: (quarter_place(s, at)[0], 0, first),
                )
            )
    rows = products[0][0].shape[0] // net.wide
    cols = sum(p[4] for p in products)
    extra = more[0].shape[3] if more else 0
    for a in more or ():

        def corner(s, at):
            y, x = quarter_place(s, at)
            return (y, 0, x, 0, 0)

        ins.append((a, (1, lines, 1, extra, cols), corner))

    def body(place, *refs):
        outs = refs[len(ins) :]
        quarters = []
        start = 0
        for i, (_, _, _, _, size, first) in enumerate(products):
            left, left2, right, right2 = refs[4 * i : 4 * i + 4]
            l, l2 = (a[:, 0].reshape(lines * rows, -1) for a in (left, left2))
            r2 = right2[...] if first is None else right2[0]
            value = dot(l, right[...]) + dot(l2, r2)
            quarters.append((start, size, value.astype(LOW).reshape(lines, rows, size)))
            start += size

        def put(out):
            for z in range(lines):
                differs = place[3] ^ z
                to = sum(
                    ((differs >> bit) & 1) * (lines >> (bit + 1))
                    for bit in range(lines.bit_length() - 1)
                )
                for start, size, value in quarters:
                    out[to, :rows, start : start + size] = value[z]
                if extra:
                    a, b = refs[4 * len(products) : len(ins)]
                    value = a[0, z, 0].astype(FULL) + b[0, z, 0].astype(FULL)
                    out[to, rows:, :] = value.astype(LOW)

        step = pl.program_id(0)
        pl.when(step < 2)(lambda: put(outs[0].at[0]))
        pl.when(step == 2)(lambda: put(outs[1]))
        pl.when(step == 3)(lambda: put(outs[2]))

    shape = (lines, rows + extra, cols)
    return call(
        body,
        name,
        net,
        (4,),
        ins,
        [
            ((2,) + shape, LOW, (1,) + shape, lambda s, at: (jnp.minimum(s, 1), 0, 0, 0)),
            whole_out(shape, LOW),
            whole_out(shape, LOW),
        ],
    )


def segment_index(lengths, count):
    segment_ends = jnp.cumsum(lengths, axis=-1)
    position = jnp.arange(count, dtype=jnp.int32)
    passed = (position[None, :, None] >= segment_ends[:, None, :]).astype(jnp.int32)
    return jnp.sum(passed, axis=-1)


def per_device(
    inputs,
    memory,
    cotangent,
    dec_lengths,
    mem_lengths,
    seg_table,
    self_qkv,
    self_out,
    cross_q,
    cross_kv,
    cross_out,
    fc_in,
    fc_out,
    vec_bias,
    norm_gain,
    fc_in_bias,
    *,
    wide,
    narrow,
):
    net = Net(wide, narrow)
    Order.last = Order.soon = Order.later = ()
    pairs, length, width = inputs.shape
    held = memory.shape[1]
    x = inputs.reshape(-1, width)
    table = memory.reshape(-1, width)
    upstream = cotangent.reshape(-1, width)
    count, quarter, half = x.shape[0], width // narrow, width // 2
    hidden = fc_out.shape[0] * wide

    rows = jnp.concatenate([vec_bias, norm_gain])
    small = jnp.concatenate([rows.reshape(-1), fc_in_bias])
    extra = 16
    small_rows = jnp.zeros((extra, self_qkv.shape[1]), LOW).at[0, : small.size].set(small)
    table2 = net.over_core(table)
    g2 = Weight(net, jnp.concatenate([self_qkv, small_rows])).at_once()
    g2.rows = self_qkv.shape[0]
    shards = jnp.concatenate([cross_kv, cross_out, self_out, cross_q], axis=1)
    g3, g4, g5 = Weight(net, shards), Weight(net, fc_in), PairedWeight(net, fc_out).begin()
    g2.start(g5.mate)
    g3.line(g2.held, g5.mate)
    Order.need(table2, *g2.copy("held", after=g5.mate))
    g3.line_on()
    g4.line()
    g2.turn()
    Order.need(*g2.copy("one", "two"))
    if net.lines == 4:
        Order.need(g4.got)
    g3.line_end()
    g3.start()
    g4.line_on()
    g5.pair().line()
    g2.copy("three")

    segments = segment_index(dec_lengths, length)
    tables = segment_index(mem_lengths, held)
    matches = segments[:, :, None] == jnp.arange(dec_lengths.shape[-1], dtype=jnp.int32)
    query_table = jnp.sum(jnp.where(matches, seg_table[:, None, :], 0), axis=-1)
    seg_col, seg_row = segments.reshape(-1, 1), segments.reshape(pairs, 1, length)
    table_col, table_row = query_table.reshape(-1, 1), tables.reshape(pairs, 1, held)

    def in_place(pieces):
        sides = []
        for side, (same, one, two, three) in enumerate((pieces[:4], pieces[4:])):
            first = (net.c ^ side) == 0
            by_x = jnp.where(first, one, two)
            by_y = jnp.where(first, two, one)
            sides.append(jnp.stack([jnp.stack([same, by_x]), jnp.stack([by_y, three])]))
        out = jnp.stack(net.swap(*sides))
        out = jnp.where(net.y == 0, out, out[:, ::-1])
        out = jnp.where(net.x == 0, out, out[:, :, ::-1])
        return jnp.transpose(out, (3, 2, 1, 0, 4)).reshape(wide, narrow, -1)

    vectors = in_place([p[:, self_qkv.shape[0], : small.size] for p in g2.arrays()]).astype(FULL)
    fc_bias = vectors[:, :, rows.size :].reshape(1, -1)
    vec = vectors[:, :, : rows.size].reshape(wide * narrow, rows.shape[0], -1)
    vec = jnp.transpose(vec, (1, 0, 2)).reshape(rows.shape[0], width)
    joined_bias = jnp.concatenate([vec[0], jnp.zeros((width,), FULL), vec[1]])[None]

    heads = width // PAIR
    joined, self_probs, self_mix, x_t, self_mix_t = call(
        self_forward,
        "self_forward",
        net,
        (1,),
        [whole(x), whole(joined_bias), whole(seg_col), whole(seg_row)],
        [
            whole_out((count, 3 * width), LOW),
            whole_out((pairs * heads * length, 2 * length), LOW),
            whole_out((count, width), LOW),
            whole_out((width, count), LOW),
            whole_out((width, count), LOW),
        ],
        weights=[(g2, 0, 3 * quarter)],
    )
    g4.line_end()
    g5.line_on()
    g3.turn()
    copies = g3.copy("held", "one", "two")
    g4.start(*copies)
    g3.copy("three")
    first_sum, first_low_t, query = call(
        first_half,
        "first_half",
        net,
        (1,),
        [whole(self_mix), whole(x), whole(vec)],
        [
            whole_out((count, width), FULL),
            whole_out((width, count), LOW),
            whole_out((count, width), LOW),
        ],
        [pltpu.VMEM((count, width), FULL)],
        weights=[(g3, 3 * quarter, quarter), (g3, 4 * quarter, quarter)],
    )
    tile = 512
    kv, table_t, table_t2 = call(
        table_keys,
        "table_keys",
        net,
        (table.shape[0] // tile,),
        [
            (table, (tile, width), lambda t, at: (t, 0)),
            (table2, (tile, width), lambda t, at: (t, 0)),
            whole(vec),
        ],
        [
            ((2, table.shape[0], width), LOW, (2, tile, width), lambda t, at: (0, t, 0)),
            ((width, table.shape[0]), LOW, (width, tile), lambda t, at: (0, t)),
            ((width, table.shape[0]), LOW, (width, tile), lambda t, at: (0, t)),
        ],
        weights=[(g3, 0, half)],
    )
    g4.turn()
    g4.copy("held", "one")
    g5.line_end()
    g5.turn()
    g5.copy("held")
    score_rows = half // PAIR * 2 * length
    core_block = ((length, half), lambda s, p, at: (p, at[2] ^ s))
    cross_mix, cross_probs, cross_mix_t = call(
        cross_forward,
        "cross_forward",
        net,
        (2, pairs),
        [
            (query, *core_block),
            (kv, (1, held, width), lambda s, p, at: (s, p, 0)),
            (table_col, (length, 1), lambda s, p, at: (p, 0)),
            (table_row, (1, 1, held), lambda s, p, at: (p, 0, 0)),
        ],
        [
            ((count, width), LOW, *core_block),
            (
                (2, pairs, score_rows, held),
                LOW,
                (1, 1, score_rows, held),
                lambda s, p, at: (s, p, 0, 0),
            ),
            ((width, count), LOW, (half, length), lambda s, p, at: (at[2] ^ s, p)),
        ],
    )
    g4.copy("two", "three")
    second_sum, second_low, second_low_t = call(
        second_half,
        "second_half",
        net,
        (1,),
        [whole(cross_mix), whole(first_sum), whole(vec)],
        [
            whole_out((count, width), FULL),
            whole_out((count, width), LOW),
            whole_out((width, count), LOW),
        ],
        [pltpu.VMEM((count, width), FULL)],
        weights=[(g3, half, quarter)],
    )
    active, slope, active_t = call(
        feed_in,
        "feed_in",
        net,
        (1,),
        [whole(second_low), whole(fc_bias)],
        [
            whole_out((count, hidden), LOW),
            whole_out((count, hidden), LOW),
            whole_out((hidden, count), LOW),
        ],
        weights=[(g4, 0, hidden // 4)],
    )
    g5.copy("far")
    active_t2, second_low_t2 = (net.over_core(a, g5.far) for a in (active_t, second_low_t))
    output, d_third, d_low3, grads3, send3 = call(
        feed_out,
        "feed_out",
        net,
        (1,),
        [whole(active), whole(second_sum), whole(upstream), whole(vec)],
        [
            whole_out((count, width), LOW),
            whole_out((count, width), FULL),
            whole_out((count, width), LOW),
            whole_out((8, width), FULL),
            whole_out((2, count, quarter), LOW),
        ],
        [pltpu.VMEM((count, width), FULL)],
        weights=[(g5, 0, quarter)],
    )

    got3 = net.over_core(send3)
    first_low_t2, self_mix_t2, cross_mix_t2, x_t2 = Order.pin(
        *(net.over_core(a) for a in (first_low_t, self_mix_t, cross_mix_t, x_t))
    )
    r_out = Reduction(net, "grad_out", [(active_t, active_t2, d_low3, got3, quarter, 0)]).start()
    d_hidden, g_fc_bias, send_hidden = call(
        feed_out_back,
        "feed_out_back",
        net,
        (1,),
        [whole(d_low3), whole(slope)],
        [
            whole_out((count, hidden), LOW),
            whole_out((1, hidden), FULL),
            whole_out((2, count, hidden // 4), LOW),
        ],
        weights=[(g5, 0, quarter)],
    )
    got_hidden = net.over_core(send_hidden)
    r_in = Reduction(
        net, "grad_in", [(second_low_t, second_low_t2, d_hidden, got_hidden, hidden // 4, 0)]
    ).start()
    d_sum2, d_low2, d_mix, grads2, send2 = call(
        feed_in_back,
        "feed_in_back",
        net,
        (1,),
        [whole(d_hidden), whole(d_third), whole(second_sum), whole(vec)],
        [
            whole_out((count, width), FULL),
            whole_out((count, width), LOW),
            whole_out((count, width), LOW),
            whole_out((8, width), FULL),
            whole_out((2, count, quarter), LOW),
        ],
        weights=[(g4, 0, hidden // 4), (g3, half, quarter)],
    )
    r_out.turn()
    def tables_back(side, into=()):
        block = ((length, half), lambda p, at: (p, at[2] ^ side))
        return call(
            cross_backward,
            "cross_backward",
            net,
            (pairs,),
            [
                (query, *block),
                (kv, (1, held, width), lambda p, at: (side, p, 0)),
                (cross_probs, (1, 1, score_rows, held), lambda p, at: (side, p, 0, 0)),
                (d_mix, *block),
                (cross_mix, *block),
            ],
            [
                ((count, width), LOW, *block),
                (table.shape, LOW, (held, width), lambda p, at: (p, 0)),
                whole_out((1, half), FULL),
            ],
            into=into,
        )

    d_query, d_other, grads_other = tables_back(1)
    d_query, d_mine, grads_mine = tables_back(0, (d_query,))
    d_sum1, d_low1, d_joined, grads1, send1 = call(
        self_backward,
        "self_backward",
        net,
        (1,),
        [
            whole(d_query),
            whole(d_sum2),
            whole(first_sum),
            whole(vec),
            whole(joined),
            whole(self_probs),
            whole(self_mix),
        ],
        [
            whole_out((count, width), FULL),
            whole_out((count, width), LOW),
            whole_out((count, 3 * width), LOW),
            whole_out((8, width), FULL),
            whole_out((2, count, 5 * quarter), LOW),
        ],
        weights=[(g3, 4 * quarter, quarter), (g3, 3 * quarter, quarter)],
    )
    waits = (r_out.near, r_in.pair)
    got1, got_table = net.over_core(send1, *waits), net.over_core(d_other, *waits)
    r_out.line()
    r_in.turn()
    r_self = Reduction(
        net,
        "grad_self",
        [
            (x_t, x_t2, d_joined, got1, 3 * quarter, 0),
            (self_mix_t, self_mix_t2, d_low1, got1, quarter, 3),
            (first_low_t, first_low_t2, d_query, got1, quarter, 4),
        ],
    ).start(r_in.near, r_out.step, got_table)
    grads_v = jnp.concatenate(net.swap(grads_mine, grads_other), axis=1)
    g_rows = jnp.concatenate(
        [
            grads1[:4],
            grads_v,
            grads2[:1],
            grads3[:1],
            grads1[4:5],
            grads2[1:2],
            grads3[1:2],
            grads1[5:6],
            grads2[2:3],
            grads3[2:3],
        ]
    )
    g_rows = jnp.transpose(g_rows.reshape(rows.shape[0], wide, narrow, -1), (2, 1, 0, 3))
    g_small = jnp.transpose(g_fc_bias.reshape(wide, narrow, -1), (1, 0, 2))
    g_small = jnp.concatenate([g_rows.reshape(narrow, wide, -1), g_small], axis=2).astype(LOW)
    room = extra * 3 * quarter - small.size
    g_small = jnp.pad(g_small, ((0, 0), (0, 0), (0, room)))
    g_small = g_small.reshape(2, 2, wide // 2, 2, extra, -1)
    small_mine, small_other = net.swap(g_small[:, 0], g_small[:, 1])
    small_got, got2 = net.over_core(small_other), net.over_core(send2)
    r_out.line_on()
    r_in.line()
    r_cross = Reduction(
        net,
        "grad_cross",
        [
            (table_t, table_t2, d_mine, got_table, half, None),
            (cross_mix_t, cross_mix_t2, d_low2, got2, quarter, 0),
        ],
        (small_mine, small_got),
    ).start()
    r_out.line_end()
    r_in.line_on()
    (input_grad,) = call(
        input_back,
        "input_back",
        net,
        (1,),
        [whole(d_joined), whole(d_sum1)],
        [whole_out((count, width), FULL)],
        weights=[(g2, 0, 3 * quarter)],
    )
    r_in.line_end()
    r_self.turn(r_in.total, r_out.total)
    tile = 512
    (memory_grad,) = call(
        table_back,
        "table_back",
        net,
        (table.shape[0] // tile,),
        [(d, (tile, width), lambda t, at: (t, 0)) for d in (d_mine, d_other)],
        [(table.shape, FULL, (tile, width), lambda t, at: (t, 0))],
        weights=[(g3, 0, half)],
    )
    r_cross.turn(r_self.near)
    r_self.line(r_cross.ready)
    r_self.line_on()
    r_cross.line()
    r_self.line_end()
    r_cross.line_on().line_end()

    g_out, g_in, g_cross, g_self = (r.total for r in (r_out, r_in, r_cross, r_self))
    g_small = g_cross[-extra:].reshape(-1)[: small.size]
    g_rows, g_fc_bias = g_small[: rows.size].reshape(rows.shape), g_small[rows.size :]
    return (
        output.reshape(inputs.shape),
        input_grad.reshape(inputs.shape),
        memory_grad.reshape(memory.shape),
        g_self[:, : 3 * quarter],
        g_self[:, 3 * quarter : 4 * quarter],
        g_self[:, 4 * quarter :],
        g_cross[:-extra, : 2 * quarter],
        g_cross[:-extra, 2 * quarter :],
        g_in,
        g_out,
        g_rows[:10],
        g_rows[10:],
        g_fc_bias,
    )


def solution(mesh):
    tokens = P(BOTH, None, None)
    lengths = P(BOTH, None)
    weight = P("wide", "narrow")
    vector = P(None, BOTH)
    return jax.shard_map(
        partial(per_device, wide=mesh.shape["wide"], narrow=mesh.shape["narrow"]),
        mesh=mesh,
        in_specs=(tokens,) * 3 + (lengths,) * 3 + (weight,) * 7 + (vector, vector, P(BOTH)),
        out_specs=(tokens,) * 3 + (weight,) * 7 + (vector, vector, P(BOTH)),
        check_vma=False,
    )
```

```python
import math
from functools import partial

import jax
import jax.numpy as jnp
from jax import lax
from jax.experimental import pallas as pl
from jax.experimental.pallas import tpu as pltpu
from jax.sharding import PartitionSpec as P

HD = 64
PAIR = 2 * HD
BOTH = ("wide", "narrow")
EPS = 1e-05
MASKED_SCORE = -1000000000.0
LOW = jnp.bfloat16
FULL = jnp.float32
VMEM_BYTES = 52 * 1024 * 1024
B_QUERY, B_VALUE, B_SELF_OUT, B_CROSS_Q, B_CROSS_V, B_CROSS_OUT, B_FC_OUT = range(7)
SHIFT, GAIN = 7, 10


def after(value, *others):
    return lax.optimization_barrier((value, others))[0]


class Order:
    last, soon, later = (), (), ()

    @classmethod
    def put(cls, kernel, arrays):
        first = after(arrays[0], *cls.last, *cls.soon)
        out = kernel(first, *arrays[1:])
        cls.last, cls.soon, cls.later = (out[0],), cls.later, ()
        return out

    @classmethod
    def now(cls, value, *others):
        return after(value, *cls.last, *others)

    @classmethod
    def need(cls, *arrays):
        cls.soon += arrays

    @classmethod
    def pin(cls, *arrays):
        cls.later += arrays
        return arrays


class Net:
    def __init__(self, wide, narrow):
        self.wide, self.narrow, self.lines = wide, narrow, wide // 2
        w, n = lax.axis_index("wide"), lax.axis_index("narrow")
        self.z, self.x, self.y, self.c = w // 2, w % 2, n // 2, n % 2
        self.place = jnp.stack([self.y, self.x, self.c, self.z]).astype(jnp.int32)
        both = [(i, j) for i in range(wide) for j in range(narrow)]

        def flat(i, j):
            return i * narrow + j

        def pairs(x_core):
            return [
                (flat(i, j), flat(i ^ 1, j) if j % 2 == x_core else flat(i, j ^ 2)) for i, j in both
            ]

        self.first, self.second = pairs(0), pairs(1)
        self.core = [(j, j ^ 1) for j in range(narrow)]
        self.groups = [[z * 2 + x for z in range(self.lines)] for x in range(2)]

    def across(self, value, way, *others):
        return lax.ppermute(Order.now(value, *others), BOTH, way)

    def over_core(self, value, *others):
        return lax.ppermute(Order.now(value, *others), "narrow", self.core)

    def along(self, value, step, *others):
        way = [(w, ((w // 2) ^ step) * 2 + w % 2) for w in range(self.wide)]
        return lax.ppermute(Order.now(value, *others), "wide", way)

    def swap(self, a, b):
        first = self.c == 0
        return jnp.where(first, a, b), jnp.where(first, b, a)


class Weight:
    def __init__(self, net, shard, before=()):
        self.net = net
        self.rows = shard.shape[0]
        self.shard = after(shard, *before)

    def at_once(self):
        self.held = lax.all_gather(
            self.shard, "wide", axis=0, axis_index_groups=self.net.groups
        )
        return self

    def line(self, *others):
        net = self.net
        if net.lines == 4:
            self.got = net.along(self.shard, 2, *others)
        return self

    def line_on(self):
        net = self.net
        if net.lines == 4:
            self.held = stack(net, [self.shard, self.got], 1)
            self.got = net.along(self.held, 1)
        return self

    def line_end(self):
        net = self.net
        if net.lines == 4:
            self.held = stack(net, [self.held, self.got], 0)
        else:
            self.at_once()
        return self

    def start(self, *others):
        net = self.net
        self.one = net.across(self.held, net.first, *others)
        self.two = net.across(self.held, net.second, *others)
        return self

    def turn(self, *others):
        net = self.net
        self.three = net.across(self.one, net.second, self.two, *others)
        return self

    def copy(self, *names, after=None):
        others = () if after is None else (after,)
        new = [self.net.over_core(getattr(self, name), *others) for name in names]
        self.copies = [*getattr(self, "copies", ()), *new]
        return new

    def arrays(self):
        return [self.held, self.one, self.two, self.three, *self.copies]

    def spots(self):
        return [(i, 0) for i in range(8)]


class PairedWeight(Weight):
    def begin(self, *others):
        self.mate = self.net.across(self.shard, self.net.first, *others)
        return self

    def pair(self):
        self.single = self.rows
        self.shard = jnp.concatenate([self.shard, self.mate])
        return self

    def turn(self, *others):
        self.far = self.net.across(self.held, self.net.second, *others)
        return self

    def arrays(self):
        return [self.held, self.far, *self.copies]

    def spots(self):
        return [(2 * side + k // 2, k % 2 * self.rows) for side in range(2) for k in range(4)]


def piece_place(place, index):
    side, k = divmod(index, 4)
    c = place[2] ^ side
    dy, dx = ((0, 0), (c, 1 - c), (1 - c, c), (1, 1))[k]
    return place[0] ^ dy, place[1] ^ dx, side


class Loaded:
    def __init__(self, place, arrays, spots, buffer, sems, rows, col):
        self.buffer = buffer
        size = buffer.shape[-1]
        self.copies = []
        for i, (array, first) in enumerate(spots):
            y, x, side = piece_place(place, i)
            self.copies.append(
                pltpu.make_async_copy(
                    arrays[array].at[:, pl.ds(first, rows), pl.ds(col, size)],
                    buffer.at[side, y, :, x],
                    sems.at[i],
                )
            )

    def start(self):
        for copy in self.copies:
            copy.start()

    def wait(self, side):
        for copy in self.copies[4 * side : 4 * side + 4]:
            copy.wait()

    def part(self, side, y):
        return self.buffer[side, y].reshape(-1, self.buffer.shape[-1])


class Reduction:
    def __init__(self, net, name, products, more=None):
        self.net = net
        self.pair, self.near, self.own = quarter_grads(net, name, products, more)

    def start(self, *others):
        self.pair = self.net.across(self.pair, self.net.second, *others)
        return self

    def turn(self, *others):
        pair = Order.now(self.pair, *others)
        self.ready = (self.near.astype(FULL) + pair[0].astype(FULL)).astype(LOW)
        Order.need(self.ready)
        self.near = self.net.across(self.ready, self.net.first)
        return self

    def line(self, *others):
        net = self.net
        near = Order.now(self.near, *others)
        total = self.own.astype(FULL) + self.pair[1].astype(FULL) + near.astype(FULL)
        self.total = total.astype(LOW)
        Order.need(self.total)
        self.step = net.along(self.total[total.shape[0] // 2 :], 1)
        return self

    def line_on(self, *others):
        net = self.net
        half, step = self.total.shape[0] // 2, 2
        total = self.total[:half].astype(FULL) + Order.now(self.step, *others).astype(FULL)
        while half > 2:
            half //= 2
            low = total.astype(LOW)
            got = net.along(low[half:], step)
            total = low[:half].astype(FULL) + got.astype(FULL)
            step *= 2
        self.total = total.astype(LOW)
        Order.need(self.total)
        if half > 1:
            self.step = net.along(self.total[1:], step)
        return self

    def line_end(self, *others):
        total = self.total[0].astype(FULL)
        if self.total.shape[0] > 1:
            total += Order.now(self.step, *others)[0].astype(FULL)
        self.total = total
        return self


def call(body, name, net, grid, ins, outs, scratch=(), weights=(), into=()):
    operands, buffers, first = [], [], []
    for weight, _, size in weights:
        first.append(len(operands))
        operands += weight.arrays()
        shape = (2, 2, net.lines, 2, weight.rows, size)
        buffers += [pltpu.VMEM(shape, LOW), pltpu.SemaphoreType.DMA((8,))]
    plain = len(ins) + len(outs)
    fixed = len(operands)
    operands += into
    specs = [pl.BlockSpec(memory_space=pl.ANY)] * len(operands)

    def run(place, *refs):
        pieces, rest = refs[:fixed], refs[len(operands) :]
        held = rest[plain : plain + len(buffers)]
        rest = rest[:plain] + rest[plain + len(buffers) :]
        loaded = [
            Loaded(
                place,
                pieces[first[i] :],
                weight.spots(),
                held[2 * i],
                held[2 * i + 1],
                weight.rows,
                col,
            )
            for i, (weight, col, _) in enumerate(weights)
        ]

        def start():
            for weight in loaded:
                weight.start()

        if grid == (1,):
            start()
        elif loaded:
            pl.when(pl.program_id(0) == 0)(start)
        body(place, *loaded, *rest)

    kernel = pl.pallas_call(
        run,
        grid_spec=pltpu.PrefetchScalarGridSpec(
            num_scalar_prefetch=1,
            grid=grid,
            in_specs=specs + [pl.BlockSpec(b, m) for _, b, m in ins],
            out_specs=[pl.BlockSpec(b, m) for _, _, b, m in outs],
            scratch_shapes=[*buffers, *scratch],
        ),
        out_shape=[jax.ShapeDtypeStruct(s, d) for s, d, _, _ in outs],
        compiler_params=pltpu.CompilerParams(
            dimension_semantics=("arbitrary",) * len(grid), vmem_limit_bytes=VMEM_BYTES
        ),
        cost_estimate=pl.CostEstimate(flops=1000, bytes_accessed=1000, transcendentals=0),
        input_output_aliases={1 + fixed + i: i for i in range(len(into))},
        name=name,
    )
    return Order.put(partial(kernel, net.place), [*operands, *(a for a, _, _ in ins)])


def stack(net, pieces, bit):
    rows, cols = pieces[0].shape[-2:]

    def body(place, *refs):
        for i in range(2):

            @pl.when(pl.program_id(0) == i)
            def _(i=i):
                refs[-1][:, 0] = refs[i][...].reshape(-1, rows, cols)

    lead = pieces[0].size // (rows * cols)
    shape = (lead, 2, rows, cols)
    (out,) = call(
        body,
        "stack",
        net,
        (2,),
        [whole(p) for p in pieces],
        [(shape, LOW, (lead, 1, rows, cols), lambda s, at: (0, ((at[3] >> bit) & 1) ^ s, 0, 0))],
    )
    return out.reshape(2 * lead, rows, cols)


def whole(array):
    return (array, array.shape, lambda *_: (0,) * array.ndim)


def whole_out(shape, dtype):
    return (shape, dtype, shape, lambda *_: (0,) * len(shape))


def lanes(index, size):
    return pl.ds(pl.multiple_of(index * size, 128), size)


def block_of(place, side, y):
    return 2 * y + (place[2] ^ side)


def each_block(place, weight, wait=True):
    for side in range(2):
        if wait:
            weight.wait(side)
        for y in range(2):
            yield side, y, block_of(place, side, y)


def dot(a, b):
    return jnp.dot(a, b, preferred_element_type=FULL)


def dot_t(a, b):
    return lax.dot_general(a, b, (((1,), (1,)), ((), ())), preferred_element_type=FULL)


def t_dot(a, b):
    return lax.dot_general(a, b, (((0,), (0,)), ((), ())), preferred_element_type=FULL)


def norm_parts(z):
    centred = z - jnp.mean(z, axis=-1, keepdims=True)
    scale = lax.rsqrt(jnp.mean(centred * centred, axis=-1, keepdims=True) + EPS)
    return centred * scale, scale


def norm(z, vec, which):
    unit, _ = norm_parts(z)
    return unit * vec[GAIN + which : GAIN + which + 1] + vec[SHIFT + which : SHIFT + which + 1]


def norm_back(upstream, z, gain):
    unit, scale = norm_parts(z)
    d_gain = jnp.sum(upstream * unit, axis=0, keepdims=True)
    d_shift = jnp.sum(upstream, axis=0, keepdims=True)
    inner = upstream * gain
    mean = jnp.mean(inner, axis=-1, keepdims=True)
    along = jnp.mean(inner * unit, axis=-1, keepdims=True)
    return scale * (inner - mean - unit * along), d_gain, d_shift


def column_sum(values):
    return jnp.sum(values.astype(FULL), axis=0, keepdims=True)


def two_heads(rows):
    low = lax.broadcasted_iota(jnp.int32, rows.shape, 1) < HD
    none = jnp.zeros_like(rows)
    return jnp.concatenate([jnp.where(low, rows, none), jnp.where(low, none, rows)], axis=0)


def one_row(stacked):
    half = stacked.shape[0] // 2
    low = lax.broadcasted_iota(jnp.int32, (half, PAIR), 1) < HD
    return jnp.where(low, stacked[:half], stacked[half:])


def one_side(stacked):
    half = stacked.shape[1] // 2
    low = lax.broadcasted_iota(jnp.int32, (PAIR, half), 0) < HD
    return jnp.where(low, stacked[:, :half], stacked[:, half:])


def softmax_sides(query, keys, allowed):
    logits = jnp.where(allowed, dot_t(keys, two_heads(query)) * HD ** (-0.5), MASKED_SCORE)
    weight = jnp.exp(logits - jnp.max(logits, axis=0, keepdims=True))
    return (weight * (1.0 / jnp.sum(weight, axis=0, keepdims=True))).astype(LOW)


def softmax_rows(query, keys, allowed):
    logits = jnp.where(allowed, dot_t(two_heads(query), keys) * HD ** (-0.5), MASKED_SCORE)
    weight = jnp.exp(logits - jnp.max(logits, axis=-1, keepdims=True))
    return (weight * (1.0 / jnp.sum(weight, axis=-1, keepdims=True))).astype(LOW)


def attend_back_rows(query, keys, values, probs, upstream, mix):
    queries, ups = two_heads(query), two_heads(upstream)
    product = two_heads(upstream.astype(FULL) * mix.astype(FULL))
    row_dot = jnp.sum(product, axis=1, keepdims=True)
    d_scores = (probs.astype(FULL) * (dot_t(ups, values) - row_dot)).astype(LOW)
    scale = HD ** (-0.5)
    return one_row(dot(d_scores, keys)) * scale, t_dot(d_scores, queries) * scale, t_dot(probs, ups)


def row_dots(mix, upstream):
    product = (mix.astype(FULL) * upstream.astype(FULL)).T
    sums = [
        jnp.sum(product[i : i + HD], axis=0, keepdims=True) for i in range(0, product.shape[0], HD)
    ]
    return [jnp.concatenate(sums[i : i + 2], axis=1) for i in range(0, len(sums), 2)]


def attend_back_sides(query, keys, values, probs, upstream, row_dot):
    queries, ups = two_heads(query), two_heads(upstream)
    scale = HD ** (-0.5)
    d_scores = (probs.astype(FULL) * (dot_t(values, ups) - row_dot)).astype(LOW)
    d_query = one_side(t_dot(keys, d_scores)).T * scale
    return d_query, dot(d_scores, queries) * scale, dot(probs, ups)


def twice(mask, axis):
    wide = jnp.where(mask, 1, 0)
    return jnp.concatenate([wide, wide], axis=axis) == 1


def self_forward(
    place, weight, x, bias, seg_col, seg_row, joined, probs, mix, x_t, mix_t
):
    x_t[...] = x[...].T
    for side, y, n in each_block(place, weight):
        w = weight.part(side, y)
        at = lanes(n, w.shape[-1])
        joined[:, at] = (dot(x[...], w) + bias[:, at]).astype(LOW)
    width, rows = mix.shape[1], seg_row.shape[-1]
    above = lax.broadcasted_iota(jnp.int32, (rows, rows), 0) <= lax.broadcasted_iota(
        jnp.int32, (rows, rows), 1
    )
    for p in range(mix.shape[0] // rows):
        at = pl.ds(p * rows, rows)
        allowed = twice((seg_col[at, :] == seg_row[p]) & above, 1)
        for h in range(width // PAIR):
            q, k, v = (joined[at, pl.ds(i * width + h * PAIR, PAIR)] for i in range(3))
            low = softmax_sides(q, k, allowed)
            probs[pl.ds((p * (width // PAIR) + h) * rows, rows), :] = low
            mixed = one_side(t_dot(v, low)).astype(LOW)
            mix_t[pl.ds(h * PAIR, PAIR), at] = mixed
            mix[at, pl.ds(h * PAIR, PAIR)] = mixed.T


def first_half(place, w_out, w_query, mix, x, vec, first_sum, low_t, query, acc):
    for side, y, n in each_block(place, w_out):
        w = w_out.part(side, y)
        acc[:, lanes(n, w.shape[-1])] = dot(mix[...], w)
    z = x[...].astype(FULL) + (acc[...] + vec[B_SELF_OUT : B_SELF_OUT + 1, :])
    first_sum[...] = z
    low = norm(z, vec, 0).astype(LOW)
    low_t[...] = low.T
    for side, y, n in each_block(place, w_query):
        w = w_query.part(side, y)
        at = lanes(n, w.shape[-1])
        query[:, at] = (dot(low, w) + vec[B_CROSS_Q : B_CROSS_Q + 1, at]).astype(LOW)


def table_keys(place, weight, x, x2, vec, out, x_t, x_t2):
    half = out.shape[-1] // 2

    @pl.when(pl.program_id(0) == 0)
    def _():
        weight.wait(0)
        weight.wait(1)

    for side in range(2):
        bias = vec[B_CROSS_V : B_CROSS_V + 1, lanes(place[2] ^ side, half)]
        out[side, :, :half] = dot(x[...], weight.part(side, 0)).astype(LOW)
        out[side, :, half:] = (dot(x[...], weight.part(side, 1)) + bias).astype(LOW)
    x_t[...] = x[...].T
    x_t2[...] = x2[...].T


def cross_forward(place, query, kv, table_col, table_row, mix, probs, mix_t):
    rows, half = query.shape
    allowed = twice(table_col[...] == table_row[0], 0)
    for h in range(half // PAIR):
        at = pl.ds(h * PAIR, PAIR)
        low = softmax_rows(query[:, at], kv[0, :, at], allowed)
        probs[0, 0, pl.ds(h * 2 * rows, 2 * rows), :] = low
        mixed = one_row(dot(low, kv[0, :, pl.ds(half + h * PAIR, PAIR)])).astype(LOW)
        mix[:, at] = mixed
        mix_t[at, :] = mixed.T


def second_half(place, weight, mix, first_sum, vec, second_sum, second_low, low_t, acc):
    for side, y, n in each_block(place, weight):
        w = weight.part(side, y)
        acc[:, lanes(n, w.shape[-1])] = dot(mix[...], w)
    z = norm(first_sum[...], vec, 0) + (acc[...] + vec[B_CROSS_OUT : B_CROSS_OUT + 1, :])
    second_sum[...] = z
    low = norm(z, vec, 1).astype(LOW)
    second_low[...] = low
    low_t[...] = low.T


def feed_in(place, weight, x, bias, active, slope, active_t):
    for side, y, n in each_block(place, weight):
        w = weight.part(side, y)
        cols = w.shape[-1]
        at = lanes(n, cols)
        hidden = dot(x[...], w) + bias[:, at]
        share = 0.5 + 0.5 * lax.erf(hidden * 2 ** (-0.5))
        low = (hidden * share).astype(LOW)
        active[:, at] = low
        active_t[pl.ds(pl.multiple_of(n * cols, 128), cols), :] = low.T
        density = jnp.exp(hidden * hidden * (-0.5)) * (2 * math.pi) ** (-0.5)
        slope[:, at] = (share + hidden * density).astype(LOW)


def give(place, send, rows, first=0):
    cols = rows.shape[-1] // 4
    for y in range(2):
        send[y, :, first : first + cols] = rows[:, lanes(block_of(place, 1, y), cols)]


def feed_out(
    place, weight, active, second_sum, cotangent, vec, output, d_third, d_low, grads, send, acc
):
    for side, y, n in each_block(place, weight):
        w = weight.part(side, y)
        acc[:, lanes(n, w.shape[-1])] = dot(active[...], w)
    z = norm(second_sum[...], vec, 1) + (acc[...] + vec[B_FC_OUT : B_FC_OUT + 1, :])
    output[...] = norm(z, vec, 2).astype(LOW)
    back, d_gain, d_shift = norm_back(cotangent[...].astype(FULL), z, vec[GAIN + 2 : GAIN + 3])
    d_third[...] = back
    low = back.astype(LOW)
    d_low[...] = low
    grads[0:1, :] = column_sum(low)
    grads[1:2, :] = d_shift
    grads[2:3, :] = d_gain
    give(place, send, d_low)


def through(place, rows, weight):
    total = 0
    for side, y, n in each_block(place, weight):
        w = weight.part(side, y)
        total += dot_t(rows[:, lanes(n, w.shape[-1])], w)
    return total


def feed_out_back(place, weight, d_third, slope, d_hidden, grads, send):
    _, _, lines, _, rows, cols = weight.buffer.shape
    weight.wait(0)
    weight.wait(1)
    step = max(1, min(lines, 1024 // (2 * rows)))
    for z in range(0, lines, step):
        total = 0
        for side, y, n in each_block(place, weight, wait=False):
            w = weight.buffer[side, y, z : z + step].reshape(-1, cols)
            total += dot_t(d_third[:, lanes(n, cols)], w)
        at = pl.ds(z * 2 * rows, step * 2 * rows)
        low = (slope[:, at].astype(FULL) * total).astype(LOW)
        d_hidden[:, at] = low
        grads[:, at] = column_sum(low)
    give(place, send, d_hidden)


def feed_in_back(
    place, w_in, w_out, d_hidden, d_third, second_sum, vec, d_sum, d_low, d_mix, grads, send
):
    upstream = d_third[...] + through(place, d_hidden, w_in)
    back, d_gain, d_shift = norm_back(upstream, second_sum[...], vec[GAIN + 1 : GAIN + 2])
    d_sum[...] = back
    low = back.astype(LOW)
    d_low[...] = low
    grads[0:1, :] = column_sum(low)
    grads[1:2, :] = d_shift
    grads[2:3, :] = d_gain
    d_mix[...] = through(place, d_low, w_out).astype(LOW)
    give(place, send, d_low)


def cross_backward(place, query, kv, probs, d_mix, mix, d_query, d_kv, grads):
    rows, half = query.shape
    for h in range(half // PAIR):
        at, beside = pl.ds(h * PAIR, PAIR), pl.ds(half + h * PAIR, PAIR)
        dq, dk, dv = attend_back_rows(
            query[:, at],
            kv[0, :, at],
            kv[0, :, beside],
            probs[0, 0, pl.ds(h * 2 * rows, 2 * rows), :],
            d_mix[:, at],
            mix[:, at],
        )
        d_query[:, at] = dq.astype(LOW)
        d_kv[:, at] = dk.astype(LOW)
        low = dv.astype(LOW)
        d_kv[:, beside] = low
        before = jnp.where(pl.program_id(0) == 0, 0.0, grads[:, at])
        grads[:, at] = before + column_sum(low)


def self_backward(
    place, w_query, w_out, d_query, d_sum2, first_sum, vec, joined, probs, mix,
    d_sum, d_low, d_joined, grads, send,
):
    width = d_sum.shape[-1]
    upstream = d_sum2[...] + through(place, d_query, w_query)
    back, d_gain, d_shift = norm_back(upstream, first_sum[...], vec[GAIN : GAIN + 1])
    d_sum[...] = back
    low = back.astype(LOW)
    d_low[...] = low
    d_mix = through(place, d_low, w_out).astype(LOW)
    rows = probs.shape[-1] // 2
    heads = width // PAIR
    for p in range(d_sum.shape[0] // rows):
        at = pl.ds(p * rows, rows)
        ups = d_mix[p * rows : (p + 1) * rows]
        dots = row_dots(mix[at, :], ups)
        for h in range(heads):
            where = [pl.ds(i * width + h * PAIR, PAIR) for i in range(3)]
            q, k, v = (joined[at, w] for w in where)
            found = attend_back_sides(
                q,
                k,
                v,
                probs[pl.ds((p * heads + h) * rows, rows), :],
                ups[:, h * PAIR : (h + 1) * PAIR],
                dots[h],
            )
            for w, value in zip(where, found):
                d_joined[at, w] = value.astype(LOW)
    grads[0:1, :] = column_sum(d_joined[:, :width])
    grads[1:2, :] = column_sum(d_joined[:, 2 * width :])
    grads[2:3, :] = column_sum(low)
    grads[3:4, :] = column_sum(d_query[...])
    grads[4:5, :] = d_shift
    grads[5:6, :] = d_gain
    give(place, send, d_joined)
    give(place, send, d_low, 3 * width // 4)
    give(place, send, d_query, width)


def input_back(place, weight, d_joined, d_sum, out):
    out[...] = d_sum[...] + through(place, d_joined, weight)


def table_back(place, weight, d_mine, d_other, out):
    @pl.when(pl.program_id(0) == 0)
    def _():
        weight.wait(0)
        weight.wait(1)

    half = d_mine.shape[-1] // 2
    total = 0
    for side, d in enumerate((d_mine, d_other)):
        for y in range(2):
            total += dot_t(d[:, y * half : (y + 1) * half], weight.part(side, y))
    out[...] = total


def quarter_place(step, place):
    c = place[2]
    dy = jnp.where(step == 0, 1, jnp.where(step == 1, 1 - c, jnp.where(step == 2, c, 0)))
    dx = jnp.where(step == 0, 1, jnp.where(step == 1, c, jnp.where(step == 2, 1 - c, 0)))
    return place[0] ^ dy, place[1] ^ dx


def quarter_grads(net, name, products, more):
    lines = net.lines
    ins = []
    for left, left2, right, right2, size, first in products:
        for a in (left, left2):
            view = a.reshape(lines, 2, -1, a.shape[-1])
            block = (lines, 1) + view.shape[2:]
            ins.append((view, block, lambda s, at: (0, quarter_place(s, at)[1], 0, 0)))
        if first is None:
            for a in (right, right2):
                ins.append(
                    (a, (a.shape[0], size), lambda s, at: (0, quarter_place(s, at)[0]))
                )
        else:
            ins.append(
                (
                    right,
                    (right.shape[0], size),
                    lambda s, at: (0, 2 * quarter_place(s, at)[0] + at[2]),
                )
            )
            ins.append(
                (
                    right2,
                    (1, right2.shape[1], size),
                    lambda s, at, first=first: (quarter_place(s, at)[0], 0, first),
                )
            )
    rows = products[0][0].shape[0] // net.wide
    cols = sum(p[4] for p in products)
    extra = more[0].shape[3] if more else 0
    for a in more or ():

        def corner(s, at):
            y, x = quarter_place(s, at)
            return (y, 0, x, 0, 0)

        ins.append((a, (1, lines, 1, extra, cols), corner))

    def body(place, *refs):
        outs = refs[len(ins) :]
        quarters = []
        start = 0
        for i, (_, _, _, _, size, first) in enumerate(products):
            left, left2, right, right2 = refs[4 * i : 4 * i + 4]
            l, l2 = (a[:, 0].reshape(lines * rows, -1) for a in (left, left2))
            r2 = right2[...] if first is None else right2[0]
            value = dot(l, right[...]) + dot(l2, r2)
            quarters.append((start, size, value.astype(LOW).reshape(lines, rows, size)))
            start += size

        def put(out):
            for z in range(lines):
                differs = place[3] ^ z
                to = sum(
                    ((differs >> bit) & 1) * (lines >> (bit + 1))
                    for bit in range(lines.bit_length() - 1)
                )
                for start, size, value in quarters:
                    out[to, :rows, start : start + size] = value[z]
                if extra:
                    a, b = refs[4 * len(products) : len(ins)]
                    value = a[0, z, 0].astype(FULL) + b[0, z, 0].astype(FULL)
                    out[to, rows:, :] = value.astype(LOW)

        step = pl.program_id(0)
        pl.when(step < 2)(lambda: put(outs[0].at[0]))
        pl.when(step == 2)(lambda: put(outs[1]))
        pl.when(step == 3)(lambda: put(outs[2]))

    shape = (lines, rows + extra, cols)
    return call(
        body,
        name,
        net,
        (4,),
        ins,
        [
            ((2,) + shape, LOW, (1,) + shape, lambda s, at: (jnp.minimum(s, 1), 0, 0, 0)),
            whole_out(shape, LOW),
            whole_out(shape, LOW),
        ],
    )


def segment_index(lengths, count):
    segment_ends = jnp.cumsum(lengths, axis=-1)
    position = jnp.arange(count, dtype=jnp.int32)
    passed = (position[None, :, None] >= segment_ends[:, None, :]).astype(jnp.int32)
    return jnp.sum(passed, axis=-1)


def per_device(
    inputs,
    memory,
    cotangent,
    dec_lengths,
    mem_lengths,
    seg_table,
    self_qkv,
    self_out,
    cross_q,
    cross_kv,
    cross_out,
    fc_in,
    fc_out,
    vec_bias,
    norm_gain,
    fc_in_bias,
    *,
    wide,
    narrow,
):
    net = Net(wide, narrow)
    Order.last = Order.soon = Order.later = ()
    pairs, length, width = inputs.shape
    held = memory.shape[1]
    x = inputs.reshape(-1, width)
    table = memory.reshape(-1, width)
    upstream = cotangent.reshape(-1, width)
    count, quarter, half = x.shape[0], width // narrow, width // 2
    hidden = fc_out.shape[0] * wide

    rows = jnp.concatenate([vec_bias, norm_gain])
    small = jnp.concatenate([rows.reshape(-1), fc_in_bias])
    extra = 16
    small_rows = jnp.zeros((extra, self_qkv.shape[1]), LOW).at[0, : small.size].set(small)
    table2 = net.over_core(table)
    g2 = Weight(net, jnp.concatenate([self_qkv, small_rows])).at_once()
    g2.rows = self_qkv.shape[0]
    shards = jnp.concatenate([cross_kv, cross_out, self_out, cross_q], axis=1)
    g3, g4, g5 = Weight(net, shards), Weight(net, fc_in), PairedWeight(net, fc_out).begin()
    g2.start(g5.mate)
    g3.line(g2.held, g5.mate)
    Order.need(table2, *g2.copy("held", after=g5.mate))
    g3.line_on()
    g4.line()
    g2.turn()
    Order.need(*g2.copy("one", "two"))
    if net.lines == 4:
        Order.need(g4.got)
    g3.line_end()
    g3.start()
    g4.line_on()
    g5.pair().line()
    g2.copy("three")

    segments = segment_index(dec_lengths, length)
    tables = segment_index(mem_lengths, held)
    matches = segments[:, :, None] == jnp.arange(dec_lengths.shape[-1], dtype=jnp.int32)
    query_table = jnp.sum(jnp.where(matches, seg_table[:, None, :], 0), axis=-1)
    seg_col, seg_row = segments.reshape(-1, 1), segments.reshape(pairs, 1, length)
    table_col, table_row = query_table.reshape(-1, 1), tables.reshape(pairs, 1, held)

    def in_place(pieces):
        sides = []
        for side, (same, one, two, three) in enumerate((pieces[:4], pieces[4:])):
            first = (net.c ^ side) == 0
            by_x = jnp.where(first, one, two)
            by_y = jnp.where(first, two, one)
            sides.append(jnp.stack([jnp.stack([same, by_x]), jnp.stack([by_y, three])]))
        out = jnp.stack(net.swap(*sides))
        out = jnp.where(net.y == 0, out, out[:, ::-1])
        out = jnp.where(net.x == 0, out, out[:, :, ::-1])
        return jnp.transpose(out, (3, 2, 1, 0, 4)).reshape(wide, narrow, -1)

    vectors = in_place([p[:, self_qkv.shape[0], : small.size] for p in g2.arrays()]).astype(FULL)
    fc_bias = vectors[:, :, rows.size :].reshape(1, -1)
    vec = vectors[:, :, : rows.size].reshape(wide * narrow, rows.shape[0], -1)
    vec = jnp.transpose(vec, (1, 0, 2)).reshape(rows.shape[0], width)
    joined_bias = jnp.concatenate([vec[0], jnp.zeros((width,), FULL), vec[1]])[None]

    heads = width // PAIR
    joined, self_probs, self_mix, x_t, self_mix_t = call(
        self_forward,
        "self_forward",
        net,
        (1,),
        [whole(x), whole(joined_bias), whole(seg_col), whole(seg_row)],
        [
            whole_out((count, 3 * width), LOW),
            whole_out((pairs * heads * length, 2 * length), LOW),
            whole_out((count, width), LOW),
            whole_out((width, count), LOW),
            whole_out((width, count), LOW),
        ],
        weights=[(g2, 0, 3 * quarter)],
    )
    g4.line_end()
    g5.line_on()
    g3.turn()
    copies = g3.copy("held", "one", "two")
    g4.start(*copies)
    g3.copy("three")
    first_sum, first_low_t, query = call(
        first_half,
        "first_half",
        net,
        (1,),
        [whole(self_mix), whole(x), whole(vec)],
        [
            whole_out((count, width), FULL),
            whole_out((width, count), LOW),
            whole_out((count, width), LOW),
        ],
        [pltpu.VMEM((count, width), FULL)],
        weights=[(g3, 3 * quarter, quarter), (g3, 4 * quarter, quarter)],
    )
    tile = 512
    kv, table_t, table_t2 = call(
        table_keys,
        "table_keys",
        net,
        (table.shape[0] // tile,),
        [
            (table, (tile, width), lambda t, at: (t, 0)),
            (table2, (tile, width), lambda t, at: (t, 0)),
            whole(vec),
        ],
        [
            ((2, table.shape[0], width), LOW, (2, tile, width), lambda t, at: (0, t, 0)),
            ((width, table.shape[0]), LOW, (width, tile), lambda t, at: (0, t)),
            ((width, table.shape[0]), LOW, (width, tile), lambda t, at: (0, t)),
        ],
        weights=[(g3, 0, half)],
    )
    g4.turn()
    g4.copy("held", "one")
    g5.line_end()
    g5.turn()
    g5.copy("held")
    score_rows = half // PAIR * 2 * length
    core_block = ((length, half), lambda s, p, at: (p, at[2] ^ s))
    cross_mix, cross_probs, cross_mix_t = call(
        cross_forward,
        "cross_forward",
        net,
        (2, pairs),
        [
            (query, *core_block),
            (kv, (1, held, width), lambda s, p, at: (s, p, 0)),
            (table_col, (length, 1), lambda s, p, at: (p, 0)),
            (table_row, (1, 1, held), lambda s, p, at: (p, 0, 0)),
        ],
        [
            ((count, width), LOW, *core_block),
            (
                (2, pairs, score_rows, held),
                LOW,
                (1, 1, score_rows, held),
                lambda s, p, at: (s, p, 0, 0),
            ),
            ((width, count), LOW, (half, length), lambda s, p, at: (at[2] ^ s, p)),
        ],
    )
    g4.copy("two", "three")
    second_sum, second_low, second_low_t = call(
        second_half,
        "second_half",
        net,
        (1,),
        [whole(cross_mix), whole(first_sum), whole(vec)],
        [
            whole_out((count, width), FULL),
            whole_out((count, width), LOW),
            whole_out((width, count), LOW),
        ],
        [pltpu.VMEM((count, width), FULL)],
        weights=[(g3, half, quarter)],
    )
    active, slope, active_t = call(
        feed_in,
        "feed_in",
        net,
        (1,),
        [whole(second_low), whole(fc_bias)],
        [
            whole_out((count, hidden), LOW),
            whole_out((count, hidden), LOW),
            whole_out((hidden, count), LOW),
        ],
        weights=[(g4, 0, hidden // 4)],
    )
    g5.copy("far")
    active_t2, second_low_t2 = (net.over_core(a, g5.far) for a in (active_t, second_low_t))
    output, d_third, d_low3, grads3, send3 = call(
        feed_out,
        "feed_out",
        net,
        (1,),
        [whole(active), whole(second_sum), whole(upstream), whole(vec)],
        [
            whole_out((count, width), LOW),
            whole_out((count, width), FULL),
            whole_out((count, width), LOW),
            whole_out((8, width), FULL),
            whole_out((2, count, quarter), LOW),
        ],
        [pltpu.VMEM((count, width), FULL)],
        weights=[(g5, 0, quarter)],
    )

    got3 = net.over_core(send3)
    first_low_t2, self_mix_t2, cross_mix_t2, x_t2 = Order.pin(
        *(net.over_core(a) for a in (first_low_t, self_mix_t, cross_mix_t, x_t))
    )
    r_out = Reduction(net, "grad_out", [(active_t, active_t2, d_low3, got3, quarter, 0)]).start()
    d_hidden, g_fc_bias, send_hidden = call(
        feed_out_back,
        "feed_out_back",
        net,
        (1,),
        [whole(d_low3), whole(slope)],
        [
            whole_out((count, hidden), LOW),
            whole_out((1, hidden), FULL),
            whole_out((2, count, hidden // 4), LOW),
        ],
        weights=[(g5, 0, quarter)],
    )
    got_hidden = net.over_core(send_hidden)
    r_in = Reduction(
        net, "grad_in", [(second_low_t, second_low_t2, d_hidden, got_hidden, hidden // 4, 0)]
    ).start()
    d_sum2, d_low2, d_mix, grads2, send2 = call(
        feed_in_back,
        "feed_in_back",
        net,
        (1,),
        [whole(d_hidden), whole(d_third), whole(second_sum), whole(vec)],
        [
            whole_out((count, width), FULL),
            whole_out((count, width), LOW),
            whole_out((count, width), LOW),
            whole_out((8, width), FULL),
            whole_out((2, count, quarter), LOW),
        ],
        weights=[(g4, 0, hidden // 4), (g3, half, quarter)],
    )
    r_out.turn()
    def tables_back(side, into=()):
        block = ((length, half), lambda p, at: (p, at[2] ^ side))
        return call(
            cross_backward,
            "cross_backward",
            net,
            (pairs,),
            [
                (query, *block),
                (kv, (1, held, width), lambda p, at: (side, p, 0)),
                (cross_probs, (1, 1, score_rows, held), lambda p, at: (side, p, 0, 0)),
                (d_mix, *block),
                (cross_mix, *block),
            ],
            [
                ((count, width), LOW, *block),
                (table.shape, LOW, (held, width), lambda p, at: (p, 0)),
                whole_out((1, half), FULL),
            ],
            into=into,
        )

    d_query, d_other, grads_other = tables_back(1)
    d_query, d_mine, grads_mine = tables_back(0, (d_query,))
    d_sum1, d_low1, d_joined, grads1, send1 = call(
        self_backward,
        "self_backward",
        net,
        (1,),
        [
            whole(d_query),
            whole(d_sum2),
            whole(first_sum),
            whole(vec),
            whole(joined),
            whole(self_probs),
            whole(self_mix),
        ],
        [
            whole_out((count, width), FULL),
            whole_out((count, width), LOW),
            whole_out((count, 3 * width), LOW),
            whole_out((8, width), FULL),
            whole_out((2, count, 5 * quarter), LOW),
        ],
        weights=[(g3, 4 * quarter, quarter), (g3, 3 * quarter, quarter)],
    )
    waits = (r_out.near, r_in.pair)
    got1, got_table = net.over_core(send1, *waits), net.over_core(d_other, *waits)
    r_out.line()
    r_in.turn()
    r_self = Reduction(
        net,
        "grad_self",
        [
            (x_t, x_t2, d_joined, got1, 3 * quarter, 0),
            (self_mix_t, self_mix_t2, d_low1, got1, quarter, 3),
            (first_low_t, first_low_t2, d_query, got1, quarter, 4),
        ],
    ).start(r_in.near, r_out.step, got_table)
    grads_v = jnp.concatenate(net.swap(grads_mine, grads_other), axis=1)
    g_rows = jnp.concatenate(
        [
            grads1[:4],
            grads_v,
            grads2[:1],
            grads3[:1],
            grads1[4:5],
            grads2[1:2],
            grads3[1:2],
            grads1[5:6],
            grads2[2:3],
            grads3[2:3],
        ]
    )
    g_rows = jnp.transpose(g_rows.reshape(rows.shape[0], wide, narrow, -1), (2, 1, 0, 3))
    g_small = jnp.transpose(g_fc_bias.reshape(wide, narrow, -1), (1, 0, 2))
    g_small = jnp.concatenate([g_rows.reshape(narrow, wide, -1), g_small], axis=2).astype(LOW)
    room = extra * 3 * quarter - small.size
    g_small = jnp.pad(g_small, ((0, 0), (0, 0), (0, room)))
    g_small = g_small.reshape(2, 2, wide // 2, 2, extra, -1)
    small_mine, small_other = net.swap(g_small[:, 0], g_small[:, 1])
    small_got, got2 = net.over_core(small_other), net.over_core(send2)
    r_out.line_on()
    r_in.line()
    r_cross = Reduction(
        net,
        "grad_cross",
        [
            (table_t, table_t2, d_mine, got_table, half, None),
            (cross_mix_t, cross_mix_t2, d_low2, got2, quarter, 0),
        ],
        (small_mine, small_got),
    ).start()
    r_out.line_end()
    r_in.line_on()
    (input_grad,) = call(
        input_back,
        "input_back",
        net,
        (1,),
        [whole(d_joined), whole(d_sum1)],
        [whole_out((count, width), FULL)],
        weights=[(g2, 0, 3 * quarter)],
    )
    r_self.turn(r_out.total)
    tile = 512
    (memory_grad,) = call(
        table_back,
        "table_back",
        net,
        (table.shape[0] // tile,),
        [(d, (tile, width), lambda t, at: (t, 0)) for d in (d_mine, d_other)],
        [(table.shape, FULL, (tile, width), lambda t, at: (t, 0))],
        weights=[(g3, 0, half)],
    )
    r_in.line_end()
    r_cross.turn(r_self.near, r_in.total)
    r_self.line(r_cross.ready)
    r_cross.line()
    r_self.line_on(r_cross.total)
    r_cross.line_on()
    r_self.line_end(r_cross.total)
    r_cross.line_end()

    g_out, g_in, g_cross, g_self = (r.total for r in (r_out, r_in, r_cross, r_self))
    g_small = g_cross[-extra:].reshape(-1)[: small.size]
    g_rows, g_fc_bias = g_small[: rows.size].reshape(rows.shape), g_small[rows.size :]
    return (
        output.reshape(inputs.shape),
        input_grad.reshape(inputs.shape),
        memory_grad.reshape(memory.shape),
        g_self[:, : 3 * quarter],
        g_self[:, 3 * quarter : 4 * quarter],
        g_self[:, 4 * quarter :],
        g_cross[:-extra, : 2 * quarter],
        g_cross[:-extra, 2 * quarter :],
        g_in,
        g_out,
        g_rows[:10],
        g_rows[10:],
        g_fc_bias,
    )


def solution(mesh):
    tokens = P(BOTH, None, None)
    lengths = P(BOTH, None)
    weight = P("wide", "narrow")
    vector = P(None, BOTH)
    return jax.shard_map(
        partial(per_device, wide=mesh.shape["wide"], narrow=mesh.shape["narrow"]),
        mesh=mesh,
        in_specs=(tokens,) * 3 + (lengths,) * 3 + (weight,) * 7 + (vector, vector, P(BOTH)),
        out_specs=(tokens,) * 3 + (weight,) * 7 + (vector, vector, P(BOTH)),
        check_vma=False,
    )
```

```python
import math
from functools import partial

import jax
import jax.numpy as jnp
from jax import lax
from jax.experimental import pallas as pl
from jax.experimental.pallas import tpu as pltpu
from jax.sharding import PartitionSpec as P

HD = 64
PAIR = 2 * HD
BOTH = ("wide", "narrow")
EPS = 1e-05
MASKED_SCORE = -1000000000.0
LOW = jnp.bfloat16
FULL = jnp.float32
VMEM_BYTES = 52 * 1024 * 1024
VMEM_OF = {"cross_backward": 46 * 1024 * 1024}
B_QUERY, B_VALUE, B_SELF_OUT, B_CROSS_Q, B_CROSS_V, B_CROSS_OUT, B_FC_OUT = range(7)
SHIFT, GAIN = 7, 10


def after(value, *others):
    return lax.optimization_barrier((value, others))[0]


class Order:
    last, soon, later = (), (), ()

    @classmethod
    def put(cls, kernel, arrays):
        first = after(arrays[0], *cls.last, *cls.soon)
        out = kernel(first, *arrays[1:])
        cls.last, cls.soon, cls.later = (out[0],), cls.later, ()
        return out

    @classmethod
    def now(cls, value, *others):
        return after(value, *cls.last, *others)

    @classmethod
    def need(cls, *arrays):
        cls.soon += arrays

    @classmethod
    def pin(cls, *arrays):
        cls.later += arrays
        return arrays


class Net:
    def __init__(self, wide, narrow):
        self.wide, self.narrow, self.lines = wide, narrow, wide // 2
        w, n = lax.axis_index("wide"), lax.axis_index("narrow")
        self.z, self.x, self.y, self.c = w // 2, w % 2, n // 2, n % 2
        self.place = jnp.stack([self.y, self.x, self.c, self.z]).astype(jnp.int32)
        both = [(i, j) for i in range(wide) for j in range(narrow)]

        def flat(i, j):
            return i * narrow + j

        def pairs(x_core):
            return [
                (flat(i, j), flat(i ^ 1, j) if j % 2 == x_core else flat(i, j ^ 2)) for i, j in both
            ]

        self.first, self.second = pairs(0), pairs(1)
        self.core = [(j, j ^ 1) for j in range(narrow)]
        self.groups = [[z * 2 + x for z in range(self.lines)] for x in range(2)]

    def across(self, value, way, *others):
        return lax.ppermute(Order.now(value, *others), BOTH, way)

    def over_core(self, value, *others):
        return lax.ppermute(Order.now(value, *others), "narrow", self.core)

    def along(self, value, step, *others):
        way = [(w, ((w // 2) ^ step) * 2 + w % 2) for w in range(self.wide)]
        return lax.ppermute(Order.now(value, *others), "wide", way)

    def swap(self, a, b):
        first = self.c == 0
        return jnp.where(first, a, b), jnp.where(first, b, a)


class Weight:
    def __init__(self, net, shard, before=()):
        self.net = net
        self.rows = shard.shape[0]
        self.shard = after(shard, *before)

    def at_once(self):
        self.held = lax.all_gather(
            self.shard, "wide", axis=0, axis_index_groups=self.net.groups
        )
        return self

    def line(self, *others):
        net = self.net
        if net.lines == 4:
            self.got = net.along(self.shard, 2, *others)
        return self

    def line_on(self):
        net = self.net
        if net.lines == 4:
            self.held = stack(net, [self.shard, self.got], 1)
            self.got = net.along(self.held, 1)
        return self

    def line_end(self):
        net = self.net
        if net.lines == 4:
            self.held = stack(net, [self.held, self.got], 0)
        else:
            self.at_once()
        return self

    def start(self, *others):
        net = self.net
        self.one = net.across(self.held, net.first, *others)
        self.two = net.across(self.held, net.second, *others)
        return self

    def turn(self, *others):
        net = self.net
        self.three = net.across(self.one, net.second, self.two, *others)
        return self

    def copy(self, *names, after=None):
        others = () if after is None else (after,)
        new = [self.net.over_core(getattr(self, name), *others) for name in names]
        self.copies = [*getattr(self, "copies", ()), *new]
        return new

    def arrays(self):
        return [self.held, self.one, self.two, self.three, *self.copies]

    def spots(self):
        return [(i, 0) for i in range(8)]


class PairedWeight(Weight):
    def begin(self, *others):
        self.mate = self.net.across(self.shard, self.net.first, *others)
        return self

    def pair(self):
        self.single = self.rows
        self.shard = jnp.concatenate([self.shard, self.mate])
        return self

    def turn(self, *others):
        self.far = self.net.across(self.held, self.net.second, *others)
        return self

    def arrays(self):
        return [self.held, self.far, *self.copies]

    def spots(self):
        return [(2 * side + k // 2, k % 2 * self.rows) for side in range(2) for k in range(4)]


def piece_place(place, index):
    side, k = divmod(index, 4)
    c = place[2] ^ side
    dy, dx = ((0, 0), (c, 1 - c), (1 - c, c), (1, 1))[k]
    return place[0] ^ dy, place[1] ^ dx, side


class Loaded:
    def __init__(self, place, arrays, spots, buffer, sems, rows, col):
        self.buffer = buffer
        size = buffer.shape[-1]
        self.copies = []
        for i, (array, first) in enumerate(spots):
            y, x, side = piece_place(place, i)
            self.copies.append(
                pltpu.make_async_copy(
                    arrays[array].at[:, pl.ds(first, rows), pl.ds(col, size)],
                    buffer.at[side, y, :, x],
                    sems.at[i],
                )
            )

    def start(self):
        for copy in self.copies:
            copy.start()

    def wait(self, side):
        for copy in self.copies[4 * side : 4 * side + 4]:
            copy.wait()

    def part(self, side, y):
        return self.buffer[side, y].reshape(-1, self.buffer.shape[-1])


class Reduction:
    def __init__(self, net, name, products, more=None):
        self.net = net
        self.pair, self.near, self.own = quarter_grads(net, name, products, more)

    def start(self, *others):
        self.pair = self.net.across(self.pair, self.net.second, *others)
        return self

    def turn(self, *others):
        pair = Order.now(self.pair, *others)
        self.ready = (self.near.astype(FULL) + pair[0].astype(FULL)).astype(LOW)
        Order.need(self.ready)
        self.near = self.net.across(self.ready, self.net.first)
        return self

    def line(self, *others):
        net = self.net
        near = Order.now(self.near, *others)
        total = self.own.astype(FULL) + self.pair[1].astype(FULL) + near.astype(FULL)
        self.total = total.astype(LOW)
        Order.need(self.total)
        self.step = net.along(self.total[total.shape[0] // 2 :], 1)
        return self

    def line_on(self, *others):
        net = self.net
        half, step = self.total.shape[0] // 2, 2
        total = self.total[:half].astype(FULL) + Order.now(self.step, *others).astype(FULL)
        while half > 2:
            half //= 2
            low = total.astype(LOW)
            got = net.along(low[half:], step)
            total = low[:half].astype(FULL) + got.astype(FULL)
            step *= 2
        self.total = total.astype(LOW)
        Order.need(self.total)
        if half > 1:
            self.step = net.along(self.total[1:], step)
        return self

    def line_end(self, *others):
        total = self.total[0].astype(FULL)
        if self.total.shape[0] > 1:
            total += Order.now(self.step, *others)[0].astype(FULL)
        self.total = total
        return self


def call(body, name, net, grid, ins, outs, scratch=(), weights=(), into=()):
    operands, buffers, first = [], [], []
    for weight, _, size in weights:
        first.append(len(operands))
        operands += weight.arrays()
        shape = (2, 2, net.lines, 2, weight.rows, size)
        buffers += [pltpu.VMEM(shape, LOW), pltpu.SemaphoreType.DMA((8,))]
    plain = len(ins) + len(outs)
    fixed = len(operands)
    operands += into
    specs = [pl.BlockSpec(memory_space=pl.ANY)] * len(operands)

    def run(place, *refs):
        pieces, rest = refs[:fixed], refs[len(operands) :]
        held = rest[plain : plain + len(buffers)]
        rest = rest[:plain] + rest[plain + len(buffers) :]
        loaded = [
            Loaded(
                place,
                pieces[first[i] :],
                weight.spots(),
                held[2 * i],
                held[2 * i + 1],
                weight.rows,
                col,
            )
            for i, (weight, col, _) in enumerate(weights)
        ]

        def start():
            for weight in loaded:
                weight.start()

        if grid == (1,):
            start()
        elif loaded:
            pl.when(pl.program_id(0) == 0)(start)
        body(place, *loaded, *rest)

    kernel = pl.pallas_call(
        run,
        grid_spec=pltpu.PrefetchScalarGridSpec(
            num_scalar_prefetch=1,
            grid=grid,
            in_specs=specs + [pl.BlockSpec(b, m) for _, b, m in ins],
            out_specs=[pl.BlockSpec(b, m) for _, _, b, m in outs],
            scratch_shapes=[*buffers, *scratch],
        ),
        out_shape=[jax.ShapeDtypeStruct(s, d) for s, d, _, _ in outs],
        compiler_params=pltpu.CompilerParams(
            dimension_semantics=("arbitrary",) * len(grid), vmem_limit_bytes=VMEM_OF.get(name, VMEM_BYTES)
        ),
        cost_estimate=pl.CostEstimate(flops=1000, bytes_accessed=1000, transcendentals=0),
        input_output_aliases={1 + fixed + i: i for i in range(len(into))},
        name=name,
    )
    return Order.put(partial(kernel, net.place), [*operands, *(a for a, _, _ in ins)])


def stack(net, pieces, bit):
    rows, cols = pieces[0].shape[-2:]

    def body(place, *refs):
        for i in range(2):

            @pl.when(pl.program_id(0) == i)
            def _(i=i):
                refs[-1][:, 0] = refs[i][...].reshape(-1, rows, cols)

    lead = pieces[0].size // (rows * cols)
    shape = (lead, 2, rows, cols)
    (out,) = call(
        body,
        "stack",
        net,
        (2,),
        [whole(p) for p in pieces],
        [(shape, LOW, (lead, 1, rows, cols), lambda s, at: (0, ((at[3] >> bit) & 1) ^ s, 0, 0))],
    )
    return out.reshape(2 * lead, rows, cols)


def whole(array):
    return (array, array.shape, lambda *_: (0,) * array.ndim)


def whole_out(shape, dtype):
    return (shape, dtype, shape, lambda *_: (0,) * len(shape))


def lanes(index, size):
    return pl.ds(pl.multiple_of(index * size, 128), size)


def block_of(place, side, y):
    return 2 * y + (place[2] ^ side)


def each_block(place, weight, wait=True):
    for side in range(2):
        if wait:
            weight.wait(side)
        for y in range(2):
            yield side, y, block_of(place, side, y)


def dot(a, b):
    return jnp.dot(a, b, preferred_element_type=FULL)


def dot_t(a, b):
    return lax.dot_general(a, b, (((1,), (1,)), ((), ())), preferred_element_type=FULL)


def t_dot(a, b):
    return lax.dot_general(a, b, (((0,), (0,)), ((), ())), preferred_element_type=FULL)


def norm_parts(z):
    centred = z - jnp.mean(z, axis=-1, keepdims=True)
    scale = lax.rsqrt(jnp.mean(centred * centred, axis=-1, keepdims=True) + EPS)
    return centred * scale, scale


def norm(z, vec, which):
    unit, _ = norm_parts(z)
    return unit * vec[GAIN + which : GAIN + which + 1] + vec[SHIFT + which : SHIFT + which + 1]


def norm_back(upstream, z, gain):
    unit, scale = norm_parts(z)
    d_gain = jnp.sum(upstream * unit, axis=0, keepdims=True)
    d_shift = jnp.sum(upstream, axis=0, keepdims=True)
    inner = upstream * gain
    mean = jnp.mean(inner, axis=-1, keepdims=True)
    along = jnp.mean(inner * unit, axis=-1, keepdims=True)
    return scale * (inner - mean - unit * along), d_gain, d_shift


def column_sum(values):
    return jnp.sum(values.astype(FULL), axis=0, keepdims=True)


def two_heads(rows):
    low = lax.broadcasted_iota(jnp.int32, rows.shape, 1) < HD
    none = jnp.zeros_like(rows)
    return jnp.concatenate([jnp.where(low, rows, none), jnp.where(low, none, rows)], axis=0)


def one_row(stacked):
    half = stacked.shape[0] // 2
    low = lax.broadcasted_iota(jnp.int32, (half, PAIR), 1) < HD
    return jnp.where(low, stacked[:half], stacked[half:])


def one_side(stacked):
    half = stacked.shape[1] // 2
    low = lax.broadcasted_iota(jnp.int32, (PAIR, half), 0) < HD
    return jnp.where(low, stacked[:, :half], stacked[:, half:])


def softmax_sides(query, keys, allowed):
    logits = jnp.where(allowed, dot_t(keys, two_heads(query)) * HD ** (-0.5), MASKED_SCORE)
    weight = jnp.exp(logits - jnp.max(logits, axis=0, keepdims=True))
    return (weight * (1.0 / jnp.sum(weight, axis=0, keepdims=True))).astype(LOW)


def softmax_rows(query, keys, allowed):
    logits = jnp.where(allowed, dot_t(two_heads(query), keys) * HD ** (-0.5), MASKED_SCORE)
    weight = jnp.exp(logits - jnp.max(logits, axis=-1, keepdims=True))
    return (weight * (1.0 / jnp.sum(weight, axis=-1, keepdims=True))).astype(LOW)


def attend_back_rows(query, keys, values, probs, upstream, mix):
    queries, ups = two_heads(query), two_heads(upstream)
    product = two_heads(upstream.astype(FULL) * mix.astype(FULL))
    row_dot = jnp.sum(product, axis=1, keepdims=True)
    d_scores = (probs.astype(FULL) * (dot_t(ups, values) - row_dot)).astype(LOW)
    scale = HD ** (-0.5)
    return one_row(dot(d_scores, keys)) * scale, t_dot(d_scores, queries) * scale, t_dot(probs, ups)


def row_dots(mix, upstream):
    product = (mix.astype(FULL) * upstream.astype(FULL)).T
    sums = [
        jnp.sum(product[i : i + HD], axis=0, keepdims=True) for i in range(0, product.shape[0], HD)
    ]
    return [jnp.concatenate(sums[i : i + 2], axis=1) for i in range(0, len(sums), 2)]


def attend_back_sides(query, keys, values, probs, upstream, row_dot):
    queries, ups = two_heads(query), two_heads(upstream)
    scale = HD ** (-0.5)
    d_scores = (probs.astype(FULL) * (dot_t(values, ups) - row_dot)).astype(LOW)
    d_query = one_side(t_dot(keys, d_scores)).T * scale
    return d_query, dot(d_scores, queries) * scale, dot(probs, ups)


def twice(mask, axis):
    wide = jnp.where(mask, 1, 0)
    return jnp.concatenate([wide, wide], axis=axis) == 1


def self_forward(
    place, weight, x, bias, seg_col, seg_row, joined, probs, mix, x_t, mix_t
):
    x_t[...] = x[...].T
    for side, y, n in each_block(place, weight):
        w = weight.part(side, y)
        at = lanes(n, w.shape[-1])
        joined[:, at] = (dot(x[...], w) + bias[:, at]).astype(LOW)
    width, rows = mix.shape[1], seg_row.shape[-1]
    above = lax.broadcasted_iota(jnp.int32, (rows, rows), 0) <= lax.broadcasted_iota(
        jnp.int32, (rows, rows), 1
    )
    for p in range(mix.shape[0] // rows):
        at = pl.ds(p * rows, rows)
        allowed = twice((seg_col[at, :] == seg_row[p]) & above, 1)
        for h in range(width // PAIR):
            q, k, v = (joined[at, pl.ds(i * width + h * PAIR, PAIR)] for i in range(3))
            low = softmax_sides(q, k, allowed)
            probs[pl.ds((p * (width // PAIR) + h) * rows, rows), :] = low
            mixed = one_side(t_dot(v, low)).astype(LOW)
            mix_t[pl.ds(h * PAIR, PAIR), at] = mixed
            mix[at, pl.ds(h * PAIR, PAIR)] = mixed.T


def first_half(place, w_out, w_query, mix, x, vec, first_sum, low_t, query, acc):
    for side, y, n in each_block(place, w_out):
        w = w_out.part(side, y)
        acc[:, lanes(n, w.shape[-1])] = dot(mix[...], w)
    z = x[...].astype(FULL) + (acc[...] + vec[B_SELF_OUT : B_SELF_OUT + 1, :])
    first_sum[...] = z
    low = norm(z, vec, 0).astype(LOW)
    low_t[...] = low.T
    for side, y, n in each_block(place, w_query):
        w = w_query.part(side, y)
        at = lanes(n, w.shape[-1])
        query[:, at] = (dot(low, w) + vec[B_CROSS_Q : B_CROSS_Q + 1, at]).astype(LOW)


def table_keys(place, weight, x, x2, vec, out, x_t, x_t2):
    half = out.shape[-1] // 2

    @pl.when(pl.program_id(0) == 0)
    def _():
        weight.wait(0)
        weight.wait(1)

    for side in range(2):
        bias = vec[B_CROSS_V : B_CROSS_V + 1, lanes(place[2] ^ side, half)]
        out[side, :, :half] = dot(x[...], weight.part(side, 0)).astype(LOW)
        out[side, :, half:] = (dot(x[...], weight.part(side, 1)) + bias).astype(LOW)
    x_t[...] = x[...].T
    x_t2[...] = x2[...].T


def cross_forward(place, query, kv, table_col, table_row, mix, probs, mix_t):
    rows, half = query.shape
    allowed = twice(table_col[...] == table_row[0], 0)
    for h in range(half // PAIR):
        at = pl.ds(h * PAIR, PAIR)
        low = softmax_rows(query[:, at], kv[0, :, at], allowed)
        probs[0, 0, pl.ds(h * 2 * rows, 2 * rows), :] = low
        mixed = one_row(dot(low, kv[0, :, pl.ds(half + h * PAIR, PAIR)])).astype(LOW)
        mix[:, at] = mixed
        mix_t[at, :] = mixed.T


def second_half(place, weight, mix, first_sum, vec, second_sum, second_low, low_t, acc):
    for side, y, n in each_block(place, weight):
        w = weight.part(side, y)
        acc[:, lanes(n, w.shape[-1])] = dot(mix[...], w)
    z = norm(first_sum[...], vec, 0) + (acc[...] + vec[B_CROSS_OUT : B_CROSS_OUT + 1, :])
    second_sum[...] = z
    low = norm(z, vec, 1).astype(LOW)
    second_low[...] = low
    low_t[...] = low.T


def feed_in(place, weight, x, bias, active, slope, active_t):
    for side, y, n in each_block(place, weight):
        w = weight.part(side, y)
        cols = w.shape[-1]
        at = lanes(n, cols)
        hidden = dot(x[...], w) + bias[:, at]
        share = 0.5 + 0.5 * lax.erf(hidden * 2 ** (-0.5))
        low = (hidden * share).astype(LOW)
        active[:, at] = low
        active_t[pl.ds(pl.multiple_of(n * cols, 128), cols), :] = low.T
        density = jnp.exp(hidden * hidden * (-0.5)) * (2 * math.pi) ** (-0.5)
        slope[:, at] = (share + hidden * density).astype(LOW)


def give(place, send, rows, first=0):
    cols = rows.shape[-1] // 4
    for y in range(2):
        send[y, :, first : first + cols] = rows[:, lanes(block_of(place, 1, y), cols)]


def feed_out(
    place, weight, active, second_sum, cotangent, vec, output, d_third, d_low, grads, send, acc
):
    for side, y, n in each_block(place, weight):
        w = weight.part(side, y)
        acc[:, lanes(n, w.shape[-1])] = dot(active[...], w)
    z = norm(second_sum[...], vec, 1) + (acc[...] + vec[B_FC_OUT : B_FC_OUT + 1, :])
    output[...] = norm(z, vec, 2).astype(LOW)
    back, d_gain, d_shift = norm_back(cotangent[...].astype(FULL), z, vec[GAIN + 2 : GAIN + 3])
    d_third[...] = back
    low = back.astype(LOW)
    d_low[...] = low
    grads[0:1, :] = column_sum(low)
    grads[1:2, :] = d_shift
    grads[2:3, :] = d_gain
    give(place, send, d_low)


def through(place, rows, weight):
    total = 0
    for side, y, n in each_block(place, weight):
        w = weight.part(side, y)
        total += dot_t(rows[:, lanes(n, w.shape[-1])], w)
    return total


def feed_out_back(place, weight, d_third, slope, d_hidden, grads, send):
    _, _, lines, _, rows, cols = weight.buffer.shape
    weight.wait(0)
    weight.wait(1)
    step = max(1, min(lines, 1024 // (2 * rows)))
    for z in range(0, lines, step):
        total = 0
        for side, y, n in each_block(place, weight, wait=False):
            w = weight.buffer[side, y, z : z + step].reshape(-1, cols)
            total += dot_t(d_third[:, lanes(n, cols)], w)
        at = pl.ds(z * 2 * rows, step * 2 * rows)
        low = (slope[:, at].astype(FULL) * total).astype(LOW)
        d_hidden[:, at] = low
        grads[:, at] = column_sum(low)
    give(place, send, d_hidden)


def feed_in_back(
    place, w_in, w_out, d_hidden, d_third, second_sum, vec, d_sum, d_low, d_mix, grads, send
):
    upstream = d_third[...] + through(place, d_hidden, w_in)
    back, d_gain, d_shift = norm_back(upstream, second_sum[...], vec[GAIN + 1 : GAIN + 2])
    d_sum[...] = back
    low = back.astype(LOW)
    d_low[...] = low
    grads[0:1, :] = column_sum(low)
    grads[1:2, :] = d_shift
    grads[2:3, :] = d_gain
    d_mix[...] = through(place, d_low, w_out).astype(LOW)
    give(place, send, d_low)


def cross_backward(place, query, kv, probs, d_mix, mix, d_query, d_kv, grads):
    rows, half = query.shape
    for h in range(half // PAIR):
        at, beside = pl.ds(h * PAIR, PAIR), pl.ds(half + h * PAIR, PAIR)
        dq, dk, dv = attend_back_rows(
            query[:, at],
            kv[0, :, at],
            kv[0, :, beside],
            probs[0, 0, pl.ds(h * 2 * rows, 2 * rows), :],
            d_mix[:, at],
            mix[:, at],
        )
        d_query[:, at] = dq.astype(LOW)
        d_kv[:, at] = dk.astype(LOW)
        low = dv.astype(LOW)
        d_kv[:, beside] = low
        before = jnp.where(pl.program_id(0) == 0, 0.0, grads[:, at])
        grads[:, at] = before + column_sum(low)


def self_backward(
    place, w_query, w_out, d_query, d_sum2, first_sum, vec, joined, probs, mix,
    d_sum, d_low, d_joined, grads, send,
):
    width = d_sum.shape[-1]
    upstream = d_sum2[...] + through(place, d_query, w_query)
    back, d_gain, d_shift = norm_back(upstream, first_sum[...], vec[GAIN : GAIN + 1])
    d_sum[...] = back
    low = back.astype(LOW)
    d_low[...] = low
    d_mix = through(place, d_low, w_out).astype(LOW)
    rows = probs.shape[-1] // 2
    heads = width // PAIR
    for p in range(d_sum.shape[0] // rows):
        at = pl.ds(p * rows, rows)
        ups = d_mix[p * rows : (p + 1) * rows]
        dots = row_dots(mix[at, :], ups)
        for h in range(heads):
            where = [pl.ds(i * width + h * PAIR, PAIR) for i in range(3)]
            q, k, v = (joined[at, w] for w in where)
            found = attend_back_sides(
                q,
                k,
                v,
                probs[pl.ds((p * heads + h) * rows, rows), :],
                ups[:, h * PAIR : (h + 1) * PAIR],
                dots[h],
            )
            for w, value in zip(where, found):
                d_joined[at, w] = value.astype(LOW)
    grads[0:1, :] = column_sum(d_joined[:, :width])
    grads[1:2, :] = column_sum(d_joined[:, 2 * width :])
    grads[2:3, :] = column_sum(low)
    grads[3:4, :] = column_sum(d_query[...])
    grads[4:5, :] = d_shift
    grads[5:6, :] = d_gain
    give(place, send, d_joined)
    give(place, send, d_low, 3 * width // 4)
    give(place, send, d_query, width)


def input_back(place, weight, d_joined, d_sum, out):
    out[...] = d_sum[...] + through(place, d_joined, weight)


def table_back(place, weight, d_mine, d_other, out):
    @pl.when(pl.program_id(0) == 0)
    def _():
        weight.wait(0)
        weight.wait(1)

    half = d_mine.shape[-1] // 2
    total = 0
    for side, d in enumerate((d_mine, d_other)):
        for y in range(2):
            total += dot_t(d[:, y * half : (y + 1) * half], weight.part(side, y))
    out[...] = total


def quarter_place(step, place):
    c = place[2]
    dy = jnp.where(step == 0, 1, jnp.where(step == 1, 1 - c, jnp.where(step == 2, c, 0)))
    dx = jnp.where(step == 0, 1, jnp.where(step == 1, c, jnp.where(step == 2, 1 - c, 0)))
    return place[0] ^ dy, place[1] ^ dx


def quarter_grads(net, name, products, more):
    lines = net.lines
    ins = []
    for left, left2, right, right2, size, first in products:
        for a in (left, left2):
            view = a.reshape(lines, 2, -1, a.shape[-1])
            block = (lines, 1) + view.shape[2:]
            ins.append((view, block, lambda s, at: (0, quarter_place(s, at)[1], 0, 0)))
        if first is None:
            for a in (right, right2):
                ins.append(
                    (a, (a.shape[0], size), lambda s, at: (0, quarter_place(s, at)[0]))
                )
        else:
            ins.append(
                (
                    right,
                    (right.shape[0], size),
                    lambda s, at: (0, 2 * quarter_place(s, at)[0] + at[2]),
                )
            )
            ins.append(
                (
                    right2,
                    (1, right2.shape[1], size),
                    lambda s, at, first=first: (quarter_place(s, at)[0], 0, first),
                )
            )
    rows = products[0][0].shape[0] // net.wide
    cols = sum(p[4] for p in products)
    extra = more[0].shape[3] if more else 0
    for a in more or ():

        def corner(s, at):
            y, x = quarter_place(s, at)
            return (y, 0, x, 0, 0)

        ins.append((a, (1, lines, 1, extra, cols), corner))

    def body(place, *refs):
        outs = refs[len(ins) :]
        quarters = []
        start = 0
        for i, (_, _, _, _, size, first) in enumerate(products):
            left, left2, right, right2 = refs[4 * i : 4 * i + 4]
            l, l2 = (a[:, 0].reshape(lines * rows, -1) for a in (left, left2))
            r2 = right2[...] if first is None else right2[0]
            value = dot(l, right[...]) + dot(l2, r2)
            quarters.append((start, size, value.astype(LOW).reshape(lines, rows, size)))
            start += size

        def put(out):
            for z in range(lines):
                differs = place[3] ^ z
                to = sum(
                    ((differs >> bit) & 1) * (lines >> (bit + 1))
                    for bit in range(lines.bit_length() - 1)
                )
                for start, size, value in quarters:
                    out[to, :rows, start : start + size] = value[z]
                if extra:
                    a, b = refs[4 * len(products) : len(ins)]
                    value = a[0, z, 0].astype(FULL) + b[0, z, 0].astype(FULL)
                    out[to, rows:, :] = value.astype(LOW)

        step = pl.program_id(0)
        pl.when(step < 2)(lambda: put(outs[0].at[0]))
        pl.when(step == 2)(lambda: put(outs[1]))
        pl.when(step == 3)(lambda: put(outs[2]))

    shape = (lines, rows + extra, cols)
    return call(
        body,
        name,
        net,
        (4,),
        ins,
        [
            ((2,) + shape, LOW, (1,) + shape, lambda s, at: (jnp.minimum(s, 1), 0, 0, 0)),
            whole_out(shape, LOW),
            whole_out(shape, LOW),
        ],
    )


def segment_index(lengths, count):
    segment_ends = jnp.cumsum(lengths, axis=-1)
    position = jnp.arange(count, dtype=jnp.int32)
    passed = (position[None, :, None] >= segment_ends[:, None, :]).astype(jnp.int32)
    return jnp.sum(passed, axis=-1)


def per_device(
    inputs,
    memory,
    cotangent,
    dec_lengths,
    mem_lengths,
    seg_table,
    self_qkv,
    self_out,
    cross_q,
    cross_kv,
    cross_out,
    fc_in,
    fc_out,
    vec_bias,
    norm_gain,
    fc_in_bias,
    *,
    wide,
    narrow,
):
    net = Net(wide, narrow)
    Order.last = Order.soon = Order.later = ()
    pairs, length, width = inputs.shape
    held = memory.shape[1]
    x = inputs.reshape(-1, width)
    table = memory.reshape(-1, width)
    upstream = cotangent.reshape(-1, width)
    count, quarter, half = x.shape[0], width // narrow, width // 2
    hidden = fc_out.shape[0] * wide

    rows = jnp.concatenate([vec_bias, norm_gain])
    small = jnp.concatenate([rows.reshape(-1), fc_in_bias])
    extra = 16
    small_rows = jnp.zeros((extra, self_qkv.shape[1]), LOW).at[0, : small.size].set(small)
    table2 = net.over_core(table)
    g2 = Weight(net, jnp.concatenate([self_qkv, small_rows])).at_once()
    g2.rows = self_qkv.shape[0]
    shards = jnp.concatenate([cross_kv, cross_out, self_out, cross_q], axis=1)
    g3, g4, g5 = Weight(net, shards), Weight(net, fc_in), PairedWeight(net, fc_out).begin()
    g2.start(g5.mate)
    g3.line(g2.held, g5.mate)
    Order.need(table2, *g2.copy("held", after=g5.mate))
    g3.line_on()
    g4.line()
    g2.turn()
    Order.need(*g2.copy("one", "two"))
    if net.lines == 4:
        Order.need(g4.got)
    g3.line_end()
    g3.start()
    g4.line_on()
    g5.pair().line()
    g2.copy("three")

    segments = segment_index(dec_lengths, length)
    tables = segment_index(mem_lengths, held)
    matches = segments[:, :, None] == jnp.arange(dec_lengths.shape[-1], dtype=jnp.int32)
    query_table = jnp.sum(jnp.where(matches, seg_table[:, None, :], 0), axis=-1)
    seg_col, seg_row = segments.reshape(-1, 1), segments.reshape(pairs, 1, length)
    table_col, table_row = query_table.reshape(-1, 1), tables.reshape(pairs, 1, held)

    def in_place(pieces):
        sides = []
        for side, (same, one, two, three) in enumerate((pieces[:4], pieces[4:])):
            first = (net.c ^ side) == 0
            by_x = jnp.where(first, one, two)
            by_y = jnp.where(first, two, one)
            sides.append(jnp.stack([jnp.stack([same, by_x]), jnp.stack([by_y, three])]))
        out = jnp.stack(net.swap(*sides))
        out = jnp.where(net.y == 0, out, out[:, ::-1])
        out = jnp.where(net.x == 0, out, out[:, :, ::-1])
        return jnp.transpose(out, (3, 2, 1, 0, 4)).reshape(wide, narrow, -1)

    vectors = in_place([p[:, self_qkv.shape[0], : small.size] for p in g2.arrays()]).astype(FULL)
    fc_bias = vectors[:, :, rows.size :].reshape(1, -1)
    vec = vectors[:, :, : rows.size].reshape(wide * narrow, rows.shape[0], -1)
    vec = jnp.transpose(vec, (1, 0, 2)).reshape(rows.shape[0], width)
    joined_bias = jnp.concatenate([vec[0], jnp.zeros((width,), FULL), vec[1]])[None]

    heads = width // PAIR
    joined, self_probs, self_mix, x_t, self_mix_t = call(
        self_forward,
        "self_forward",
        net,
        (1,),
        [whole(x), whole(joined_bias), whole(seg_col), whole(seg_row)],
        [
            whole_out((count, 3 * width), LOW),
            whole_out((pairs * heads * length, 2 * length), LOW),
            whole_out((count, width), LOW),
            whole_out((width, count), LOW),
            whole_out((width, count), LOW),
        ],
        weights=[(g2, 0, 3 * quarter)],
    )
    g4.line_end()
    g5.line_on()
    g3.turn()
    copies = g3.copy("held", "one", "two")
    g4.start(*copies)
    g3.copy("three")
    first_sum, first_low_t, query = call(
        first_half,
        "first_half",
        net,
        (1,),
        [whole(self_mix), whole(x), whole(vec)],
        [
            whole_out((count, width), FULL),
            whole_out((width, count), LOW),
            whole_out((count, width), LOW),
        ],
        [pltpu.VMEM((count, width), FULL)],
        weights=[(g3, 3 * quarter, quarter), (g3, 4 * quarter, quarter)],
    )
    tile = 512
    kv, table_t, table_t2 = call(
        table_keys,
        "table_keys",
        net,
        (table.shape[0] // tile,),
        [
            (table, (tile, width), lambda t, at: (t, 0)),
            (table2, (tile, width), lambda t, at: (t, 0)),
            whole(vec),
        ],
        [
            ((2, table.shape[0], width), LOW, (2, tile, width), lambda t, at: (0, t, 0)),
            ((width, table.shape[0]), LOW, (width, tile), lambda t, at: (0, t)),
            ((width, table.shape[0]), LOW, (width, tile), lambda t, at: (0, t)),
        ],
        weights=[(g3, 0, half)],
    )
    g4.turn()
    g4.copy("held", "one")
    g5.line_end()
    g5.turn()
    g5.copy("held")
    score_rows = half // PAIR * 2 * length
    core_block = ((length, half), lambda s, p, at: (p, at[2] ^ s))
    cross_mix, cross_probs, cross_mix_t = call(
        cross_forward,
        "cross_forward",
        net,
        (2, pairs),
        [
            (query, *core_block),
            (kv, (1, held, width), lambda s, p, at: (s, p, 0)),
            (table_col, (length, 1), lambda s, p, at: (p, 0)),
            (table_row, (1, 1, held), lambda s, p, at: (p, 0, 0)),
        ],
        [
            ((count, width), LOW, *core_block),
            (
                (2, pairs, score_rows, held),
                LOW,
                (1, 1, score_rows, held),
                lambda s, p, at: (s, p, 0, 0),
            ),
            ((width, count), LOW, (half, length), lambda s, p, at: (at[2] ^ s, p)),
        ],
    )
    g4.copy("two", "three")
    second_sum, second_low, second_low_t = call(
        second_half,
        "second_half",
        net,
        (1,),
        [whole(cross_mix), whole(first_sum), whole(vec)],
        [
            whole_out((count, width), FULL),
            whole_out((count, width), LOW),
            whole_out((width, count), LOW),
        ],
        [pltpu.VMEM((count, width), FULL)],
        weights=[(g3, half, quarter)],
    )
    active, slope, active_t = call(
        feed_in,
        "feed_in",
        net,
        (1,),
        [whole(second_low), whole(fc_bias)],
        [
            whole_out((count, hidden), LOW),
            whole_out((count, hidden), LOW),
            whole_out((hidden, count), LOW),
        ],
        weights=[(g4, 0, hidden // 4)],
    )
    g5.copy("far")
    active_t2, second_low_t2 = (net.over_core(a, g5.far) for a in (active_t, second_low_t))
    output, d_third, d_low3, grads3, send3 = call(
        feed_out,
        "feed_out",
        net,
        (1,),
        [whole(active), whole(second_sum), whole(upstream), whole(vec)],
        [
            whole_out((count, width), LOW),
            whole_out((count, width), FULL),
            whole_out((count, width), LOW),
            whole_out((8, width), FULL),
            whole_out((2, count, quarter), LOW),
        ],
        [pltpu.VMEM((count, width), FULL)],
        weights=[(g5, 0, quarter)],
    )

    got3 = net.over_core(send3)
    first_low_t2, self_mix_t2, cross_mix_t2, x_t2 = Order.pin(
        *(net.over_core(a) for a in (first_low_t, self_mix_t, cross_mix_t, x_t))
    )
    r_out = Reduction(net, "grad_out", [(active_t, active_t2, d_low3, got3, quarter, 0)]).start()
    d_hidden, g_fc_bias, send_hidden = call(
        feed_out_back,
        "feed_out_back",
        net,
        (1,),
        [whole(d_low3), whole(slope)],
        [
            whole_out((count, hidden), LOW),
            whole_out((1, hidden), FULL),
            whole_out((2, count, hidden // 4), LOW),
        ],
        weights=[(g5, 0, quarter)],
    )
    got_hidden = net.over_core(send_hidden)
    r_in = Reduction(
        net, "grad_in", [(second_low_t, second_low_t2, d_hidden, got_hidden, hidden // 4, 0)]
    ).start()
    d_sum2, d_low2, d_mix, grads2, send2 = call(
        feed_in_back,
        "feed_in_back",
        net,
        (1,),
        [whole(d_hidden), whole(d_third), whole(second_sum), whole(vec)],
        [
            whole_out((count, width), FULL),
            whole_out((count, width), LOW),
            whole_out((count, width), LOW),
            whole_out((8, width), FULL),
            whole_out((2, count, quarter), LOW),
        ],
        weights=[(g4, 0, hidden // 4), (g3, half, quarter)],
    )
    r_out.turn()
    def tables_back(side, into=()):
        block = ((length, half), lambda p, at: (p, at[2] ^ side))
        return call(
            cross_backward,
            "cross_backward",
            net,
            (pairs,),
            [
                (query, *block),
                (kv, (1, held, width), lambda p, at: (side, p, 0)),
                (cross_probs, (1, 1, score_rows, held), lambda p, at: (side, p, 0, 0)),
                (d_mix, *block),
                (cross_mix, *block),
            ],
            [
                ((count, width), LOW, *block),
                (table.shape, LOW, (held, width), lambda p, at: (p, 0)),
                whole_out((1, half), FULL),
            ],
            into=into,
        )

    d_query, d_other, grads_other = tables_back(1)
    d_query, d_mine, grads_mine = tables_back(0, (d_query,))
    d_sum1, d_low1, d_joined, grads1, send1 = call(
        self_backward,
        "self_backward",
        net,
        (1,),
        [
            whole(d_query),
            whole(d_sum2),
            whole(first_sum),
            whole(vec),
            whole(joined),
            whole(self_probs),
            whole(self_mix),
        ],
        [
            whole_out((count, width), FULL),
            whole_out((count, width), LOW),
            whole_out((count, 3 * width), LOW),
            whole_out((8, width), FULL),
            whole_out((2, count, 5 * quarter), LOW),
        ],
        weights=[(g3, 4 * quarter, quarter), (g3, 3 * quarter, quarter)],
    )
    waits = (r_out.near, r_in.pair)
    got1, got_table = net.over_core(send1, *waits), net.over_core(d_other, *waits)
    r_out.line()
    r_in.turn()
    r_self = Reduction(
        net,
        "grad_self",
        [
            (x_t, x_t2, d_joined, got1, 3 * quarter, 0),
            (self_mix_t, self_mix_t2, d_low1, got1, quarter, 3),
            (first_low_t, first_low_t2, d_query, got1, quarter, 4),
        ],
    ).start(r_in.near, r_out.step, got_table)
    grads_v = jnp.concatenate(net.swap(grads_mine, grads_other), axis=1)
    g_rows = jnp.concatenate(
        [
            grads1[:4],
            grads_v,
            grads2[:1],
            grads3[:1],
            grads1[4:5],
            grads2[1:2],
            grads3[1:2],
            grads1[5:6],
            grads2[2:3],
            grads3[2:3],
        ]
    )
    g_rows = jnp.transpose(g_rows.reshape(rows.shape[0], wide, narrow, -1), (2, 1, 0, 3))
    g_small = jnp.transpose(g_fc_bias.reshape(wide, narrow, -1), (1, 0, 2))
    g_small = jnp.concatenate([g_rows.reshape(narrow, wide, -1), g_small], axis=2).astype(LOW)
    room = extra * 3 * quarter - small.size
    g_small = jnp.pad(g_small, ((0, 0), (0, 0), (0, room)))
    g_small = g_small.reshape(2, 2, wide // 2, 2, extra, -1)
    small_mine, small_other = net.swap(g_small[:, 0], g_small[:, 1])
    small_got, got2 = net.over_core(small_other), net.over_core(send2)
    r_out.line_on()
    r_in.line()
    r_cross = Reduction(
        net,
        "grad_cross",
        [
            (table_t, table_t2, d_mine, got_table, half, None),
            (cross_mix_t, cross_mix_t2, d_low2, got2, quarter, 0),
        ],
        (small_mine, small_got),
    ).start()
    r_out.line_end()
    r_in.line_on()
    (input_grad,) = call(
        input_back,
        "input_back",
        net,
        (1,),
        [whole(d_joined), whole(d_sum1)],
        [whole_out((count, width), FULL)],
        weights=[(g2, 0, 3 * quarter)],
    )
    r_self.turn(r_out.total)
    tile = 512
    (memory_grad,) = call(
        table_back,
        "table_back",
        net,
        (table.shape[0] // tile,),
        [(d, (tile, width), lambda t, at: (t, 0)) for d in (d_mine, d_other)],
        [(table.shape, FULL, (tile, width), lambda t, at: (t, 0))],
        weights=[(g3, 0, half)],
    )
    r_in.line_end()
    r_cross.turn(r_self.near, r_in.total)
    r_self.line(r_cross.ready)
    r_cross.line()
    r_self.line_on(r_cross.total)
    r_cross.line_on()
    r_self.line_end(r_cross.total)
    r_cross.line_end()

    g_out, g_in, g_cross, g_self = (r.total for r in (r_out, r_in, r_cross, r_self))
    g_small = g_cross[-extra:].reshape(-1)[: small.size]
    g_rows, g_fc_bias = g_small[: rows.size].reshape(rows.shape), g_small[rows.size :]
    return (
        output.reshape(inputs.shape),
        input_grad.reshape(inputs.shape),
        memory_grad.reshape(memory.shape),
        g_self[:, : 3 * quarter],
        g_self[:, 3 * quarter : 4 * quarter],
        g_self[:, 4 * quarter :],
        g_cross[:-extra, : 2 * quarter],
        g_cross[:-extra, 2 * quarter :],
        g_in,
        g_out,
        g_rows[:10],
        g_rows[10:],
        g_fc_bias,
    )


def solution(mesh):
    tokens = P(BOTH, None, None)
    lengths = P(BOTH, None)
    weight = P("wide", "narrow")
    vector = P(None, BOTH)
    return jax.shard_map(
        partial(per_device, wide=mesh.shape["wide"], narrow=mesh.shape["narrow"]),
        mesh=mesh,
        in_specs=(tokens,) * 3 + (lengths,) * 3 + (weight,) * 7 + (vector, vector, P(BOTH)),
        out_specs=(tokens,) * 3 + (weight,) * 7 + (vector, vector, P(BOTH)),
        check_vma=False,
    )
```
